32 devices in a mesh: dp: 16 (over z, y, x), mp: 2 (over core).
Axes of the slice: x: 2, y: 2, z: 4, core: 2. Of those that a mesh axis runs over, the one named last changes fastest.
Arguments:
- hidden_in: bfloat16 [8192, 768], P(('dp', 'mp')), may hold values from -6 to 6
- memory: bfloat16 [8192, 768], P(('dp', 'mp')), may hold values from -6 to 6
- output_grad: bfloat16 [8192, 768], P(('dp', 'mp')), may hold values from -6 to 6
- segment_ids: int32 [16, 512], P('dp'), may hold values from 0 to 3, never falling along the last dimension, each value on 1 to 384 neighbouring positions
- route_counts: int32 [16, 16], replicated, may hold values from 0 to 32, as said below
- norm_gains: bfloat16 [3, 768], replicated, may hold values from 0.5 to 1.5
- self_qkv: bfloat16 [3, 768, 768], P(None, None, 'mp'), may hold values from -0.109375 to 0.109375
- self_out: bfloat16 [768, 768], P('mp'), may hold values from -1.75 to 1.75
- cross_qkv: bfloat16 [3, 768, 768], P(None, None, 'mp'), may hold values from -0.109375 to 0.109375
- cross_out: bfloat16 [768, 768], P('mp'), may hold values from -1.75 to 1.75
- ff_in: bfloat16 [768, 3072], P(None, 'mp'), may hold values from -0.21875 to 0.21875
- ff_out: bfloat16 [3072, 768], P('mp'), may hold values from -0.109375 to 0.109375
- rel_bias: bfloat16 [32, 12], P(None, 'mp'), may hold values from -4 to 4
Outputs:
- block_out: bfloat16 [8192, 768], P(('dp', 'mp'))
- input_grad: bfloat16 [8192, 768], P(('dp', 'mp'))
- memory_grad: bfloat16 [8192, 768], P(('dp', 'mp'))
- gains_grad: float32 [3, 768], replicated
- bias_grad: float32 [32, 12], replicated
- self_qkv_grad: float32 [3, 768, 768], P(None, 'dp', 'mp')
- self_out_grad: float32 [768, 768], P('mp', 'dp')
- cross_qkv_grad: float32 [3, 768, 768], P(None, 'dp', 'mp')
- cross_out_grad: float32 [768, 768], P('mp', 'dp')
- ff_in_grad: float32 [768, 3072], P('dp', 'mp')
- ff_out_grad: float32 [3072, 768], P('mp', 'dp')
The draws below stay inside these ranges and needn't reach their ends.
Inputs may be any that keep to these rules, and one draw needn't show every extreme that they name: route_counts[s, o] is the number of rows that each core of dp index s sends to the same core of dp index o; every row and every column of the table sums to 256. `segment_ids`: each row holds the example ids of one dp index's rows in the owners' layout; they start at 0 and never fall, and each of the 4 examples has 1 to 384 rows.
All inputs are finite; a program needn't handle non-finite values.
Results may differ from the reference program's by a relative error of at most 0.04.
The reference program's roundings to bfloat16 on the way count: a program that leaves them out, or rounds other values in their place, can miss the bound.
Values may be sent and summed in bfloat16 or wider, within the bound.
No kernel may reach another device: no remote copies, remote signals or barrier semaphores. Data moves between devices by JAX's collectives and lax.ppermute only.
A program may use at most 128 MiB of HBM per device.

```python
import math
from functools import partial
import jax
import jax.numpy as jnp
import numpy as np
from jax import lax

D = 768
HEADS = 12
HEAD_DIM = 64
FF = 3072
BUCKETS = 32
MAX_DIST = 128
TOK_DEV = 512
EXAMPLES = 4
SEQ_MAX = 384
TOKENS = 8192
N_DP = 16
N_MP = 2


def draw_route_counts(key, part):
    key = jax.random.fold_in(key, 7)
    level_key, peak_key, source_key, owner_key = jax.random.split(key, 4)
    mean_share = TOK_DEV // N_MP // N_DP
    levels = jax.random.randint(level_key, (N_DP,), 0, mean_share + 1)
    peak_slot = jax.random.randint(peak_key, (), 0, N_DP)
    slot_index = jnp.arange(N_DP)
    levels = jnp.where(slot_index == peak_slot, mean_share, levels)
    levels = jnp.where(slot_index == (peak_slot + 1) % N_DP, 0, levels)
    level_steps = levels - jnp.roll(levels, -1)
    source_order = jax.random.permutation(source_key, N_DP)
    owner_order = jax.random.permutation(owner_key, N_DP)
    offsets = (owner_order[None, :] - source_order[:, None]) % N_DP
    return (mean_share + jnp.take(level_steps, offsets)).astype(jnp.int32)


def shard_levels(key, dims, pieces, smallest, high):
    loudness, own = 1.0, jax.random.fold_in(key, 6)
    for position, blocks in pieces:
        heights = jnp.exp(jax.random.uniform(jax.random.fold_in(own, position), (blocks,), jnp.float32, smallest / len(pieces), high / len(pieces)))
        loudness = loudness * jnp.repeat(heights, dims[position] // blocks).reshape([-1 if axis == position else 1 for axis in range(len(dims))])
    return loudness


def length_profile(amount, total, limit, slope):
    loads = [(1 << 20) // math.isqrt(rank ** slope) + 1 for rank in range(2, amount + 1)]
    spare, counts = total - limit - (amount - 1), [1] * (amount - 1)
    while spare > 0:
        free = [i for i in range(amount - 1) if counts[i] < limit]
        whole, budget = sum([loads[i] for i in free]), spare
        for i in free:
            addition = min(limit - counts[i], max(1, budget * loads[i] // whole), spare)
            counts[i] = counts[i] + addition
            spare = spare - addition
    return np.array([limit] + counts)


def uneven(own_key, number_of, total, bound, skew):
    if number_of == 2:
        one = jax.random.randint(own_key, (), max(1, total - bound), min(bound, total - 1) + 1)
        return jnp.stack([one, total - one])
    sizes = jnp.asarray(length_profile(number_of, total, bound, skew), jnp.int32)
    pairs = (number_of - 1) // 2
    giver, taker = sizes[1:1 + 2 * pairs:2], sizes[2:2 + 2 * pairs:2]
    slack = jnp.minimum(giver - 1, bound - taker)
    passed = jax.random.randint(jax.random.fold_in(own_key, 1), (pairs,), 0, 1 << 20) % (slack + 1)
    sizes = sizes.at[1:1 + 2 * pairs:2].set(giver - passed).at[2:2 + 2 * pairs:2].set(taker + passed)
    return sizes[jax.random.permutation(jax.random.fold_in(own_key, 2), number_of)]


def centred(rng, shape, width, most, cuts=(), held_as=jnp.bfloat16):
    values = jax.random.normal(rng, shape, jnp.float32) * width
    if len(cuts) > 0:
        values = shard_levels(rng, shape, cuts, -0.22, 0.18) * values
    return jnp.clip(values, min=-most, max=most).astype(held_as)


def setup_inputs(seed: int = 0) -> dict:
    seeds = jax.random.split(jax.random.key(seed), 14)
    hidden_in = centred(seeds[0], (TOKENS, D), 1.0, 6.0, ((0, 32),))
    memory = centred(seeds[1], (TOKENS, D), 1.0, 6.0, ((0, 32),))
    output_grad = centred(seeds[2], (TOKENS, D), 1.0, 6.0, ((0, 32),))
    segment_ids = jax.vmap(lambda own: jnp.searchsorted(jnp.cumsum(uneven(own, EXAMPLES, TOK_DEV, SEQ_MAX, 0)), jnp.arange(TOK_DEV), side="right"))(jax.random.split(seeds[3], N_DP)).reshape((N_DP, TOK_DEV)).astype(jnp.int32)
    route_counts = draw_route_counts(jax.random.fold_in(seeds[13], 71), 0)
    norm_gains = jnp.clip(1.0 + 0.1 * jax.random.normal(seeds[5], (3, D), jnp.float32), 0.5, 1.5).astype(jnp.bfloat16)
    self_qkv = centred(seeds[6], (3, D, HEADS * HEAD_DIM), (4 * D) ** -0.5, 0.109375, ((2, 2),))
    self_out = centred(seeds[7], (HEADS * HEAD_DIM, D), (D // 64) ** -0.5, 1.75, ((0, 2),))
    cross_qkv = centred(seeds[8], (3, D, HEADS * HEAD_DIM), (4 * D) ** -0.5, 0.109375, ((2, 2),))
    cross_out = centred(seeds[9], (HEADS * HEAD_DIM, D), (D // 64) ** -0.5, 1.75, ((0, 2),))
    ff_in = centred(seeds[10], (D, FF), D ** -0.5, 0.21875, ((1, 2),))
    ff_out = centred(seeds[11], (FF, D), FF ** -0.5, 0.109375, ((0, 2),))
    rel_bias = centred(seeds[12], (BUCKETS, HEADS), 1.0, 4.0, ((1, 2),))
    return dict(hidden_in=hidden_in, memory=memory, output_grad=output_grad, segment_ids=segment_ids, route_counts=route_counts, norm_gains=norm_gains, self_qkv=self_qkv, self_out=self_out, cross_qkv=cross_qkv, cross_out=cross_out, ff_in=ff_in, ff_out=ff_out, rel_bias=rel_bias)


epsilon = 1e-06
masked_score = -1e+30

@jax.custom_vjp
def low(v):
    return lax.optimization_barrier(v.astype(jnp.bfloat16)).astype(jnp.float32)

@jax.custom_vjp
def low_back(v):
    return v

def low_keep(v):
    return (low(v), None)

def low_pass(kept, grad):
    return (grad,)

def back_keep(v):
    return (v, None)

def back_low(kept, grad):
    return (low(grad),)
low.defvjp(low_keep, low_pass)
low_back.defvjp(back_keep, back_low)

def bucket_edges(buckets, distance):
    exact_span = buckets // 2
    edge_list = []
    for offset in range(1, 4 * distance):
        if offset < exact_span:
            bucket_now = offset
        else:
            log_ratio = np.log(offset / exact_span) / np.log(distance / exact_span)
            bucket_now = min(buckets - 1, exact_span + int(log_ratio * (buckets - exact_span)))
        while len(edge_list) < bucket_now:
            edge_list.append(offset)
    return np.array(edge_list, dtype=np.int32)

def rms_norm(values, gain_row):
    scale = lax.rsqrt(lax.optimization_barrier(jnp.mean(values * values, axis=-1, keepdims=True)) + epsilon)
    return values * scale * gain_row

def exact_dot(left, right):
    return jnp.dot(left, right, precision=lax.Precision.HIGHEST)

def attend(queries, keys, values, allowed, bias_grid):
    scores = jnp.einsum('qhd,khd->hqk', queries, keys, precision=lax.Precision.HIGHEST)
    if bias_grid is not None:
        scores = scores + bias_grid
    scores = jnp.where(allowed[None], low_back(scores), masked_score)
    peak = lax.optimization_barrier(jnp.max(scores, axis=-1, keepdims=True))
    weights = jnp.exp(scores - peak)
    probs = low(weights / lax.optimization_barrier(jnp.sum(weights, axis=-1, keepdims=True)))
    mixed = jnp.einsum('hqk,khd->qhd', probs, values, precision=lax.Precision.HIGHEST)
    return mixed.reshape(mixed.shape[0], -1)

def arrival_order(route_counts):
    half_rows = TOK_DEV // N_MP
    in_end = jnp.cumsum(route_counts, axis=0).astype(jnp.int32)
    input_begin_row = (in_end - route_counts).astype(jnp.int32)
    out_start = (jnp.cumsum(route_counts, axis=1) - route_counts).astype(jnp.int32)
    positions = jnp.arange(half_rows, dtype=jnp.int32)
    source_of = lax.optimization_barrier(jnp.sum((positions[None, :, None] >= in_end.T[:, None, :]).astype(jnp.int32), axis=2)).astype(jnp.int32)
    within = positions[None, :] - jnp.take_along_axis(input_begin_row.T, source_of, axis=1)
    offset_of = jnp.take_along_axis(out_start.T, source_of, axis=1)
    core_index = jnp.arange(N_MP, dtype=jnp.int32)
    arrival = (source_of[:, None, :] * N_MP + core_index[None, :, None]) * half_rows + offset_of[:, None, :] + within[:, None, :]
    return arrival.reshape(-1).astype(jnp.int32)

def owner_forward(params, inputs, memory_rows, example_ids):
    gains, self_qkv, self_out, cross_qkv, cross_out, ff_in, ff_out, rel_bias = params
    row_total = inputs.shape[0]
    positions = jnp.arange(row_total, dtype=jnp.int32)
    distance = positions[:, None] - positions[None, :]
    same_example = example_ids[:, None] == example_ids[None, :]
    causal = same_example & (distance >= 0)
    bucket = jnp.searchsorted(jnp.asarray(bucket_edges(BUCKETS, MAX_DIST)), distance, side='right').astype(jnp.int32)
    bias_grid = jnp.transpose(jnp.take(rel_bias, bucket, axis=0), (2, 0, 1))

    def split_heads(tensor):
        return tensor.reshape(row_total, HEADS, HEAD_DIM)
    normed = low(rms_norm(inputs, gains[0]))
    self_query = split_heads(low(low_back(exact_dot(normed, self_qkv[0]))))
    self_key = split_heads(low(low_back(exact_dot(normed, self_qkv[1]))))
    self_value = split_heads(low(low_back(exact_dot(normed, self_qkv[2]))))
    mixed_heads = low(low_back(attend(self_query, self_key, self_value, causal, bias_grid)))
    hidden = inputs + low_back(exact_dot(mixed_heads, self_out))
    normed = low(rms_norm(hidden, gains[1]))
    cross_query = split_heads(low(low_back(exact_dot(normed, cross_qkv[0]))))
    cross_key = split_heads(low(low_back(exact_dot(memory_rows, cross_qkv[1]))))
    cross_value = split_heads(low(low_back(exact_dot(memory_rows, cross_qkv[2]))))
    mixed_heads = low(low_back(attend(cross_query, cross_key, cross_value, same_example, None)))
    hidden = hidden + low_back(exact_dot(mixed_heads, cross_out))
    normed = low(rms_norm(hidden, gains[2]))
    pre_act = low_back(exact_dot(normed, ff_in))
    activated = low(jax.nn.gelu(pre_act, approximate=True))
    return hidden + low_back(exact_dot(activated, ff_out))

def reference(hidden_in, memory, output_grad, segment_ids, route_counts, norm_gains, self_qkv, self_out, cross_qkv, cross_out, ff_in, ff_out, rel_bias):
    order = arrival_order(route_counts)
    params = tuple((item.astype(jnp.float32) for item in (norm_gains, self_qkv, self_out, cross_qkv, cross_out, ff_in, ff_out, rel_bias)))

    def forward(inputs, memory_rows, weights):
        owner_inputs = jnp.take(inputs, order, axis=0).reshape(N_DP, TOK_DEV, D)
        owner_memory = jnp.take(memory_rows, order, axis=0).reshape(N_DP, TOK_DEV, D)
        owner_step = jax.checkpoint(partial(owner_forward, weights))

        def run_owner(items):
            return owner_step(items[0], items[1], items[2])
        outputs = lax.map(run_owner, (owner_inputs, owner_memory, segment_ids))
        return outputs.reshape(TOKENS, D)
    block_out, pull = jax.vjp(forward, hidden_in.astype(jnp.float32), memory.astype(jnp.float32), params)
    input_grad, memory_grad, weight_grads = pull(output_grad.astype(jnp.float32))
    gains_grad, self_qkv_grad, self_out_grad, cross_qkv_grad, cross_out_grad, ff_in_grad, ff_out_grad, bias_grad = weight_grads
    return (block_out.astype(jnp.bfloat16), input_grad.astype(jnp.bfloat16), memory_grad.astype(jnp.bfloat16), gains_grad, bias_grad, self_qkv_grad, self_out_grad, cross_qkv_grad, cross_out_grad, ff_in_grad, ff_out_grad)
```

```python
from functools import partial

import jax
import jax.numpy as jnp
import numpy as np
from jax import lax
from jax.sharding import PartitionSpec as P

HEAD_DIM = 64
MAX_DIST = 128
EPS = 1e-06
MASKED = -1e30
F32 = jnp.float32
BF16 = jnp.bfloat16


def bucket_edges(buckets, distance):
    exact_span = buckets // 2
    edge_list = []
    for offset in range(1, 4 * distance):
        if offset < exact_span:
            bucket_now = offset
        else:
            log_ratio = np.log(offset / exact_span) / np.log(distance / exact_span)
            bucket_now = min(buckets - 1, exact_span + int(log_ratio * (buckets - exact_span)))
        while len(edge_list) < bucket_now:
            edge_list.append(offset)
    return np.array(edge_list, dtype=np.int32)


def dot(a, b):
    return jnp.dot(a, b, preferred_element_type=F32)


def dot_nt(a, b):
    return lax.dot_general(a, b, (((1,), (1,)), ((), ())), preferred_element_type=F32)


def dot_tn(a, b):
    return lax.dot_general(a, b, (((0,), (0,)), ((), ())), preferred_element_type=F32)


def rms_norm(values, gain_row):
    scale = lax.rsqrt(jnp.mean(values * values, axis=-1, keepdims=True) + EPS)
    return values * scale * gain_row


def norm_back(values, gain_row, upstream):
    scale = lax.rsqrt(jnp.mean(values * values, axis=-1, keepdims=True) + EPS)
    scaled = gain_row * upstream
    back = scale * scaled - values * (
        scale * scale * scale * jnp.mean(scaled * values, axis=-1, keepdims=True)
    )
    return back, upstream * values * scale


def slot_matrix(counts, capacity, row_total):
    peers = counts.shape[0]
    order = jnp.arange(peers, dtype=jnp.int32)
    starts = jnp.sum(jnp.where(order[None, :] < order[:, None], counts[None, :], 0), axis=1)
    within = jnp.arange(capacity, dtype=jnp.int32)
    rows = jnp.where(within[None, :] < counts[:, None], starts[:, None] + within[None, :], -1)
    return (
        rows.reshape(-1)[:, None] == jnp.arange(row_total, dtype=jnp.int32)[None, :]
    ).astype(BF16)


def exchange_rows(packed, peers):
    shape = packed.shape
    blocks = packed.reshape(peers, shape[0] // peers, shape[1])
    return lax.all_to_all(blocks, "dp", split_axis=0, concat_axis=0, tiled=True).reshape(shape)


def swap(values):
    return lax.ppermute(values, "mp", [(0, 1), (1, 0)])


def neighbour(values, bit, peers):
    return lax.ppermute(values, "dp", [(i, i ^ (1 << bit)) for i in range(peers)])


def order_matrix(order, peers, me, width):
    size = width // peers
    row = lax.broadcasted_iota(jnp.int32, (width, width), 0)
    column = lax.broadcasted_iota(jnp.int32, (width, width), 1)
    block, within = row // size, row % size
    relative = jnp.zeros_like(block)
    steps = len(order)
    for position, bit in enumerate(order):
        relative = relative + (((block >> (steps - 1 - position)) & 1) << bit)
    return (column == (relative ^ me) * size + within).astype(BF16)


def halve(grads, order, peers):
    for bit in order:
        half = grads.shape[0] // 2
        arrived = neighbour(grads[half:], bit, peers)
        grads = (grads[:half].astype(F32) + arrived.astype(F32)).astype(BF16)
    return grads


def local(
    hidden_in,
    memory,
    output_grad,
    segment_ids,
    route_counts,
    norm_gains,
    self_qkv,
    self_out,
    cross_qkv,
    cross_out,
    ff_in,
    ff_out,
    rel_bias,
):
    peers = lax.axis_size("dp")
    me = lax.axis_index("dp")
    core = lax.axis_index("mp")
    half_rows, width = hidden_in.shape
    rows = 2 * half_rows
    capacity = 2 * (half_rows // peers)
    heads = rel_bias.shape[1]
    bits = peers.bit_length() - 1
    order_a = tuple(range(bits))
    order_b = (1, 0) + tuple(range(2, bits))

    def own(values):
        return lax.dynamic_slice_in_dim(values, core * half_rows, half_rows, 0)

    def both(values):
        return lax.all_gather(values, "mp", axis=0, tiled=True)

    sent = lax.dynamic_index_in_dim(route_counts, me, 0, keepdims=False)
    taken = lax.dynamic_index_in_dim(route_counts, me, 1, keepdims=False)
    send_slots = slot_matrix(sent, capacity, half_rows)
    take_slots = slot_matrix(taken, capacity, half_rows)

    def there(values):
        arrived = exchange_rows(dot(send_slots, values).astype(BF16), peers)
        return dot_tn(take_slots, arrived).astype(BF16)

    def back(values):
        arrived = exchange_rows(dot(take_slots, values).astype(BF16), peers)
        return dot_tn(send_slots, arrived).astype(BF16)

    x_full = both(there(hidden_in))
    mem_full = both(there(memory))
    og_full = both(output_grad)

    perm_a = order_matrix(order_a, peers, me, width)
    perm_b = order_matrix(order_b, peers, me, width)

    def left_a(values):
        return dot_nt(perm_a, values).astype(BF16)

    def left_b(values):
        return dot_nt(perm_b, values).astype(BF16)

    gains = norm_gains.astype(F32)
    ids = segment_ids[0]
    position = jnp.arange(rows, dtype=jnp.int32)
    distance = position[:, None] - position[None, :]
    same = ids[:, None] == ids[None, :]
    causal = same & (distance >= 0)
    edges = bucket_edges(rel_bias.shape[0], MAX_DIST)
    bucket = jnp.zeros_like(distance)
    for edge in edges.tolist():
        bucket = bucket + (distance >= edge).astype(jnp.int32)
    indicator = (
        bucket[None] == jnp.arange(rel_bias.shape[0], dtype=jnp.int32)[:, None, None]
    ).astype(BF16)
    bias_grid = jnp.einsum("bij,bh->hij", indicator, rel_bias, preferred_element_type=F32)

    def split(values):
        return values.reshape(rows, -1, HEAD_DIM)

    def merge(values):
        return values.reshape(rows, -1)

    def attend(q, k, v, allowed, bias):
        scores = jnp.einsum("qhd,khd->hqk", split(q), split(k), preferred_element_type=F32)
        if bias is not None:
            scores = scores + bias
        scores = jnp.where(allowed[None], scores, MASKED)
        peak = jnp.max(scores, axis=-1, keepdims=True)
        weights = jnp.exp(scores - peak)
        probs = weights / jnp.sum(weights, axis=-1, keepdims=True)
        mix = jnp.einsum("hqk,khd->qhd", probs.astype(BF16), split(v), preferred_element_type=F32)
        return merge(mix).astype(BF16), probs

    def attend_back(q, k, v, probs, d_mix):
        d_mix = split(d_mix)
        d_probs = jnp.einsum("qhd,khd->hqk", d_mix, split(v), preferred_element_type=F32)
        dv = jnp.einsum("hqk,qhd->khd", probs.astype(BF16), d_mix, preferred_element_type=F32)
        d_scores = (
            probs * (d_probs - jnp.sum(probs * d_probs, axis=-1, keepdims=True))
        ).astype(BF16)
        dq = jnp.einsum("hqk,khd->qhd", d_scores, split(k), preferred_element_type=F32)
        dk = jnp.einsum("hqk,qhd->khd", d_scores, split(q), preferred_element_type=F32)
        return (
            merge(dq).astype(BF16),
            merge(dk).astype(BF16),
            merge(dv).astype(BF16),
            d_scores,
        )

    def branch(partial_sum):
        kept = partial_sum.astype(BF16)
        return kept.astype(F32) + swap(kept).astype(F32)

    x = x_full.astype(F32)
    n1 = rms_norm(x, gains[0]).astype(BF16)
    sq, sk, sv = (dot(n1, self_qkv[i]).astype(BF16) for i in range(3))
    self_mix, self_probs = attend(sq, sk, sv, causal, bias_grid)
    h1 = x + branch(dot(self_mix, self_out))
    n2 = rms_norm(h1, gains[1]).astype(BF16)
    cq = dot(n2, cross_qkv[0]).astype(BF16)
    ck, cv = (dot(mem_full, cross_qkv[i]).astype(BF16) for i in (1, 2))
    cross_mix, cross_probs = attend(cq, ck, cv, same, None)
    h2 = h1 + branch(dot(cross_mix, cross_out))
    n3 = rms_norm(h2, gains[2]).astype(BF16)
    pre = dot(n3, ff_in)
    d_act = dot_nt(og_full, ff_out)
    act, gelu_pull = jax.vjp(partial(jax.nn.gelu, approximate=True), pre)
    act = act.astype(BF16)
    d_pre = gelu_pull(d_act)[0].astype(BF16)
    block_out = own(h2) + branch_own(dot(act, ff_out), core, half_rows)

    middle = act.shape[1] // 2
    ff_out_a = halve(dot(left_a(og_full), act[:, :middle]).astype(BF16), order_a, peers)
    ff_out_b = halve(dot(left_b(og_full), act[:, middle:]).astype(BF16), order_b, peers)
    ff_in_a = halve(dot(left_a(n3), d_pre[:, :middle]).astype(BF16), order_a, peers)
    ff_in_b = halve(dot(left_b(n3), d_pre[:, middle:]).astype(BF16), order_b, peers)

    dn3 = branch(dot_nt(d_pre, ff_in))
    dv3, gain3 = norm_back(h2, gains[2], dn3)
    g2 = og_full.astype(F32) + dv3
    g2s = g2.astype(BF16)
    d_cmix = dot_nt(g2s, cross_out).astype(BF16)
    dcq, dck, dcv, unused = attend_back(cq, ck, cv, cross_probs, d_cmix)
    dcols = dcq.shape[1]
    cross_a = halve(
        jnp.concatenate([dot(left_a(g2s), cross_mix), dot(left_a(n2), dcq)], axis=1).astype(BF16),
        order_a,
        peers,
    )
    cross_b = halve(
        dot(left_b(mem_full), jnp.concatenate([dck, dcv], axis=1)).astype(BF16), order_b, peers
    )
    d_mem = branch_own(dot_nt(dck, cross_qkv[1]) + dot_nt(dcv, cross_qkv[2]), core, half_rows)
    memory_grad = back(d_mem.astype(BF16))
    dn2 = branch(dot_nt(dcq, cross_qkv[0]))
    dv2, gain2 = norm_back(h1, gains[1], dn2)
    g1 = g2 + dv2
    g1s = g1.astype(BF16)
    d_smix = dot_nt(g1s, self_out).astype(BF16)
    dsq, dsk, dsv, d_scores = attend_back(sq, sk, sv, self_probs, d_smix)
    self_a = halve(
        jnp.concatenate([dot(left_a(g1s), self_mix), dot(left_a(n1), dsq)], axis=1).astype(BF16),
        order_a,
        peers,
    )
    self_b = halve(
        dot(left_b(n1), jnp.concatenate([dsk, dsv], axis=1)).astype(BF16), order_b, peers
    )
    bias_part = jnp.einsum("hij,bij->bh", d_scores, indicator, preferred_element_type=F32)
    dn1 = branch_own(
        dot_nt(dsq, self_qkv[0]) + dot_nt(dsk, self_qkv[1]) + dot_nt(dsv, self_qkv[2]),
        core,
        half_rows,
    )
    dv1, gain1 = norm_back(own(x), gains[0], dn1)
    input_grad = back((own(g1) + dv1).astype(BF16))

    small = jnp.zeros((rel_bias.shape[0], heads * 2), F32)
    small = lax.dynamic_update_slice_in_dim(small, bias_part, core * heads, 1)
    gain_rows = jnp.stack(
        [jnp.sum(gain1, axis=0), jnp.sum(own(gain2), axis=0), jnp.sum(own(gain3), axis=0)]
    )
    small = jnp.concatenate([gain_rows.reshape(-1), small.reshape(-1)])
    small = small + swap(small)
    for bit in order_a:
        small = small + neighbour(small, bit, peers)
    gains_total = small[: 3 * width].reshape(3, width)
    bias_total = small[3 * width :].reshape(rel_bias.shape[0], heads * 2)

    ff_out_total = jnp.concatenate([ff_out_a, ff_out_b], axis=1).astype(F32).T
    ff_in_total = jnp.concatenate([ff_in_a, ff_in_b], axis=1).astype(F32)
    cross_out_total = cross_a[:, :dcols].astype(F32).T
    cross_qkv_total = jnp.stack([cross_a[:, dcols:], cross_b[:, :dcols], cross_b[:, dcols:]])
    self_out_total = self_a[:, :dcols].astype(F32).T
    self_qkv_total = jnp.stack([self_a[:, dcols:], self_b[:, :dcols], self_b[:, dcols:]])
    return (
        block_out.astype(BF16),
        input_grad,
        memory_grad,
        gains_total,
        bias_total,
        self_qkv_total.astype(F32),
        self_out_total,
        cross_qkv_total.astype(F32),
        cross_out_total,
        ff_in_total,
        ff_out_total,
    )


def branch_own(partial_sum, core, half_rows):
    kept = lax.dynamic_slice_in_dim(partial_sum, core * half_rows, half_rows, 0)
    sent = lax.dynamic_slice_in_dim(partial_sum, (1 - core) * half_rows, half_rows, 0)
    return kept + swap(sent.astype(BF16)).astype(F32)


def solution(mesh):
    both = ("dp", "mp")
    in_specs = (
        P(both, None),
        P(both, None),
        P(both, None),
        P("dp", None),
        P(),
        P(),
        P(None, None, "mp"),
        P("mp", None),
        P(None, None, "mp"),
        P("mp", None),
        P(None, "mp"),
        P("mp", None),
        P(None, "mp"),
    )
    out_specs = (
        P(both, None),
        P(both, None),
        P(both, None),
        P(),
        P(),
        P(None, "dp", "mp"),
        P("mp", "dp"),
        P(None, "dp", "mp"),
        P("mp", "dp"),
        P("dp", "mp"),
        P("mp", "dp"),
    )
    return jax.shard_map(local, mesh=mesh, in_specs=in_specs, out_specs=out_specs, check_vma=False)
```

```python
from functools import partial

import jax
import jax.numpy as jnp
import numpy as np
from jax import lax
from jax.experimental import pallas as pl
from jax.experimental.pallas import tpu as pltpu
from jax.sharding import PartitionSpec as P

HEAD_DIM = 64
MAX_DIST = 128
EPS = 1e-06
MASKED = -1e30
TILE = 256
F32 = jnp.float32
BF16 = jnp.bfloat16
VMEM_LIMIT = 56 * 1024 * 1024


def bucket_edges(buckets, distance):
    exact_span = buckets // 2
    edge_list = []
    for offset in range(1, 4 * distance):
        if offset < exact_span:
            bucket_now = offset
        else:
            log_ratio = np.log(offset / exact_span) / np.log(distance / exact_span)
            bucket_now = min(buckets - 1, exact_span + int(log_ratio * (buckets - exact_span)))
        while len(edge_list) < bucket_now:
            edge_list.append(offset)
    return np.array(edge_list, dtype=np.int32)


def dot(a, b):
    return jnp.dot(a, b, preferred_element_type=F32)


def dot_nt(a, b):
    return lax.dot_general(a, b, (((1,), (1,)), ((), ())), preferred_element_type=F32)


def dot_tn(a, b):
    return lax.dot_general(a, b, (((0,), (0,)), ((), ())), preferred_element_type=F32)


def rms_scale(values):
    return lax.rsqrt(jnp.mean(values * values, axis=-1, keepdims=True) + EPS)


def norm_back(values, gain_row, upstream):
    scale = rms_scale(values)
    scaled = gain_row * upstream
    back = scale * scaled - values * (
        scale * scale * scale * jnp.mean(scaled * values, axis=-1, keepdims=True)
    )
    return back, upstream * values * scale


def call(body, outs, args, flops=0, moved=None, transcendentals=0, scratch=(), smem=()):
    size = sum(a.size * a.dtype.itemsize for a in args) + sum(
        o.size * o.dtype.itemsize for o in outs
    )
    return pl.pallas_call(
        body,
        out_shape=outs,
        in_specs=[
            pl.BlockSpec(memory_space=pltpu.SMEM if i in smem else pltpu.VMEM)
            for i in range(len(args))
        ],
        out_specs=[pl.BlockSpec(memory_space=pltpu.VMEM) for _ in outs],
        scratch_shapes=list(scratch),
        compiler_params=pltpu.CompilerParams(vmem_limit_bytes=VMEM_LIMIT),
        cost_estimate=pl.CostEstimate(
            flops=flops, bytes_accessed=moved or size, transcendentals=transcendentals
        ),
    )(*args)


def shape(dims, dtype):
    return jax.ShapeDtypeStruct(dims, dtype)


def tables_body(vec_ref, ids_row_ref, ids_col_ref, bias_ref, mask_ref):
    heads = bias_ref.shape[0]
    row = lax.broadcasted_iota(jnp.int32, (MAX_DIST, 2 * MAX_DIST), 0)
    column = lax.broadcasted_iota(jnp.int32, (MAX_DIST, 2 * MAX_DIST), 1)
    for head in range(heads):
        line = vec_ref[head : head + 1, :]
        near = pltpu.roll(
            jnp.broadcast_to(line, (MAX_DIST, 2 * MAX_DIST)), 0, 1, stride=1, stride_axis=0
        )
        near = jnp.where(column > row + MAX_DIST, MASKED, near)
        far = jnp.broadcast_to(line[:, 2 * MAX_DIST - 1 :], (MAX_DIST, MAX_DIST))
        none = jnp.full((MAX_DIST, MAX_DIST), MASKED, F32)
        upper = jnp.concatenate([far, near, none], axis=1)
        lower = jnp.concatenate([far, far, near], axis=1)
        bias_ref[head] = jnp.concatenate([upper, lower], axis=0).astype(BF16)
    mask_ref[...] = jnp.where(ids_col_ref[...] == ids_row_ref[...], 0.0, MASKED)


def lane_half(values, which):
    lane = lax.broadcasted_iota(jnp.int32, values.shape, 1)
    keep = (lane < HEAD_DIM) if which == 0 else (lane >= HEAD_DIM)
    return jnp.where(keep, values, jnp.zeros_like(values))


def attend(q_ref, k_ref, v_ref, mask_ref, bias_ref, probs_ref, mix_ref):
    rows, columns = q_ref.shape
    causal = bias_ref is not None
    for tile in range(rows // TILE):
        here = slice(tile * TILE, (tile + 1) * TILE)
        reach = (tile + 1) * TILE if causal else rows
        for pair in range(columns // (2 * HEAD_DIM)):
            lanes = slice(pair * 2 * HEAD_DIM, (pair + 1) * 2 * HEAD_DIM)
            q, k, v = q_ref[here, lanes], k_ref[:reach, lanes], v_ref[:reach, lanes]
            mixed = None
            for which in range(2):
                head = 2 * pair + which
                scores = dot_nt(lane_half(q, which), k) + mask_ref[here, :reach]
                if causal:
                    scores = scores + bias_ref[head, :, rows - reach :].astype(F32)
                peak = jnp.max(scores, axis=-1, keepdims=True)
                weights = jnp.exp(scores - peak)
                total = jnp.sum(weights, axis=-1, keepdims=True)
                probs = (weights * (1.0 / total)).astype(BF16)
                probs_ref[head, here, :reach] = probs
                part = dot(probs, lane_half(v, which))
                mixed = part if mixed is None else mixed + part
            mix_ref[here, lanes] = mixed.astype(BF16)


def attend_back(
    q_ref, k_ref, v_ref, probs_ref, d_mix_ref, dq_ref, dk_ref, dv_ref, diag_ref, causal
):
    rows, columns = q_ref.shape
    for pair in range(columns // (2 * HEAD_DIM)):
        lanes = slice(pair * 2 * HEAD_DIM, (pair + 1) * 2 * HEAD_DIM)
        q_turned = q_ref[:, lanes].T
        d_turned = d_mix_ref[:, lanes].T
        dk_turned, dv_turned = [], []
        near = [None, None]
        for which in range(2):
            head = 2 * pair + which
            halves = slice(which * HEAD_DIM, (which + 1) * HEAD_DIM)
            dk_sum = dv_sum = None
            grown = None
            for tile in reversed(range(rows // TILE)):
                here = slice(tile * TILE, (tile + 1) * TILE)
                reach = (tile + 1) * TILE if causal else rows
                k, v = k_ref[:reach, lanes], v_ref[:reach, lanes]
                probs16 = probs_ref[head, here, :reach]
                probs = probs16.astype(F32)
                d_probs = dot_nt(lane_half(d_mix_ref[here, lanes], which), v)
                product = probs * d_probs
                delta = jnp.sum(product, axis=-1, keepdims=True)
                d_scores = product - probs * delta
                d_scores16 = d_scores.astype(BF16)
                dq = dot(d_scores16, lane_half(k, which))
                if which == 0:
                    near[tile] = dq
                else:
                    dq_ref[here, lanes] = (near[tile] + dq).astype(BF16)
                dk = dot(q_turned[halves, here], d_scores16)
                dv = dot(d_turned[halves, here], probs16)
                if causal and reach < rows:
                    pad = jnp.zeros((HEAD_DIM, rows - reach), F32)
                    dk = jnp.concatenate([dk, pad], axis=1)
                    dv = jnp.concatenate([dv, pad], axis=1)
                dk_sum = dk if dk_sum is None else dk_sum + dk
                dv_sum = dv if dv_sum is None else dv_sum + dv
                if causal:
                    kept = d_scores16.astype(F32)
                    if reach < rows:
                        kept = jnp.concatenate(
                            [jnp.zeros((TILE, rows - reach), F32), kept], axis=1
                        )
                    grown = kept if grown is None else grown + kept
            dk_turned.append(dk_sum)
            dv_turned.append(dv_sum)
            if causal:
                d = MAX_DIST
                close = grown[:d, d : 3 * d] + grown[d:, 2 * d :]
                row = lax.broadcasted_iota(jnp.int32, close.shape, 0)
                turned, shift = close, 1
                while shift < d:
                    moved = pltpu.roll(turned, 2 * d - shift, 1)
                    turned = jnp.where((row & shift) > 0, moved, turned)
                    shift *= 2
                far = jnp.sum(grown[:d, :d] + grown[d:, :d] + grown[d:, d : 2 * d], axis=0)
                line = jnp.sum(turned, axis=0, keepdims=True)
                diag_ref[head : head + 1, : 2 * d] = line
                diag_ref[head : head + 1, 2 * d :] = far[None]
        dk_ref[:, lanes] = jnp.concatenate(dk_turned, axis=0).T.astype(BF16)
        dv_ref[:, lanes] = jnp.concatenate(dv_turned, axis=0).T.astype(BF16)


def self_forward_body(
    x_ref, gain_ref, w_ref, wo_ref, mask_ref, bias_ref,
    n_ref, q_ref, k_ref, v_ref, probs_ref, mix_ref, part_ref,
):
    x = x_ref[...].astype(F32)
    n_ref[...] = (x * rms_scale(x) * gain_ref[...]).astype(BF16)
    for i, out in enumerate((q_ref, k_ref, v_ref)):
        out[...] = dot(n_ref[...], w_ref[i]).astype(BF16)
    attend(q_ref, k_ref, v_ref, mask_ref, bias_ref, probs_ref, mix_ref)
    part_ref[...] = dot(mix_ref[...], wo_ref[...]).astype(BF16)


def cross_forward_body(
    x_ref, a_ref, b_ref, gain_ref, wq_ref, wo_ref, k_ref, v_ref, mask_ref,
    h_ref, n_ref, q_ref, probs_ref, mix_ref, part_ref,
):
    h_ref[...] = x_ref[...].astype(F32) + (a_ref[...].astype(F32) + b_ref[...].astype(F32))
    h = h_ref[...]
    n_ref[...] = (h * rms_scale(h) * gain_ref[...]).astype(BF16)
    q_ref[...] = dot(n_ref[...], wq_ref[...]).astype(BF16)
    attend(q_ref, k_ref, v_ref, mask_ref, None, probs_ref, mix_ref)
    part_ref[...] = dot(mix_ref[...], wo_ref[...]).astype(BF16)


def gelu_pair(v):
    scale = float(np.sqrt(2 / np.pi))
    square = v * v
    t = jnp.tanh(scale * (v + 0.044715 * (square * v)))
    half = 0.5 * (1.0 + t)
    slope = half + 0.5 * v * (1.0 - t * t) * (scale * (1.0 + 3 * 0.044715 * square))
    return v * half, slope


def own_rows(core_ref, half):
    return pl.ds(pl.multiple_of(core_ref[0] * half, half), half)


def their_rows(core_ref, half):
    return pl.ds(pl.multiple_of((1 - core_ref[0]) * half, half), half)


def ff_body(
    core_ref, h_ref, a_ref, b_ref, gain_ref, og_ref, win_ref, wout_ref,
    h2_ref, n_ref, act_ref, d_pre_ref, base_ref, both_ref, out_sum, back_sum,
):
    step, steps = pl.program_id(0), pl.num_programs(0)
    rows, half = h_ref.shape[0], h_ref.shape[0] // 2

    @pl.when(step == 0)
    def start():
        h = h_ref[...] + (a_ref[...].astype(F32) + b_ref[...].astype(F32))
        h2_ref[...] = h
        n_ref[...] = (h * rms_scale(h) * gain_ref[...]).astype(BF16)
        out_sum[...] = jnp.zeros_like(out_sum)
        back_sum[...] = jnp.zeros_like(back_sum)

    value, slope = gelu_pair(dot(n_ref[...], win_ref[...]))
    act_ref[...] = value.astype(BF16)
    d_pre_ref[...] = (dot_nt(og_ref[...], wout_ref[...]) * slope).astype(BF16)
    out_sum[...] += dot(act_ref[...], wout_ref[...])
    back_sum[...] += dot_nt(d_pre_ref[...], win_ref[...])

    @pl.when(step == steps - 1)
    def end():
        own, theirs = own_rows(core_ref, half), their_rows(core_ref, half)
        base_ref[...] = h2_ref[own, :] + out_sum[own, :]
        both_ref[:rows] = back_sum[...].astype(BF16)
        both_ref[rows:] = out_sum[theirs, :].astype(BF16)


def ff_phase(core, h, a, b, gain, og, win, wout):
    rows, width = h.shape
    units = win.shape[1]
    half = rows // 2
    block = 512
    whole = pl.BlockSpec((rows, width), lambda i: (0, 0))
    tile = pl.BlockSpec((rows, block), lambda i: (0, i))
    return pl.pallas_call(
        ff_body,
        grid=(units // block,),
        in_specs=[
            pl.BlockSpec(memory_space=pltpu.SMEM),
            whole, whole, whole,
            pl.BlockSpec((1, width), lambda i: (0, 0)),
            whole,
            pl.BlockSpec((width, block), lambda i: (0, i)),
            pl.BlockSpec((block, width), lambda i: (i, 0)),
        ],
        out_specs=[
            whole, whole, tile, tile,
            pl.BlockSpec((half, width), lambda i: (0, 0)),
            pl.BlockSpec((rows + half, width), lambda i: (0, 0)),
        ],
        out_shape=[
            shape((rows, width), F32),
            shape((rows, width), BF16),
            shape((rows, units), BF16),
            shape((rows, units), BF16),
            shape((half, width), F32),
            shape((rows + half, width), BF16),
        ],
        scratch_shapes=[pltpu.VMEM((rows, width), F32), pltpu.VMEM((rows, width), F32)],
        compiler_params=pltpu.CompilerParams(
            vmem_limit_bytes=VMEM_LIMIT, dimension_semantics=("arbitrary",)
        ),
        cost_estimate=pl.CostEstimate(
            flops=8 * rows * width * units,
            bytes_accessed=4 * width * units + 8 * rows * units,
            transcendentals=rows * units,
        ),
    )(core, h, a, b, gain, og, win, wout)


def gain_sum(core_ref, dgain):
    row = lax.broadcasted_iota(jnp.int32, dgain.shape, 0)
    half = dgain.shape[0] // 2
    mine = (row >= core_ref[0] * half) & (row < (core_ref[0] + 1) * half)
    return jnp.sum(jnp.where(mine, dgain, 0.0), axis=0, keepdims=True)


def cross_back_body(
    core_ref, h_ref, up_ref, a_ref, b_ref, base_ref, gain_ref, wq_ref, wk_ref, wv_ref, wo_ref,
    q_ref, k_ref, v_ref, probs_ref,
    g_ref, g16_ref, dq_ref, dk_ref, dv_ref, both_ref, dmem_ref, dgain_ref, out_ref,
    d_mix_ref, dmem_sum,
):
    rows, half = h_ref.shape[0], h_ref.shape[0] // 2
    out_ref[...] = (base_ref[...] + b_ref[rows:].astype(F32)).astype(BF16)
    up = a_ref[:rows].astype(F32) + b_ref[:rows].astype(F32)
    dv, dgain = norm_back(h_ref[...], gain_ref[...], up)
    dgain_ref[...] = gain_sum(core_ref, dgain)
    g = up_ref[...].astype(F32) + dv
    g_ref[...] = g
    g16_ref[...] = g.astype(BF16)
    d_mix_ref[...] = dot_nt(g16_ref[...], wo_ref[...]).astype(BF16)
    attend_back(
        q_ref, k_ref, v_ref, probs_ref, d_mix_ref, dq_ref, dk_ref, dv_ref, None, False
    )
    both_ref[:rows] = dot_nt(dq_ref[...], wq_ref[...]).astype(BF16)
    dmem_sum[...] = dot_nt(dk_ref[...], wk_ref[...]) + dot_nt(dv_ref[...], wv_ref[...])
    dmem_ref[...] = dmem_sum[own_rows(core_ref, half), :]
    both_ref[rows:] = dmem_sum[their_rows(core_ref, half), :].astype(BF16)


def self_back_body(
    core_ref, h_ref, up_ref, a_ref, b_ref, gain_ref, w_ref, wo_ref,
    q_ref, k_ref, v_ref, probs_ref,
    g_ref, g16_ref, dq_ref, dk_ref, dv_ref, dn_ref, sent_ref, dgain_ref, diag_ref,
    d_mix_ref, total,
):
    rows, half = h_ref.shape[0], h_ref.shape[0] // 2
    own, theirs = own_rows(core_ref, half), their_rows(core_ref, half)
    up = a_ref[:rows].astype(F32) + b_ref[:rows].astype(F32)
    dv, dgain = norm_back(h_ref[...], gain_ref[...], up)
    dgain_ref[...] = gain_sum(core_ref, dgain)
    total[...] = up_ref[...] + dv
    g_ref[...] = total[own, :]
    g16_ref[...] = total[...].astype(BF16)
    d_mix_ref[...] = dot_nt(g16_ref[...], wo_ref[...]).astype(BF16)
    attend_back(
        q_ref, k_ref, v_ref, probs_ref, d_mix_ref, dq_ref, dk_ref, dv_ref, diag_ref, True
    )
    total[...] = (
        dot_nt(dq_ref[...], w_ref[0]) + dot_nt(dk_ref[...], w_ref[1]) + dot_nt(dv_ref[...], w_ref[2])
    )
    dn_ref[...] = total[own, :]
    sent_ref[...] = total[theirs, :].astype(BF16)


def last_body(
    x_ref, g_ref, a_ref, b_ref, gain_ref, slots_ref, packed_ref, dgain_ref,
):
    dv, dgain = norm_back(
        x_ref[...].astype(F32), gain_ref[...], a_ref[...] + b_ref[...].astype(F32)
    )
    dgain_ref[...] = jnp.sum(dgain, axis=0, keepdims=True)
    packed_ref[...] = dot(slots_ref[...], (g_ref[...] + dv).astype(BF16)).astype(BF16)


def weight_body(plan, n_in, *refs):
    ins, outs = refs[: n_in], refs[n_in : n_in + 4]
    turned = refs[n_in + 4]
    perms = ins[:2]
    half = turned.shape[0] // 2
    for side in range(2):
        keep, send = outs[2 * side], outs[2 * side + 1]
        at = 0
        for left, rights in plan[side]:
            turned[...] = dot_nt(perms[side][...], ins[left][...]).astype(BF16)
            for right in rights:
                columns = ins[right].shape[1]
                send[:, at : at + columns] = dot(turned[half:], ins[right][...]).astype(BF16)
                keep[:, at : at + columns] = dot(turned[:half], ins[right][...]).astype(BF16)
                at += columns


def weight_halves(perm_a, perm_b, side_a, side_b):
    args = [perm_a, perm_b]
    plan, sizes = [], []
    flops = 0
    for side in (side_a, side_b):
        steps, total = [], 0
        for left, rights in side:
            args.append(left)
            at = len(args) - 1
            steps.append((at, tuple(range(len(args), len(args) + len(rights)))))
            args.extend(rights)
            total += sum(r.shape[1] for r in rights)
            flops += 2 * left.size * left.shape[1]
        plan.append(tuple(steps))
        sizes.append(total)
        flops += 2 * side[0][0].size * total
    rows, width = side_a[0][0].shape
    outs = [shape((width // 2, n), BF16) for n in sizes for _ in range(2)]
    return call(
        partial(weight_body, tuple(plan), len(args)), outs, args, flops=flops,
        scratch=[pltpu.VMEM((width, rows), BF16)],
    )


def add_split_body(*refs):
    count = len(refs) // 4
    for i in range(count):
        kept, arrived = refs[2 * i], refs[2 * i + 1]
        keep, send = refs[2 * count + 2 * i], refs[2 * count + 2 * i + 1]
        half = keep.shape[0]
        send[...] = (kept[half:].astype(F32) + arrived[half:].astype(F32)).astype(BF16)
        keep[...] = (kept[:half].astype(F32) + arrived[:half].astype(F32)).astype(BF16)


def add_join_body(kept_a, arrived_a, kept_b, arrived_b, keep, send):
    half, edge = keep.shape[0], kept_a.shape[1]
    for kept, arrived, columns in (
        (kept_a, arrived_a, slice(0, edge)),
        (kept_b, arrived_b, slice(edge, keep.shape[1])),
    ):
        send[:, columns] = (kept[half:].astype(F32) + arrived[half:].astype(F32)).astype(BF16)
        keep[:, columns] = (kept[:half].astype(F32) + arrived[:half].astype(F32)).astype(BF16)


def halves_sum(halves, order, peers):
    keep_a, send_a, keep_b, send_b = halves
    first, second = order[0], order[1]
    arrived_a = neighbour(send_a, first, peers)
    arrived_b = neighbour(send_b, second, peers)

    def pieces(rows, columns):
        return [shape((rows, columns), BF16)] * 2

    half = keep_a.shape[0] // 2
    keep_a, send_a, keep_b, send_b = call(
        add_split_body,
        pieces(half, keep_a.shape[1]) + pieces(half, keep_b.shape[1]),
        [keep_a, arrived_a, keep_b, arrived_b],
    )
    arrived_a = neighbour(send_a, second, peers)
    arrived_b = neighbour(send_b, first, peers)
    half //= 2
    keep, send = call(
        add_join_body,
        pieces(half, keep_a.shape[1] + keep_b.shape[1]),
        [keep_a, arrived_a, keep_b, arrived_b],
    )
    rest = order[2:]
    for place, bit in enumerate(rest):
        arrived = neighbour(send, bit, peers)
        if place == len(rest) - 1:
            return keep.astype(F32) + arrived.astype(F32)
        half = keep.shape[0] // 2
        if half % 16 == 0:
            keep, send = call(add_split_body, pieces(half, keep.shape[1]), [keep, arrived])
        else:
            total = (keep.astype(F32) + arrived.astype(F32)).astype(BF16)
            keep, send = total[:half], total[half:]


def slot_matrix(counts, capacity, row_total):
    peers = counts.shape[0]
    order = jnp.arange(peers, dtype=jnp.int32)
    starts = jnp.sum(jnp.where(order[None, :] < order[:, None], counts[None, :], 0), axis=1)
    within = jnp.arange(capacity, dtype=jnp.int32)
    rows = jnp.where(within[None, :] < counts[:, None], starts[:, None] + within[None, :], -1)
    return (
        rows.reshape(-1)[:, None] == jnp.arange(row_total, dtype=jnp.int32)[None, :]
    ).astype(BF16)


def exchange_rows(packed, peers):
    dims = packed.shape
    blocks = packed.reshape(peers, dims[0] // peers, dims[1])
    return lax.all_to_all(blocks, "dp", split_axis=0, concat_axis=0, tiled=True).reshape(dims)


def swap(values):
    return lax.ppermute(values, "mp", [(0, 1), (1, 0)])


def neighbour(values, bit, peers):
    return lax.ppermute(values, "dp", [(i, i ^ (1 << bit)) for i in range(peers)])


def order_matrix(order, peers, me, width):
    size = width // peers
    row = lax.broadcasted_iota(jnp.int32, (width, width), 0)
    column = lax.broadcasted_iota(jnp.int32, (width, width), 1)
    block, within = row // size, row % size
    relative = jnp.zeros_like(block)
    steps = len(order)
    for position, bit in enumerate(order):
        relative = relative + (((block >> (steps - 1 - position)) & 1) << bit)
    return (column == (relative ^ me) * size + within).astype(BF16)


def local(
    hidden_in,
    memory,
    output_grad,
    segment_ids,
    route_counts,
    norm_gains,
    self_qkv,
    self_out,
    cross_qkv,
    cross_out,
    ff_in,
    ff_out,
    rel_bias,
):
    peers = lax.axis_size("dp")
    me = lax.axis_index("dp")
    core = lax.axis_index("mp")
    core_ref = core.astype(jnp.int32)[None]
    half_rows, width = hidden_in.shape
    rows = 2 * half_rows
    capacity = 2 * (half_rows // peers)
    buckets, heads = rel_bias.shape
    columns = self_out.shape[0]
    bits = peers.bit_length() - 1
    order_a = tuple(range(bits))
    order_b = (1, 0) + order_a[2:]

    def both(values):
        return lax.all_gather(values, "mp", axis=0, tiled=True)

    sent = lax.dynamic_index_in_dim(route_counts, me, 0, keepdims=False)
    taken = lax.dynamic_index_in_dim(route_counts, me, 1, keepdims=False)
    send_slots = slot_matrix(sent, capacity, half_rows)
    take_slots = slot_matrix(taken, capacity, half_rows)

    def there(values):
        arrived = exchange_rows(dot(send_slots, values).astype(BF16), peers)
        return dot_tn(take_slots, arrived).astype(BF16)

    def unpack_back(packed):
        return dot_tn(send_slots, exchange_rows(packed, peers)).astype(BF16)

    x_own = there(hidden_in)
    x = both(x_own)
    mem = both(there(memory))
    og = both(output_grad)

    perm_a = order_matrix(order_a, peers, me, width)
    perm_b = order_matrix(order_b, peers, me, width)

    gains = norm_gains.astype(F32)
    gain_one, gain_two, gain_three = gains[0:1], gains[1:2], gains[2:3]
    edges = bucket_edges(buckets, MAX_DIST)
    offset = MAX_DIST - np.arange(3 * MAX_DIST)
    bucket_of = np.where(
        (offset >= 0), np.searchsorted(edges, offset, side="right"), buckets - 1
    )
    bucket_hot = bucket_of[:, None] == np.arange(buckets)[None, :]
    lines = jnp.dot(
        bucket_hot[: 2 * MAX_DIST].astype(jnp.bfloat16), rel_bias, preferred_element_type=F32
    ).T
    bias, mask = call(
        tables_body,
        [shape((heads, TILE, rows), BF16), shape((rows, rows), F32)],
        [lines, segment_ids, segment_ids.reshape(rows, 1)],
    )
    wide, narrow = shape((rows, width), BF16), shape((rows, columns), BF16)
    wide32, gain_shape = shape((rows, width), F32), shape((1, width), F32)
    half16, half32 = shape((half_rows, width), BF16), shape((half_rows, width), F32)
    more16 = shape((rows + half_rows, width), BF16)
    probs_shape = shape((heads, rows, rows), BF16)
    square = rows * width * columns
    scores = heads * rows * rows

    n1, sq, sk, sv, self_probs, self_mix, part = call(
        self_forward_body,
        [wide, narrow, narrow, narrow, probs_shape, narrow, wide],
        [x, gain_one, self_qkv, self_out, mask, bias],
        flops=8 * square + 8 * scores * HEAD_DIM,
        transcendentals=scores,
    )
    ck, cv = (dot(mem, cross_qkv[i]).astype(BF16) for i in (1, 2))
    h1, n2, cq, cross_probs, cross_mix, part2 = call(
        cross_forward_body,
        [wide32, wide, narrow, probs_shape, narrow, wide],
        [x, part, swap(part), gain_two, cross_qkv[0], cross_out, ck, cv, mask],
        flops=4 * square + 8 * scores * HEAD_DIM,
        transcendentals=scores,
    )
    h2, n3, act, d_pre, base, pack3 = ff_phase(
        core_ref, h1, part2, swap(part2), gain_three, og, ff_in, ff_out
    )
    ff_halves = weight_halves(perm_a, perm_b, [(og, [act])], [(n3, [d_pre])])
    g2, g2s, dcq, dck, dcv, pack2, d_mem, dgain3, block_out = call(
        cross_back_body,
        [wide32, wide, narrow, narrow, narrow, more16, half32, gain_shape, half16],
        [
            core_ref, h2, og, pack3, swap(pack3), base, gain_three,
            cross_qkv[0], cross_qkv[1], cross_qkv[2], cross_out, cq, ck, cv, cross_probs,
        ],
        flops=8 * square + 14 * scores * HEAD_DIM,
        scratch=[pltpu.VMEM((rows, columns), BF16), pltpu.VMEM((rows, width), F32)],
        smem=(0,),
    )
    cross_halves = weight_halves(
        perm_a, perm_b, [(g2s, [cross_mix]), (n2, [dcq])], [(mem, [dck, dcv])]
    )
    pack2_there = swap(pack2)
    g1_own, g1s, dsq, dsk, dsv, dn1, dn1_sent, dgain2, diag = call(
        self_back_body,
        [half32, wide, narrow, narrow, narrow, half32, half16, gain_shape,
         shape((heads, 3 * MAX_DIST), F32)],
        [
            core_ref, h1, g2, pack2, pack2_there, gain_two, self_qkv, self_out,
            sq, sk, sv, self_probs,
        ],
        flops=8 * square + 14 * scores * HEAD_DIM,
        scratch=[pltpu.VMEM((rows, columns), BF16), pltpu.VMEM((rows, width), F32)],
        smem=(0,),
    )
    self_halves = weight_halves(
        perm_a, perm_b, [(g1s, [self_mix]), (n1, [dsq])], [(n1, [dsk, dsv])]
    )
    packed, dgain1 = call(
        last_body,
        [shape((take_slots.shape[0], width), BF16), gain_shape],
        [x_own, g1_own, dn1, swap(dn1_sent), gain_one, take_slots],
    )
    d_mem = (d_mem + pack2_there[rows:].astype(F32)).astype(BF16)
    memory_grad = unpack_back(dot(take_slots, d_mem).astype(BF16))
    input_grad = unpack_back(packed)

    ff_sum = halves_sum(ff_halves, order_a, peers)
    cross_sum = halves_sum(cross_halves, order_a, peers)
    self_sum = halves_sum(self_halves, order_a, peers)

    bias_part = jnp.sum(
        jnp.where(bucket_hot[:, :, None], diag.T[:, None, :], 0.0), axis=0
    )
    small = jnp.zeros((buckets, heads * 2), F32)
    small = lax.dynamic_update_slice_in_dim(small, bias_part, core * heads, 1)
    small = jnp.concatenate(
        [dgain1.reshape(-1), dgain2.reshape(-1), dgain3.reshape(-1), small.reshape(-1)]
    ).reshape(-1, 128)
    small = small + swap(small)
    for bit in order_a:
        small = small + neighbour(small, bit, peers)
    small = small.reshape(-1)
    gains_total = small[: 3 * width].reshape(3, width)
    bias_total = small[3 * width :].reshape(buckets, heads * 2)

    units = ff_out.shape[0]

    def thirds(total):
        return total[:, :columns].T, jnp.stack(
            [total[:, i * columns : (i + 1) * columns] for i in (1, 2, 3)]
        )

    cross_out_total, cross_qkv_total = thirds(cross_sum)
    self_out_total, self_qkv_total = thirds(self_sum)
    return (
        block_out,
        input_grad,
        memory_grad,
        gains_total,
        bias_total,
        self_qkv_total,
        self_out_total,
        cross_qkv_total,
        cross_out_total,
        ff_sum[:, units:],
        ff_sum[:, :units].T,
    )


def solution(mesh):
    both = ("dp", "mp")
    in_specs = (
        P(both, None),
        P(both, None),
        P(both, None),
        P("dp", None),
        P(),
        P(),
        P(None, None, "mp"),
        P("mp", None),
        P(None, None, "mp"),
        P("mp", None),
        P(None, "mp"),
        P("mp", None),
        P(None, "mp"),
    )
    out_specs = (
        P(both, None),
        P(both, None),
        P(both, None),
        P(),
        P(),
        P(None, "dp", "mp"),
        P("mp", "dp"),
        P(None, "dp", "mp"),
        P("mp", "dp"),
        P("dp", "mp"),
        P("mp", "dp"),
    )
    return jax.shard_map(local, mesh=mesh, in_specs=in_specs, out_specs=out_specs, check_vma=False)
```

```python
from functools import partial

import jax
import jax.numpy as jnp
import numpy as np
from jax import lax
from jax.experimental import pallas as pl
from jax.experimental.pallas import tpu as pltpu
from jax.sharding import PartitionSpec as P

HEAD_DIM = 64
MAX_DIST = 128
EPS = 1e-06
MASKED = -1e30
TILE = 256
F32 = jnp.float32
BF16 = jnp.bfloat16
VMEM_LIMIT = 24 * 1024 * 1024
WEIGHT = 3 * 10**10
LIGHT = 10**6
AFTER_SELF = 10**10
FF_STEPS = 3


def bucket_edges(buckets, distance):
    exact_span = buckets // 2
    edge_list = []
    for offset in range(1, 4 * distance):
        if offset < exact_span:
            bucket_now = offset
        else:
            log_ratio = np.log(offset / exact_span) / np.log(distance / exact_span)
            bucket_now = min(buckets - 1, exact_span + int(log_ratio * (buckets - exact_span)))
        while len(edge_list) < bucket_now:
            edge_list.append(offset)
    return np.array(edge_list, dtype=np.int32)


def dot(a, b):
    return jnp.dot(a, b, preferred_element_type=F32)


def dot_nt(a, b):
    return lax.dot_general(a, b, (((1,), (1,)), ((), ())), preferred_element_type=F32)


def dot_tn(a, b):
    return lax.dot_general(a, b, (((0,), (0,)), ((), ())), preferred_element_type=F32)


def rms_scale(values):
    return lax.rsqrt(jnp.mean(values * values, axis=-1, keepdims=True) + EPS)


def norm_back(values, gain_row, upstream):
    scale = rms_scale(values)
    scaled = gain_row * upstream
    back = scale * scaled - values * (
        scale * scale * scale * jnp.mean(scaled * values, axis=-1, keepdims=True)
    )
    return back, upstream * values * scale


class Far:
    def __init__(self, array, axis=0, count=1):
        self.array, self.axis, self.count = array, axis, count
        self.shape, self.dtype = array.shape, array.dtype


def part(ref, axis, count, i):
    size = ref.shape[axis] // count
    index = tuple(
        pl.ds(i * size, size) if at == axis else slice(None) for at in range(len(ref.shape))
    )
    return ref.at[index]


class Inbound:
    def __init__(self, ref, copies):
        self.ref, self.copies, self.shape = ref, copies, ref.shape
        self.waiting = set(range(len(copies)))

    def need(self, i):
        if i in self.waiting:
            self.waiting.discard(i)
            self.copies[i].wait()

    def __getitem__(self, index):
        for i in range(len(self.copies)):
            self.need(i)
        return self.ref[index]


class Outbound:
    def __init__(self, ref, copies):
        self.ref, self.copies, self.shape, self.dtype = ref, copies, ref.shape, ref.dtype
        self.pending, self.flying = set(range(len(copies))), set()

    def __getitem__(self, index):
        return self.ref[index]

    def __setitem__(self, index, value):
        self.ref[index] = value

    def flush(self, i=None):
        for at in sorted(self.pending) if i is None else [i]:
            self.pending.discard(at)
            self.flying.add(at)
            self.copies[at].start()

    def end(self):
        self.flush()
        for at in sorted(self.flying):
            self.copies[at].wait()


def need(ref, i):
    if isinstance(ref, Inbound):
        ref.need(i % len(ref.copies))
        return ref.ref
    return ref


def flush(*refs, i=None):
    for ref in refs:
        if isinstance(ref, Outbound):
            ref.flush(i)


def call(body, outs, args, flops=0, scratch=(), smem=(), after=(), weight=WEIGHT):
    count, extra, made = len(args), len(after), len(outs)
    far_in = [i for i in range(count) if isinstance(args[i], Far)]
    far_out = [i for i in range(made) if isinstance(outs[i], Far)]
    arrays = [a.array if isinstance(a, Far) else a for a in args]
    shapes = [o.array if isinstance(o, Far) else o for o in outs]
    size = sum(a.size * a.dtype.itemsize for a in arrays + shapes)
    sems = sum(args[i].count for i in far_in) + sum(outs[i].count for i in far_out)

    given = [
        pltpu.with_memory_space_constraint(a, pltpu.HBM) if i in far_in else a
        for i, a in enumerate(arrays)
    ]

    def kernel(*refs):
        ins, refs = list(refs[:count]), refs[count + extra :]
        to, refs = list(refs[:made]), refs[made:]
        rooms, refs = refs[: len(far_in)], refs[len(far_in) :]
        shelves, rest = refs[: len(far_out)], refs[len(far_out) :]
        if sems:
            sem, rest = rest[0], rest[1:]
        at = 0
        for i, room in zip(far_in, rooms):
            copies = []
            for j in range(args[i].count):
                cut = (args[i].axis, args[i].count, j)
                copies.append(
                    pltpu.make_async_copy(part(ins[i], *cut), part(room, *cut), sem.at[at])
                )
                copies[-1].start()
                at += 1
            ins[i] = Inbound(room, copies)
        for i, shelf in zip(far_out, shelves):
            copies = []
            for j in range(outs[i].count):
                cut = (outs[i].axis, outs[i].count, j)
                copies.append(
                    pltpu.make_async_copy(part(shelf, *cut), part(to[i], *cut), sem.at[at])
                )
                at += 1
            to[i] = Outbound(shelf, copies)
        body(*ins, *to, *rest)
        for i in far_in:
            for j in sorted(ins[i].waiting):
                ins[i].need(j)
        for i in far_out:
            to[i].flush()
        for i in far_out:
            to[i].end()

    hbm, vmem = pl.BlockSpec(memory_space=pltpu.HBM), pl.BlockSpec(memory_space=pltpu.VMEM)
    return pl.pallas_call(
        kernel,
        out_shape=[
            (pltpu.HBM if i in far_out else pltpu.VMEM)(o.shape, o.dtype) for i, o in enumerate(shapes)
        ],
        in_specs=[
            pl.BlockSpec(memory_space=pltpu.SMEM) if i in smem else hbm if i in far_in else vmem
            for i in range(count)
        ]
        + [hbm] * extra,
        out_specs=[hbm if i in far_out else vmem for i in range(made)],
        scratch_shapes=[pltpu.VMEM(arrays[i].shape, arrays[i].dtype) for i in far_in]
        + [pltpu.VMEM(shapes[i].shape, shapes[i].dtype) for i in far_out]
        + ([pltpu.SemaphoreType.DMA((sems,))] if sems else [])
        + list(scratch),
        compiler_params=pltpu.CompilerParams(vmem_limit_bytes=VMEM_LIMIT),
        cost_estimate=pl.CostEstimate(
            flops=int(weight), bytes_accessed=0, transcendentals=0
        ),
    )(*given, *(pltpu.with_memory_space_constraint(a, pltpu.HBM) for a in after))


def shape(dims, dtype):
    return jax.ShapeDtypeStruct(dims, dtype)


def own_rows(core_ref, half):
    return pl.ds(pl.multiple_of(core_ref[0] * half, half), half)


def their_rows(core_ref, half):
    return pl.ds(pl.multiple_of((1 - core_ref[0]) * half, half), half)


def tables_body(vec_ref, ids_ref, bias_ref, mask_ref):
    heads, rows = bias_ref.shape[0], mask_ref.shape[0]
    row = lax.broadcasted_iota(jnp.int32, (MAX_DIST, 2 * MAX_DIST), 0)
    column = lax.broadcasted_iota(jnp.int32, (MAX_DIST, 2 * MAX_DIST), 1)
    for head in range(heads):
        line = vec_ref[head : head + 1, :]
        near = pltpu.roll(
            jnp.broadcast_to(line, (MAX_DIST, 2 * MAX_DIST)), 0, 1, stride=1, stride_axis=0
        )
        near = jnp.where(column > row + MAX_DIST, MASKED, near)
        far = jnp.broadcast_to(line[:, 2 * MAX_DIST - 1 :], (MAX_DIST, MAX_DIST))
        none = jnp.full((MAX_DIST, MAX_DIST), MASKED, F32)
        upper = jnp.concatenate([far, near, none], axis=1)
        lower = jnp.concatenate([far, far, near], axis=1)
        bias_ref[head] = jnp.concatenate([upper, lower], axis=0).astype(BF16)
    ids = ids_ref[...].astype(F32)
    down = jnp.broadcast_to(ids, (128, rows)).T[:, :1]
    mask_ref[...] = jnp.where(down == ids, 0.0, MASKED)


def slot_line(count_of, peers, capacity):
    lane = lax.broadcasted_iota(jnp.int32, (1, peers * capacity), 1)
    line = jnp.full_like(lane, -1)
    start = jnp.int32(0)
    for peer in range(peers):
        count, within = count_of(peer), lane - peer * capacity
        line = jnp.where((within >= 0) & (within < count), start + within, line)
        start = start + count
    return line


def rows_of(line, rows):
    row = lax.broadcasted_iota(jnp.int32, (rows, line.shape[1]), 0)
    return (line == row).astype(BF16)


def pack_body(counts_ref, me_ref, a_ref, b_ref, packed_ref, sent_ref, taken_ref):
    peers, (half, width) = counts_ref.shape[0], a_ref.shape
    capacity = packed_ref.shape[0] // peers
    sent = slot_line(lambda o: counts_ref[me_ref[0], o], peers, capacity)
    sent_ref[...] = sent
    taken_ref[...] = slot_line(lambda s: counts_ref[s, me_ref[0]], peers, capacity)
    slots = rows_of(sent, half)
    packed_ref[:, :width] = dot_tn(slots, a_ref[...]).astype(BF16)
    packed_ref[:, width:] = dot_tn(slots, b_ref[...]).astype(BF16)


def pack_sum_body(line_ref, a_ref, b_ref, packed_ref):
    half = a_ref.shape[0]
    skip = b_ref.shape[0] - half
    rows = (a_ref[...] + b_ref[skip:].astype(F32)).astype(BF16)
    packed_ref[...] = dot_tn(rows_of(line_ref[...], half), rows).astype(BF16)


def unpack_body(line_ref, packed_ref, rows_ref):
    rows_ref[...] = dot(rows_of(line_ref[...], rows_ref.shape[0]), packed_ref[...]).astype(BF16)


def lane_half(values, which):
    lane = lax.broadcasted_iota(jnp.int32, values.shape, 1)
    keep = (lane < HEAD_DIM) if which == 0 else (lane >= HEAD_DIM)
    return jnp.where(keep, values, jnp.zeros_like(values))


def attend(q_ref, k_ref, v_ref, mask_ref, bias_ref, probs_ref, mix_ref):
    rows, columns = q_ref.shape
    causal = bias_ref is not None
    for pair in range(columns // (2 * HEAD_DIM)):
        lanes = slice(pair * 2 * HEAD_DIM, (pair + 1) * 2 * HEAD_DIM)
        for tile in range(rows // TILE):
            here = slice(tile * TILE, (tile + 1) * TILE)
            reach = (tile + 1) * TILE if causal else rows
            q, k, v = q_ref[here, lanes], k_ref[:reach, lanes], v_ref[:reach, lanes]
            mixed = None
            for which in range(2):
                head = 2 * pair + which
                scores = dot_nt(lane_half(q, which), k) + mask_ref[here, :reach]
                if causal:
                    bias = need(bias_ref, head)[head, :, rows - reach :]
                    scores = scores + bias.astype(F32)
                peak = jnp.max(scores, axis=-1, keepdims=True)
                weights = jnp.exp(scores - peak)
                total = jnp.sum(weights, axis=-1, keepdims=True)
                probs = (weights * (1.0 / total)).astype(BF16)
                probs_ref[head, here, :reach] = probs
                each = dot(probs, lane_half(v, which))
                mixed = each if mixed is None else mixed + each
            mix_ref[here, lanes] = mixed.astype(BF16)
        flush(probs_ref, i=2 * pair)
        flush(probs_ref, i=2 * pair + 1)
    flush(mix_ref)


def attend_back(
    q_ref, k_ref, v_ref, probs_ref, d_mix_ref, dq_ref, dk_ref, dv_ref, diag_ref, causal
):
    rows, columns = q_ref.shape
    for pair in range(columns // (2 * HEAD_DIM)):
        lanes = slice(pair * 2 * HEAD_DIM, (pair + 1) * 2 * HEAD_DIM)
        q_turned = q_ref[:, lanes].T
        d_turned = d_mix_ref[:, lanes].T
        dk_turned, dv_turned = [], []
        near = [None, None]
        for which in range(2):
            head = 2 * pair + which
            halves = slice(which * HEAD_DIM, (which + 1) * HEAD_DIM)
            dk_sum = dv_sum = None
            grown = None
            for tile in reversed(range(rows // TILE)):
                here = slice(tile * TILE, (tile + 1) * TILE)
                reach = (tile + 1) * TILE if causal else rows
                k, v = k_ref[:reach, lanes], v_ref[:reach, lanes]
                probs16 = need(probs_ref, head)[head, here, :reach]
                probs = probs16.astype(F32)
                d_probs = dot_nt(lane_half(d_mix_ref[here, lanes], which), v)
                product = probs * d_probs
                delta = jnp.sum(product, axis=-1, keepdims=True)
                d_scores = product - probs * delta
                d_scores16 = d_scores.astype(BF16)
                dq = dot(d_scores16, lane_half(k, which))
                if which == 0:
                    near[tile] = dq
                else:
                    dq_ref[here, lanes] = (near[tile] + dq).astype(BF16)
                dk = dot(q_turned[halves, here], d_scores16)
                dv = dot(d_turned[halves, here], probs16)
                if causal and reach < rows:
                    pad = jnp.zeros((HEAD_DIM, rows - reach), F32)
                    dk = jnp.concatenate([dk, pad], axis=1)
                    dv = jnp.concatenate([dv, pad], axis=1)
                dk_sum = dk if dk_sum is None else dk_sum + dk
                dv_sum = dv if dv_sum is None else dv_sum + dv
                if causal:
                    kept = d_scores16.astype(F32)
                    if reach < rows:
                        kept = jnp.concatenate(
                            [jnp.zeros((TILE, rows - reach), F32), kept], axis=1
                        )
                    grown = kept if grown is None else grown + kept
            dk_turned.append(dk_sum)
            dv_turned.append(dv_sum)
            if causal:
                d = MAX_DIST
                close = grown[:d, d : 3 * d] + grown[d:, 2 * d :]
                row = lax.broadcasted_iota(jnp.int32, close.shape, 0)
                turned, shift = close, 1
                while shift < d:
                    moved = pltpu.roll(turned, 2 * d - shift, 1)
                    turned = jnp.where((row & shift) > 0, moved, turned)
                    shift *= 2
                far = jnp.sum(grown[:d, :d] + grown[d:, :d] + grown[d:, d : 2 * d], axis=0)
                line = jnp.sum(turned, axis=0, keepdims=True)
                spread = jnp.concatenate([line, far[None]], axis=1)
                diag_ref[head] = jnp.broadcast_to(spread, (8, 3 * d))
        dk_ref[:, lanes] = jnp.concatenate(dk_turned, axis=0).T.astype(BF16)
        dv_ref[:, lanes] = jnp.concatenate(dv_turned, axis=0).T.astype(BF16)


def self_forward_body(
    core_ref, own_ref, other_ref, gain_ref, w_ref, mask_ref, bias_ref, wo_ref,
    x_ref, nt_ref, q_ref, k_ref, v_ref, probs_ref, mix_ref, part_ref, n_ref,
):
    half, width = own_ref.shape[0], gain_ref.shape[1]
    x_ref[own_rows(core_ref, half), :] = own_ref[:, :width]
    x_ref[their_rows(core_ref, half), :] = other_ref[:, :width]
    flush(x_ref)
    x = x_ref[...].astype(F32)
    n_ref[...] = (x * rms_scale(x) * gain_ref[...]).astype(BF16)
    for i, out in enumerate((q_ref, k_ref, v_ref)):
        out[...] = dot(n_ref[...], need(w_ref, i)[i]).astype(BF16)
    nt_ref[...] = n_ref[...].T
    flush(q_ref, k_ref, v_ref, nt_ref)
    attend(q_ref, k_ref, v_ref, mask_ref, bias_ref, probs_ref, mix_ref)
    part_ref[...] = dot(mix_ref[...], wo_ref[...]).astype(BF16)


def keys_body(core_ref, own_ref, other_ref, w_ref, k_ref, v_ref, memt_ref, mem_ref):
    half, width = own_ref.shape[0], w_ref.shape[1]
    mem_ref[own_rows(core_ref, half), :] = own_ref[:, width:]
    mem_ref[their_rows(core_ref, half), :] = other_ref[:, width:]
    for i, out in ((1, k_ref), (2, v_ref)):
        out[...] = dot(mem_ref[...], need(w_ref, i)[i]).astype(BF16)
    memt_ref[...] = mem_ref[...].T


def cross_forward_body(
    a_ref, b_ref, x_ref, gain_ref, w_ref, k_ref, mask_ref, v_ref, wo_ref,
    h_ref, h_far_ref, nt_ref, q_ref, probs_ref, mix_ref, part_ref, n_ref,
):
    h_ref[...] = x_ref[...].astype(F32) + (a_ref[...].astype(F32) + b_ref[...].astype(F32))
    h_far_ref[...] = h_ref[...]
    flush(h_far_ref)
    h = h_ref[...]
    n_ref[...] = (h * rms_scale(h) * gain_ref[...]).astype(BF16)
    q_ref[...] = dot(n_ref[...], need(w_ref, 0)[0]).astype(BF16)
    nt_ref[...] = n_ref[...].T
    flush(q_ref, nt_ref)
    attend(q_ref, k_ref, v_ref, mask_ref, None, probs_ref, mix_ref)
    part_ref[...] = dot(mix_ref[...], wo_ref[...]).astype(BF16)


def gelu_pair(v):
    scale = float(np.sqrt(2 / np.pi))
    square = v * v
    t = jnp.tanh(scale * (v + 0.044715 * (square * v)))
    half = 0.5 * (1.0 + t)
    slope = half + 0.5 * v * (1.0 - t * t) * (scale * (1.0 + 3 * 0.044715 * square))
    return v * half, slope


def ff_body(
    core_ref, a_ref, b_ref, h_ref, gain_ref, win_ref, og_ref, wout_ref,
    nt_ref, h2_ref, act_ref, d_pre_ref, base_ref, both_ref, out_sum, back_sum, n_ref,
):
    rows, half = h_ref.shape[0], h_ref.shape[0] // 2
    h = h_ref[...] + (a_ref[...].astype(F32) + b_ref[...].astype(F32))
    h2_ref[...] = h
    n_ref[...] = (h * rms_scale(h) * gain_ref[...]).astype(BF16)
    nt_ref[...] = n_ref[...].T
    steps = FF_STEPS
    block = win_ref.shape[1] // steps
    for step in range(steps):
        units = slice(step * block, (step + 1) * block)
        win, wout = need(win_ref, step), need(wout_ref, step)
        value, slope = gelu_pair(dot(n_ref[...], win[:, units]))
        act_ref[:, units] = value.astype(BF16)
        d_act = dot_nt(og_ref[...], wout[units, :])
        d_pre_ref[:, units] = (d_act * slope).astype(BF16)
        out = dot(act_ref[:, units], wout[units, :])
        back = dot_nt(d_pre_ref[:, units], win[:, units])
        if step:
            out, back = out_sum[...] + out, back_sum[...] + back
        out_sum[...] = out
        if step < steps - 1:
            back_sum[...] = back
        else:
            both_ref[:rows] = back.astype(BF16)
    own, theirs = own_rows(core_ref, half), their_rows(core_ref, half)
    both_ref[rows:] = out_sum[theirs, :].astype(BF16)
    base_ref[...] = h2_ref[own, :] + out_sum[own, :]


def gain_sum(core_ref, dgain):
    row = lax.broadcasted_iota(jnp.int32, dgain.shape, 0)
    half = dgain.shape[0] // 2
    mine = (row >= core_ref[0] * half) & (row < (core_ref[0] + 1) * half)
    return jnp.sum(jnp.where(mine, dgain, 0.0), axis=0, keepdims=True)


def cross_back_body(
    core_ref, a_ref, b_ref, h_ref, up_ref, gain_ref, wo_ref, v_ref, probs_ref, k_ref, q_ref,
    w_ref, base_ref,
    g_ref, gt_ref, dq_ref, dk_ref, dv_ref, both_ref, dmem_ref, dgain_ref, out_ref,
    d_mix_ref, dmem_sum, g16_ref,
):
    rows, half = h_ref.shape[0], h_ref.shape[0] // 2
    up = a_ref[:rows].astype(F32) + b_ref[:rows].astype(F32)
    dv, dgain = norm_back(h_ref[...], gain_ref[...], up)
    dgain_ref[...] = gain_sum(core_ref, dgain)
    g = up_ref[...].astype(F32) + dv
    g_ref[...] = g
    g16_ref[...] = g.astype(BF16)
    d_mix_ref[...] = dot_nt(g16_ref[...], wo_ref[...]).astype(BF16)
    gt_ref[...] = g16_ref[...].T
    attend_back(
        q_ref, k_ref, v_ref, probs_ref, d_mix_ref, dq_ref, dk_ref, dv_ref, None, False
    )
    both_ref[:rows] = dot_nt(dq_ref[...], w_ref[0]).astype(BF16)
    dmem_sum[...] = dot_nt(dk_ref[...], w_ref[1]) + dot_nt(dv_ref[...], w_ref[2])
    both_ref[rows:] = dmem_sum[their_rows(core_ref, half), :].astype(BF16)
    dmem_ref[...] = dmem_sum[own_rows(core_ref, half), :]
    out_ref[...] = (base_ref[...] + b_ref[rows:].astype(F32)).astype(BF16)


def self_back_body(
    core_ref, a_ref, b_ref, h_ref, up_ref, gain_ref, wo_ref, v_ref, probs_ref, k_ref, q_ref, w_ref,
    g_ref, gt_ref, dq_ref, dk_ref, dv_ref, dn_ref, sent_ref, dgain_ref, diag_ref,
    d_mix_ref, total, g16_ref,
):
    rows, half = h_ref.shape[0], h_ref.shape[0] // 2
    own, theirs = own_rows(core_ref, half), their_rows(core_ref, half)
    up = a_ref[:rows].astype(F32) + b_ref[:rows].astype(F32)
    dv, dgain = norm_back(h_ref[...], gain_ref[...], up)
    dgain_ref[...] = gain_sum(core_ref, dgain)
    total[...] = up_ref[...] + dv
    g_ref[...] = total[own, :]
    g16_ref[...] = total[...].astype(BF16)
    d_mix_ref[...] = dot_nt(g16_ref[...], wo_ref[...]).astype(BF16)
    gt_ref[...] = g16_ref[...].T
    attend_back(
        q_ref, k_ref, v_ref, probs_ref, d_mix_ref, dq_ref, dk_ref, dv_ref, diag_ref, True
    )
    total[...] = (
        dot_nt(dq_ref[...], w_ref[0]) + dot_nt(dk_ref[...], w_ref[1]) + dot_nt(dv_ref[...], w_ref[2])
    )
    sent_ref[...] = total[theirs, :].astype(BF16)
    dn_ref[...] = total[own, :]


def last_body(core_ref, line_ref, b_ref, a_ref, x_ref, gain_ref, g_ref, packed_ref, dgain_ref):
    half = b_ref.shape[0]
    x_ref[:8]
    x = x_ref.ref[own_rows(core_ref, half), :].astype(F32)
    dv, dgain = norm_back(x, gain_ref[...], a_ref[...] + b_ref[...].astype(F32))
    rows = (g_ref[...] + dv).astype(BF16)
    packed_ref[...] = dot_tn(rows_of(line_ref[...], half), rows).astype(BF16)
    dgain_ref[...] = jnp.sum(dgain, axis=0, keepdims=True)


def grads_in_body(core_ref, own_ref, other_ref, og_ref, turned_ref):
    half = own_ref.shape[0]
    og_ref[own_rows(core_ref, half), :] = own_ref[...]
    og_ref[their_rows(core_ref, half), :] = other_ref[...]
    turned_ref[...] = og_ref[...].T


def relative_block(order, place):
    steps = len(order)
    return sum(((place >> (steps - 1 - at)) & 1) << bit for at, bit in enumerate(order))


def weight_body(plan, peers, me_ref, *refs):
    outs = refs[-2 * len(plan) :]
    for side, (order, steps) in enumerate(plan):
        keep, send = outs[2 * side], outs[2 * side + 1]
        at = 0
        for left, rights in steps:
            width = refs[left].shape[0]
            size = width // peers

            def rows(first, last):
                ref = need(refs[left], 0)
                if order is None:
                    return ref[first * size : last * size, :]
                blocks = [
                    ref[pl.ds(pl.multiple_of((relative_block(order, p) ^ me_ref[0]) * size, size), size), :]
                    for p in range(first, last)
                ]
                return jnp.concatenate(blocks, axis=0)

            for out, left_rows in ((send, rows(peers // 2, peers)), (keep, rows(0, peers // 2))):
                edge = at
                for right, low, high in rights:
                    out[:, edge : edge + high - low] = dot(
                        left_rows, refs[right][:, low:high]
                    ).astype(BF16)
                    edge += high - low
            at = edge
        flush(send, keep)


def weight_halves(me, peers, orders, sides, after=(), weight=WEIGHT):
    args, plan, outs = [me], [], []
    flops = 0
    plain = {}

    def place(array):
        far = isinstance(array, Far)
        for i, known in enumerate(args):
            if known is array or (far and isinstance(known, Far) and known.array is array.array):
                return i
        args.append(array)
        return len(args) - 1

    for order, side in zip(orders, sides):
        steps, total = [], 0
        for left, rights in side:
            width, rows = left.shape
            if (width // peers) % 16:
                array = left.array if isinstance(left, Far) else left
                blocks = np.array([relative_block(order, p) for p in range(peers)])
                index = (blocks ^ me[0])[:, None] * (width // peers) + np.arange(width // peers)
                left = jnp.take(array, index.reshape(-1), axis=0)
                order_here = None
            else:
                order_here = order
            steps.append((
                place(left) - 1,
                tuple((place(right) - 1, low, high) for right, low, high in rights),
            ))
            columns = sum(high - low for _, low, high in rights)
            total += columns
            flops += 2 * rows * width * columns
        plan.append((order_here, tuple(steps)))
        outs += pieces(width // 2, total)
    return call(
        partial(weight_body, tuple(plan), peers), outs, args, flops=flops, smem=(0,),
        after=after, weight=weight,
    )


def add_split_body(*refs):
    count = len(refs) // 4
    for i in range(count):
        kept, arrived = refs[2 * i], refs[2 * i + 1]
        keep, send = refs[2 * count + 2 * i], refs[2 * count + 2 * i + 1]
        half = keep.shape[0]
        send[...] = (kept[half:].astype(F32) + arrived[half:].astype(F32)).astype(BF16)
        flush(send)
        keep[...] = (kept[:half].astype(F32) + arrived[:half].astype(F32)).astype(BF16)
        flush(keep)


def add_join_body(*refs):
    keep, send = refs[-2:]
    half, at = keep.shape[0], 0
    for i in range(len(refs) // 2 - 1):
        kept, arrived = refs[2 * i], refs[2 * i + 1]
        columns = slice(at, at + kept.shape[1])
        at += kept.shape[1]
        send[:, columns] = (kept[half:].astype(F32) + arrived[half:].astype(F32)).astype(BF16)
        keep[:, columns] = (kept[:half].astype(F32) + arrived[:half].astype(F32)).astype(BF16)


def finish_body(moves, kept_ref, arrived_ref, *outs):
    total = kept_ref[...].astype(F32) + arrived_ref[...].astype(F32)
    for out, index, turned, spans in moves:
        at = 0
        for low, high in spans:
            part = total[:, low:high]
            edge = at + high - low
            if turned:
                outs[out][at:edge, :] = part.T
            elif index is None:
                outs[out][:, at:edge] = part
            else:
                outs[out][index, :, at:edge] = part
            at = edge


def exchange_rows(packed, peers):
    dims = packed.shape
    blocks = packed.reshape(peers, dims[0] // peers, dims[1])
    return lax.all_to_all(blocks, "dp", split_axis=0, concat_axis=0, tiled=True).reshape(dims)


def swap(values):
    return lax.ppermute(values, "mp", [(0, 1), (1, 0)])


def neighbour(values, bit, peers):
    return lax.ppermute(values, "dp", [(i, i ^ (1 << bit)) for i in range(peers)])


def pieces(rows, *columns):
    return [kind(shape((rows, n), BF16)) for n in columns for kind in (Far, lambda s: s)]


class Sum:
    def __init__(self, halves, orders, peers):
        self.halves, self.orders, self.peers, self.place = halves, orders, peers, 0
        self.send()

    def send(self):
        self.arrived = [
            neighbour(self.halves[2 * i + 1], order[self.place], self.peers)
            for i, order in enumerate(self.orders[: len(self.halves) // 2])
        ]
        self.place += 1

    def pairs(self):
        return [
            a for i, got in enumerate(self.arrived) for a in (Far(self.halves[2 * i]), got)
        ]

    def step(self, after=()):
        kept = self.halves[0::2]
        half = kept[0].shape[0] // 2
        if half % 16:
            total = (kept[0].astype(F32) + self.arrived[0].astype(F32)).astype(BF16)
            self.halves = [total[:half], total[half:]]
        elif self.place < len(self.orders) or len(kept) == 1:
            outs = pieces(half, *(k.shape[1] for k in kept))
            self.halves = call(add_split_body, outs, self.pairs(), after=after, weight=LIGHT)
        else:
            outs = pieces(half, sum(k.shape[1] for k in kept))
            self.halves = call(add_join_body, outs, self.pairs(), after=after, weight=LIGHT)
        self.send()
        return self.halves[0]

    def finish(self, outs, moves, after=()):
        while self.place < len(self.orders[0]):
            self.step()
        return call(partial(finish_body, moves), outs, self.pairs(), after=after, weight=LIGHT)


def local(
    hidden_in,
    memory,
    output_grad,
    segment_ids,
    route_counts,
    norm_gains,
    self_qkv,
    self_out,
    cross_qkv,
    cross_out,
    ff_in,
    ff_out,
    rel_bias,
):
    peers = lax.axis_size("dp")
    me = lax.axis_index("dp")
    core = lax.axis_index("mp")
    core_ref = core.astype(jnp.int32)[None]
    half_rows, width = hidden_in.shape
    rows = 2 * half_rows
    capacity = 2 * (half_rows // peers)
    buckets, heads = rel_bias.shape
    columns = self_out.shape[0]
    units = ff_out.shape[0]
    block = width // peers
    bits = peers.bit_length() - 1
    rest = tuple(range(3, bits))
    orders = ((0, 1, 2) + rest, (1, 2, 0) + rest, (2, 0, 1) + rest)
    pair_orders = ((0, 1, 2) + rest, (1, 0, 2) + rest)
    me_ref = me.astype(jnp.int32)[None]
    slots = peers * capacity
    wide, narrow = shape((rows, width), BF16), shape((rows, columns), BF16)
    wide32, gain_shape = shape((rows, width), F32), shape((1, width), F32)
    half16, half32 = shape((half_rows, width), BF16), shape((half_rows, width), F32)
    more16 = shape((rows + half_rows, width), BF16)
    turned = shape((width, rows), BF16)
    probs_shape = shape((heads, rows, rows), BF16)
    square = rows * width * columns
    scores = heads * rows * rows

    packed, sent, taken = call(
        pack_body,
        [shape((slots, 2 * width), BF16)] + [Far(shape((1, slots), jnp.int32))] * 2,
        [route_counts, me_ref, Far(hidden_in), Far(memory)],
        smem=(0, 1),
    )
    arrived = exchange_rows(packed, peers)

    gains = norm_gains.astype(F32)
    gain_one, gain_two, gain_three = gains[0:1], gains[1:2], gains[2:3]
    edges = bucket_edges(buckets, MAX_DIST)
    offset = MAX_DIST - np.arange(3 * MAX_DIST)
    bucket_of = np.where(
        (offset >= 0), np.searchsorted(edges, offset, side="right"), buckets - 1
    )
    bucket_hot = bucket_of[:, None] == np.arange(buckets)[None, :]
    lines = jnp.dot(
        bucket_hot[: 2 * MAX_DIST].astype(jnp.bfloat16), rel_bias, preferred_element_type=F32
    ).T
    bias, mask = call(
        tables_body,
        [Far(shape((heads, TILE, rows), BF16)), Far(shape((rows, rows), F32))],
        [lines, segment_ids],
        after=[sent],
    )
    og, og_turned = call(
        grads_in_body,
        [Far(wide), Far(turned)],
        [core_ref, output_grad, swap(output_grad)],
        smem=(0,),
        after=[mask],
    )
    [own] = call(
        unpack_body,
        [shape((half_rows, 2 * width), BF16)],
        [taken, arrived],
        after=[mask, og_turned],
    )
    other = swap(own)

    by_head = partial(Far, axis=0, count=heads)
    x, n1_turned, sq, sk, sv, self_probs, self_mix, part_one = call(
        self_forward_body,
        [
            Far(wide), Far(turned), Far(narrow), Far(narrow), Far(narrow), by_head(probs_shape),
            Far(narrow), wide,
        ],
        [core_ref, own, other, gain_one, self_qkv, mask, bias, self_out],
        flops=8 * square + 8 * scores * HEAD_DIM,
        scratch=[pltpu.VMEM((rows, width), BF16)],
        smem=(0,),
    )
    part_there = swap(part_one)
    ck, cv, mem_turned = call(
        keys_body,
        [narrow, narrow, Far(turned)],
        [core_ref, own, other, cross_qkv],
        flops=4 * square,
        scratch=[pltpu.VMEM((rows, width), BF16)],
        smem=(0,),
        after=[x],
    )
    h1, h1_far, n2_turned, cq, cross_probs, cross_mix, part_two = call(
        cross_forward_body,
        [wide32, Far(wide32), Far(turned), Far(narrow), by_head(probs_shape), Far(narrow), wide],
        [part_one, part_there, Far(x), gain_two, cross_qkv, ck, mask, cv, cross_out],
        flops=4 * square + 8 * scores * HEAD_DIM,
        scratch=[pltpu.VMEM((rows, width), BF16)],
    )
    n3_turned, h2, act, d_pre, base, pack3 = call(
        ff_body,
        [turned, wide32, shape((rows, units), BF16), shape((rows, units), BF16), half32, more16],
        [core_ref, part_two, swap(part_two), h1, gain_three, ff_in, og, ff_out],
        flops=8 * rows * width * units,
        scratch=[
            pltpu.VMEM((rows, width), F32), pltpu.VMEM((rows, width), F32),
            pltpu.VMEM((rows, width), BF16),
        ],
        smem=(0,),
    )
    pack3_there = swap(pack3)

    ff_sum = Sum(
        weight_halves(me_ref, peers, pair_orders, [
            [(Far(og_turned), [(act, 0, units)])],
            [(n3_turned, [(d_pre, 0, units)])],
        ]),
        pair_orders, peers,
    )
    g2, g2_turned, dcq, dck, dcv, pack2, d_mem, dgain3, block_out = call(
        cross_back_body,
        [
            Far(wide32), turned, narrow, narrow, narrow, Far(more16), half32, Far(gain_shape), half16,
        ],
        [
            core_ref, pack3, pack3_there, h2, Far(og), gain_three, Far(cross_out), cv,
            by_head(cross_probs), ck, Far(cq), Far(cross_qkv), base,
        ],
        flops=8 * square + 14 * scores * HEAD_DIM,
        scratch=[
            pltpu.VMEM((rows, columns), BF16), pltpu.VMEM((rows, width), F32),
            pltpu.VMEM((rows, width), BF16),
        ],
        smem=(0,),
        after=[ff_sum.halves[0]],
    )
    pack2_there = swap(pack2)
    cross_sum = Sum(
        weight_halves(me_ref, peers, pair_orders, [
            [(g2_turned, [(Far(cross_mix), 0, columns)]), (Far(n2_turned), [(dcq, 0, columns)])],
            [(Far(mem_turned), [(dck, 0, columns), (dcv, 0, columns)])],
        ]),
        pair_orders, peers,
    )
    [mem_packed] = call(
        pack_sum_body, [shape((slots, width), BF16)], [taken, d_mem, pack2_there],
        after=[cross_sum.halves[0]],
        weight=LIGHT,
    )
    mem_back = exchange_rows(mem_packed, peers)
    ff_token = ff_sum.step(after=[cross_sum.halves[0]])
    g1_own, g1_turned, dsq, dsk, dsv, dn1, dn1_sent, dgain2, diag = call(
        self_back_body,
        [Far(half32), turned, narrow, narrow, narrow, Far(half32), half16, Far(gain_shape),
         Far(shape((heads, 8, 3 * MAX_DIST), F32))],
        [
            core_ref, Far(pack2), pack2_there, Far(h1_far), Far(g2), gain_two, Far(self_out), Far(sv),
            Far(self_probs), Far(sk), Far(sq), Far(self_qkv),
        ],
        flops=8 * square + 14 * scores * HEAD_DIM,
        scratch=[
            pltpu.VMEM((rows, columns), BF16), pltpu.VMEM((rows, width), F32),
            pltpu.VMEM((rows, width), BF16),
        ],
        smem=(0,),
        after=[ff_token],
    )

    def unpack(values, line):
        return call(unpack_body, [half16], [line, values], weight=LIGHT)[0]

    memory_grad = unpack(mem_back, sent)
    dn1_there = swap(dn1_sent)
    self_sum = Sum(
        weight_halves(
            me_ref, peers, pair_orders,
            [
                [(g1_turned, [(Far(self_mix), 0, columns)]), (Far(n1_turned), [(dsq, 0, columns)])],
                [(Far(n1_turned), [(dsk, 0, columns), (dsv, 0, columns)])],
            ],
            weight=AFTER_SELF,
        ),
        pair_orders, peers,
    )
    packed, dgain1 = call(
        last_body,
        [shape((slots, width), BF16), Far(gain_shape)],
        [core_ref, taken, dn1_there, Far(dn1), Far(x), gain_one, Far(g1_own)],
        smem=(0,),
        after=[self_sum.halves[0]],
        weight=LIGHT,
    )
    back = exchange_rows(packed, peers)
    cross_token = cross_sum.step(after=[dgain1])
    ff_token = ff_sum.step(after=[cross_token])
    self_token = self_sum.step(after=[ff_token])
    cross_token = cross_sum.step(after=[self_token])
    ff_token = ff_sum.step(after=[cross_token])
    self_token = self_sum.step(after=[ff_token])
    cross_token = cross_sum.step(after=[self_token])
    ff_in_total, ff_out_total = ff_sum.finish(
        [shape((block, units), F32), shape((units, block), F32)],
        ((0, None, False, [(units, 2 * units)]), (1, None, True, [(0, units)])),
        after=[cross_token],
    )
    out_shapes = [shape((columns, block), F32), shape((3, block, columns), F32)]

    cross_moves = ((0, None, True, [(0, columns)]),) + tuple(
        (1, i, False, [((i + 1) * columns, (i + 2) * columns)]) for i in range(3)
    )
    cross_out_total, cross_qkv_total = cross_sum.finish(out_shapes, cross_moves)
    self_out_total, self_qkv_total = self_sum.finish(out_shapes, cross_moves)

    bias_part = jnp.sum(jnp.where(bucket_hot[:, :, None], diag[:, 0].T[:, None, :], 0.0), axis=0)
    small = jnp.zeros((buckets, heads * 2), F32)
    small = lax.dynamic_update_slice_in_dim(small, bias_part, core * heads, 1)
    small = jnp.concatenate(
        [dgain1.reshape(-1), dgain2.reshape(-1), dgain3.reshape(-1), small.reshape(-1)]
    ).reshape(-1, 128)
    small = small + swap(small)
    for bit in orders[0]:
        small = small + neighbour(small, bit, peers)
    small = small.reshape(-1)
    gains_total = small[: 3 * width].reshape(3, width)
    bias_total = small[3 * width :].reshape(buckets, heads * 2)
    input_grad = unpack(back, sent)
    return (
        block_out,
        input_grad,
        memory_grad,
        gains_total,
        bias_total,
        self_qkv_total,
        self_out_total,
        cross_qkv_total,
        cross_out_total,
        ff_in_total,
        ff_out_total,
    )


def solution(mesh):
    both = ("dp", "mp")
    in_specs = (
        P(both, None),
        P(both, None),
        P(both, None),
        P("dp", None),
        P(),
        P(),
        P(None, None, "mp"),
        P("mp", None),
        P(None, None, "mp"),
        P("mp", None),
        P(None, "mp"),
        P("mp", None),
        P(None, "mp"),
    )
    out_specs = (
        P(both, None),
        P(both, None),
        P(both, None),
        P(),
        P(),
        P(None, "dp", "mp"),
        P("mp", "dp"),
        P(None, "dp", "mp"),
        P("mp", "dp"),
        P("dp", "mp"),
        P("mp", "dp"),
    )
    return jax.shard_map(local, mesh=mesh, in_specs=in_specs, out_specs=out_specs, check_vma=False)
```

```python
from functools import partial

import jax
import jax.numpy as jnp
import numpy as np
from jax import lax
from jax.experimental import pallas as pl
from jax.experimental.pallas import tpu as pltpu
from jax.sharding import PartitionSpec as P

HEAD_DIM = 64
MAX_DIST = 128
EPS = 1e-06
MASKED = -1e30
TILE = 256
F32 = jnp.float32
BF16 = jnp.bfloat16
VMEM_LIMIT = 24 * 1024 * 1024
WEIGHT = 3 * 10**10
LIGHT = 10**6
AFTER_SELF = 3 * 10**9
LAST_WEIGHT = 7 * 10**9
FF_FIRST = True
TWO_FIRST = True
FF_STEPS = 3
EXTRA = 8


def bucket_edges(buckets, distance):
    exact_span = buckets // 2
    edge_list = []
    for offset in range(1, 4 * distance):
        if offset < exact_span:
            bucket_now = offset
        else:
            log_ratio = np.log(offset / exact_span) / np.log(distance / exact_span)
            bucket_now = min(buckets - 1, exact_span + int(log_ratio * (buckets - exact_span)))
        while len(edge_list) < bucket_now:
            edge_list.append(offset)
    return np.array(edge_list, dtype=np.int32)


def dot(a, b):
    return jnp.dot(a, b, preferred_element_type=F32)


def dot_nt(a, b):
    return lax.dot_general(a, b, (((1,), (1,)), ((), ())), preferred_element_type=F32)


def dot_tn(a, b):
    return lax.dot_general(a, b, (((0,), (0,)), ((), ())), preferred_element_type=F32)


def rms_scale(values):
    return lax.rsqrt(jnp.mean(values * values, axis=-1, keepdims=True) + EPS)


def norm_back(values, gain_row, upstream):
    scale = rms_scale(values)
    scaled = gain_row * upstream
    back = scale * scaled - values * (
        scale * scale * scale * jnp.mean(scaled * values, axis=-1, keepdims=True)
    )
    return back, upstream * values * scale


class Near:
    def __init__(self, array):
        self.array = array


class Far:
    def __init__(self, array, axis=0, count=1):
        self.array, self.axis, self.count = array, axis, count
        self.shape, self.dtype = array.shape, array.dtype


def part(ref, axis, count, i):
    size = ref.shape[axis] // count
    index = tuple(
        pl.ds(i * size, size) if at == axis else slice(None) for at in range(len(ref.shape))
    )
    return ref.at[index]


class Inbound:
    def __init__(self, ref, copies):
        self.ref, self.copies, self.shape = ref, copies, ref.shape
        self.waiting = set(range(len(copies)))

    def need(self, i):
        if i in self.waiting:
            self.waiting.discard(i)
            self.copies[i].wait()

    def __getitem__(self, index):
        for i in range(len(self.copies)):
            self.need(i)
        return self.ref[index]


class Outbound:
    def __init__(self, ref, copies):
        self.ref, self.copies, self.shape, self.dtype = ref, copies, ref.shape, ref.dtype
        self.pending, self.flying = set(range(len(copies))), set()

    def __getitem__(self, index):
        return self.ref[index]

    def __setitem__(self, index, value):
        self.ref[index] = value

    def flush(self, i=None):
        for at in sorted(self.pending) if i is None else [i]:
            self.pending.discard(at)
            self.flying.add(at)
            self.copies[at].start()

    def end(self):
        self.flush()
        for at in sorted(self.flying):
            self.copies[at].wait()


def need(ref, i):
    if isinstance(ref, Inbound):
        ref.need(i % len(ref.copies))
        return ref.ref
    return ref


def flush(*refs, i=None):
    for ref in refs:
        if isinstance(ref, Outbound):
            ref.flush(i)


def call(body, outs, args, flops=0, scratch=(), smem=(), after=(), weight=WEIGHT):
    count, extra, made = len(args), len(after), len(outs)
    far_in = [i for i in range(count) if isinstance(args[i], Far)]
    far_out = [i for i in range(made) if isinstance(outs[i], Far)]
    arrays = [a.array if isinstance(a, Far) else a for a in args]
    shapes = [o.array if isinstance(o, Far) else o for o in outs]
    size = sum(a.size * a.dtype.itemsize for a in arrays + shapes)
    sems = sum(args[i].count for i in far_in) + sum(outs[i].count for i in far_out)

    given = [
        pltpu.with_memory_space_constraint(a, pltpu.HBM) if i in far_in else a
        for i, a in enumerate(arrays)
    ]

    def kernel(*refs):
        ins, refs = list(refs[:count]), refs[count + extra :]
        to, refs = list(refs[:made]), refs[made:]
        rooms, refs = refs[: len(far_in)], refs[len(far_in) :]
        shelves, rest = refs[: len(far_out)], refs[len(far_out) :]
        if sems:
            sem, rest = rest[0], rest[1:]
        at = 0
        for i, room in zip(far_in, rooms):
            copies = []
            for j in range(args[i].count):
                cut = (args[i].axis, args[i].count, j)
                copies.append(
                    pltpu.make_async_copy(part(ins[i], *cut), part(room, *cut), sem.at[at])
                )
                copies[-1].start()
                at += 1
            ins[i] = Inbound(room, copies)
        for i, shelf in zip(far_out, shelves):
            copies = []
            for j in range(outs[i].count):
                cut = (outs[i].axis, outs[i].count, j)
                copies.append(
                    pltpu.make_async_copy(part(shelf, *cut), part(to[i], *cut), sem.at[at])
                )
                at += 1
            to[i] = Outbound(shelf, copies)
        body(*ins, *to, *rest)
        for i in far_in:
            for j in sorted(ins[i].waiting):
                ins[i].need(j)
        for i in far_out:
            to[i].flush()
        for i in far_out:
            to[i].end()

    hbm, vmem = pl.BlockSpec(memory_space=pltpu.HBM), pl.BlockSpec(memory_space=pltpu.VMEM)
    return pl.pallas_call(
        kernel,
        out_shape=[
            (pltpu.HBM if i in far_out else pltpu.VMEM)(o.shape, o.dtype) for i, o in enumerate(shapes)
        ],
        in_specs=[
            pl.BlockSpec(memory_space=pltpu.SMEM) if i in smem else hbm if i in far_in else vmem
            for i in range(count)
        ]
        + [pl.BlockSpec(memory_space=pl.ANY) if isinstance(a, Near) else hbm for a in after],
        out_specs=[hbm if i in far_out else vmem for i in range(made)],
        scratch_shapes=[pltpu.VMEM(arrays[i].shape, arrays[i].dtype) for i in far_in]
        + [pltpu.VMEM(shapes[i].shape, shapes[i].dtype) for i in far_out]
        + ([pltpu.SemaphoreType.DMA((sems,))] if sems else [])
        + list(scratch),
        compiler_params=pltpu.CompilerParams(vmem_limit_bytes=VMEM_LIMIT),
        cost_estimate=pl.CostEstimate(
            flops=int(weight), bytes_accessed=0, transcendentals=0
        ),
    )(
        *given,
        *(
            a.array if isinstance(a, Near) else pltpu.with_memory_space_constraint(a, pltpu.HBM)
            for a in after
        ),
    )


def shape(dims, dtype):
    return jax.ShapeDtypeStruct(dims, dtype)


def own_rows(core_ref, half):
    return pl.ds(pl.multiple_of(core_ref[0] * half, half), half)


def their_rows(core_ref, half):
    return pl.ds(pl.multiple_of((1 - core_ref[0]) * half, half), half)


def tables_body(
    counts_ref, me_ref, vec_ref, ids_ref, bias_ref, mask_ref, taken_ref, sent_wide_ref, taken_wide_ref
):
    peers = counts_ref.shape[0]
    capacity = taken_ref.shape[1] // peers
    taken_ref[...] = slot_line(lambda s: counts_ref[s, me_ref[0]], peers, capacity)
    stride = capacity + EXTRA
    sent_wide_ref[...] = slot_line(lambda o: counts_ref[me_ref[0], o], peers, stride)
    taken_wide_ref[...] = slot_line(lambda s: counts_ref[s, me_ref[0]], peers, stride)
    heads, rows = bias_ref.shape[0], mask_ref.shape[0]
    row = lax.broadcasted_iota(jnp.int32, (MAX_DIST, 2 * MAX_DIST), 0)
    column = lax.broadcasted_iota(jnp.int32, (MAX_DIST, 2 * MAX_DIST), 1)
    for head in range(heads):
        line = vec_ref[head : head + 1, :]
        near = pltpu.roll(
            jnp.broadcast_to(line, (MAX_DIST, 2 * MAX_DIST)), 0, 1, stride=1, stride_axis=0
        )
        near = jnp.where(column > row + MAX_DIST, MASKED, near)
        far = jnp.broadcast_to(line[:, 2 * MAX_DIST - 1 :], (MAX_DIST, MAX_DIST))
        none = jnp.full((MAX_DIST, MAX_DIST), MASKED, F32)
        upper = jnp.concatenate([far, near, none], axis=1)
        lower = jnp.concatenate([far, far, near], axis=1)
        bias_ref[head] = jnp.concatenate([upper, lower], axis=0).astype(BF16)
    ids = ids_ref[...].astype(F32)
    down = jnp.broadcast_to(ids, (128, rows)).T[:, :1]
    mask_ref[...] = jnp.where(down == ids, 0.0, MASKED)


def slot_line(count_of, peers, capacity):
    lane = lax.broadcasted_iota(jnp.int32, (1, peers * capacity), 1)
    line = jnp.full_like(lane, -1)
    start = jnp.int32(0)
    for peer in range(peers):
        count, within = count_of(peer), lane - peer * capacity
        line = jnp.where((within >= 0) & (within < count), start + within, line)
        start = start + count
    return line


def rows_of(line, rows):
    row = lax.broadcasted_iota(jnp.int32, (rows, line.shape[1]), 0)
    return (line == row).astype(BF16)


def pack_body(counts_ref, me_ref, a_ref, b_ref, packed_ref, sent_ref):
    peers, (half, width) = counts_ref.shape[0], a_ref.shape
    capacity = packed_ref.shape[0] // peers
    sent = slot_line(lambda o: counts_ref[me_ref[0], o], peers, capacity)
    sent_ref[...] = sent
    flush(sent_ref)
    slots = rows_of(sent, half)
    packed_ref[:, :width] = dot_tn(slots, a_ref[...]).astype(BF16)
    packed_ref[:, width:] = dot_tn(slots, b_ref[...]).astype(BF16)


def pack_sum_body(line_ref, a_ref, b_ref, packed_ref, token_ref):
    half = a_ref.shape[0]
    skip = b_ref.shape[0] - half
    token_ref[...] = jnp.zeros_like(token_ref)
    rows = (a_ref[...] + b_ref[skip:].astype(F32)).astype(BF16)
    packed_ref[...] = dot_tn(rows_of(line_ref[...], half), rows).astype(BF16)


def unpack_body(line_ref, packed_ref, rows_ref):
    rows_ref[...] = dot(rows_of(line_ref[...], rows_ref.shape[0]), packed_ref[...]).astype(BF16)


def lane_half(values, which):
    lane = lax.broadcasted_iota(jnp.int32, values.shape, 1)
    keep = (lane < HEAD_DIM) if which == 0 else (lane >= HEAD_DIM)
    return jnp.where(keep, values, jnp.zeros_like(values))


def attend(q_ref, k_ref, v_ref, mask_ref, bias_ref, probs_ref, mix_ref):
    rows, columns = q_ref.shape
    causal = bias_ref is not None
    for pair in range(columns // (2 * HEAD_DIM)):
        lanes = slice(pair * 2 * HEAD_DIM, (pair + 1) * 2 * HEAD_DIM)
        for tile in range(rows // TILE):
            here = slice(tile * TILE, (tile + 1) * TILE)
            reach = (tile + 1) * TILE if causal else rows
            q, k, v = q_ref[here, lanes], k_ref[:reach, lanes], v_ref[:reach, lanes]
            mixed = None
            for which in range(2):
                head = 2 * pair + which
                scores = dot_nt(lane_half(q, which), k) + mask_ref[here, :reach]
                if causal:
                    bias = need(bias_ref, head)[head, :, rows - reach :]
                    scores = scores + bias.astype(F32)
                peak = jnp.max(scores, axis=-1, keepdims=True)
                weights = jnp.exp(scores - peak)
                total = jnp.sum(weights, axis=-1, keepdims=True)
                probs = (weights * (1.0 / total)).astype(BF16)
                probs_ref[head, here, :reach] = probs
                each = dot(probs, lane_half(v, which))
                mixed = each if mixed is None else mixed + each
            mix_ref[here, lanes] = mixed.astype(BF16)
        flush(probs_ref, i=2 * pair)
        flush(probs_ref, i=2 * pair + 1)
    flush(mix_ref)


def attend_back(
    q_ref, k_ref, v_ref, probs_ref, d_mix_ref, dq_ref, dk_ref, dv_ref, diag_ref, causal
):
    rows, columns = q_ref.shape
    for pair in range(columns // (2 * HEAD_DIM)):
        lanes = slice(pair * 2 * HEAD_DIM, (pair + 1) * 2 * HEAD_DIM)
        q_turned = q_ref[:, lanes].T
        d_turned = d_mix_ref[:, lanes].T
        dk_turned, dv_turned = [], []
        near = [None, None]
        for which in range(2):
            head = 2 * pair + which
            halves = slice(which * HEAD_DIM, (which + 1) * HEAD_DIM)
            dk_sum = dv_sum = None
            grown = None
            for tile in reversed(range(rows // TILE)):
                here = slice(tile * TILE, (tile + 1) * TILE)
                reach = (tile + 1) * TILE if causal else rows
                k, v = k_ref[:reach, lanes], v_ref[:reach, lanes]
                probs16 = need(probs_ref, head)[head, here, :reach]
                probs = probs16.astype(F32)
                d_probs = dot_nt(lane_half(d_mix_ref[here, lanes], which), v)
                product = probs * d_probs
                delta = jnp.sum(product, axis=-1, keepdims=True)
                d_scores = product - probs * delta
                d_scores16 = d_scores.astype(BF16)
                dq = dot(d_scores16, lane_half(k, which))
                if which == 0:
                    near[tile] = dq
                else:
                    dq_ref[here, lanes] = (near[tile] + dq).astype(BF16)
                dk = dot(q_turned[halves, here], d_scores16)
                dv = dot(d_turned[halves, here], probs16)
                if causal and reach < rows:
                    pad = jnp.zeros((HEAD_DIM, rows - reach), F32)
                    dk = jnp.concatenate([dk, pad], axis=1)
                    dv = jnp.concatenate([dv, pad], axis=1)
                dk_sum = dk if dk_sum is None else dk_sum + dk
                dv_sum = dv if dv_sum is None else dv_sum + dv
                if causal:
                    kept = d_scores16.astype(F32)
                    if reach < rows:
                        kept = jnp.concatenate(
                            [jnp.zeros((TILE, rows - reach), F32), kept], axis=1
                        )
                    grown = kept if grown is None else grown + kept
            dk_turned.append(dk_sum)
            dv_turned.append(dv_sum)
            if causal:
                d = MAX_DIST
                close = grown[:d, d : 3 * d] + grown[d:, 2 * d :]
                row = lax.broadcasted_iota(jnp.int32, close.shape, 0)
                turned, shift = close, 1
                while shift < d:
                    moved = pltpu.roll(turned, 2 * d - shift, 1)
                    turned = jnp.where((row & shift) > 0, moved, turned)
                    shift *= 2
                far = jnp.sum(grown[:d, :d] + grown[d:, :d] + grown[d:, d : 2 * d], axis=0)
                line = jnp.sum(turned, axis=0, keepdims=True)
                spread = jnp.concatenate([line, far[None]], axis=1)
                diag_ref[head] = jnp.broadcast_to(spread, (8, 3 * d))
        dk_ref[:, lanes] = jnp.concatenate(dk_turned, axis=0).T.astype(BF16)
        dv_ref[:, lanes] = jnp.concatenate(dv_turned, axis=0).T.astype(BF16)


def self_forward_body(
    core_ref, own_ref, other_ref, gain_ref, w_ref, mask_ref, bias_ref, wo_ref,
    x_ref, nt_ref, q_ref, k_ref, v_ref, probs_ref, mix_ref, part_ref, n_ref,
):
    half, width = own_ref.shape[0], gain_ref.shape[1]
    x_ref[own_rows(core_ref, half), :] = own_ref[:, :width]
    x_ref[their_rows(core_ref, half), :] = other_ref[:, :width]
    flush(x_ref)
    x = x_ref[...].astype(F32)
    n_ref[...] = (x * rms_scale(x) * gain_ref[...]).astype(BF16)
    for i, out in enumerate((q_ref, k_ref, v_ref)):
        out[...] = dot(n_ref[...], need(w_ref, i)[i]).astype(BF16)
    nt_ref[...] = n_ref[...].T
    flush(q_ref, k_ref, v_ref, nt_ref)
    attend(q_ref, k_ref, v_ref, mask_ref, bias_ref, probs_ref, mix_ref)
    part_ref[...] = dot(mix_ref[...], wo_ref[...]).astype(BF16)


def keys_body(core_ref, own_ref, other_ref, w_ref, k_ref, v_ref, memt_ref, mem_ref):
    half, width = own_ref.shape[0], w_ref.shape[1]
    mem_ref[own_rows(core_ref, half), :] = own_ref[:, width:]
    mem_ref[their_rows(core_ref, half), :] = other_ref[:, width:]
    for i, out in ((1, k_ref), (2, v_ref)):
        out[...] = dot(mem_ref[...], need(w_ref, i)[i]).astype(BF16)
    memt_ref[...] = mem_ref[...].T


def cross_forward_body(
    a_ref, b_ref, x_ref, gain_ref, w_ref, k_ref, mask_ref, v_ref, wo_ref,
    h_ref, h_far_ref, nt_ref, q_ref, probs_ref, mix_ref, part_ref, n_ref,
):
    h_ref[...] = x_ref[...].astype(F32) + (a_ref[...].astype(F32) + b_ref[...].astype(F32))
    h_far_ref[...] = h_ref[...]
    flush(h_far_ref)
    h = h_ref[...]
    n_ref[...] = (h * rms_scale(h) * gain_ref[...]).astype(BF16)
    q_ref[...] = dot(n_ref[...], need(w_ref, 0)[0]).astype(BF16)
    nt_ref[...] = n_ref[...].T
    flush(q_ref, nt_ref)
    attend(q_ref, k_ref, v_ref, mask_ref, None, probs_ref, mix_ref)
    part_ref[...] = dot(mix_ref[...], wo_ref[...]).astype(BF16)


def gelu_pair(v):
    scale = float(np.sqrt(2 / np.pi))
    square = v * v
    t = jnp.tanh(scale * (v + 0.044715 * (square * v)))
    half = 0.5 * (1.0 + t)
    slope = half + 0.5 * v * (1.0 - t * t) * (scale * (1.0 + 3 * 0.044715 * square))
    return v * half, slope


def ff_body(
    core_ref, a_ref, b_ref, h_ref, gain_ref, win_ref, og_ref, wout_ref,
    nt_ref, h2_ref, act_ref, d_pre_ref, base_ref, both_ref, out_sum, back_sum, n_ref,
):
    rows, half = h_ref.shape[0], h_ref.shape[0] // 2
    h = h_ref[...] + (a_ref[...].astype(F32) + b_ref[...].astype(F32))
    h2_ref[...] = h
    n_ref[...] = (h * rms_scale(h) * gain_ref[...]).astype(BF16)
    nt_ref[...] = n_ref[...].T
    steps = FF_STEPS
    block = win_ref.shape[1] // steps
    for step in range(steps):
        units = slice(step * block, (step + 1) * block)
        win, wout = need(win_ref, step), need(wout_ref, step)
        value, slope = gelu_pair(dot(n_ref[...], win[:, units]))
        act_ref[:, units] = value.astype(BF16)
        d_act = dot_nt(og_ref[...], wout[units, :])
        d_pre_ref[:, units] = (d_act * slope).astype(BF16)
        out = dot(act_ref[:, units], wout[units, :])
        back = dot_nt(d_pre_ref[:, units], win[:, units])
        if step:
            out, back = out_sum[...] + out, back_sum[...] + back
        out_sum[...] = out
        if step < steps - 1:
            back_sum[...] = back
        else:
            both_ref[:rows] = back.astype(BF16)
    own, theirs = own_rows(core_ref, half), their_rows(core_ref, half)
    both_ref[rows:] = out_sum[theirs, :].astype(BF16)
    base_ref[...] = h2_ref[own, :] + out_sum[own, :]


def gain_sum(core_ref, dgain):
    row = lax.broadcasted_iota(jnp.int32, dgain.shape, 0)
    half = dgain.shape[0] // 2
    mine = (row >= core_ref[0] * half) & (row < (core_ref[0] + 1) * half)
    return jnp.sum(jnp.where(mine, dgain, 0.0), axis=0, keepdims=True)


def cross_back_body(
    core_ref, a_ref, b_ref, h_ref, up_ref, gain_ref, wo_ref, v_ref, probs_ref, k_ref, q_ref,
    w_ref, base_ref,
    g_ref, gt_ref, dq_ref, dk_ref, dv_ref, both_ref, dmem_ref, dgain_ref, out_ref,
    d_mix_ref, dmem_sum, g16_ref,
):
    rows, half = h_ref.shape[0], h_ref.shape[0] // 2
    up = a_ref[:rows].astype(F32) + b_ref[:rows].astype(F32)
    dv, dgain = norm_back(h_ref[...], gain_ref[...], up)
    dgain_ref[...] = gain_sum(core_ref, dgain)
    g = up_ref[...].astype(F32) + dv
    g_ref[...] = g
    g16_ref[...] = g.astype(BF16)
    d_mix_ref[...] = dot_nt(g16_ref[...], wo_ref[...]).astype(BF16)
    gt_ref[...] = g16_ref[...].T
    attend_back(
        q_ref, k_ref, v_ref, probs_ref, d_mix_ref, dq_ref, dk_ref, dv_ref, None, False
    )
    both_ref[:rows] = dot_nt(dq_ref[...], w_ref[0]).astype(BF16)
    dmem_sum[...] = dot_nt(dk_ref[...], w_ref[1]) + dot_nt(dv_ref[...], w_ref[2])
    both_ref[rows:] = dmem_sum[their_rows(core_ref, half), :].astype(BF16)
    dmem_ref[...] = dmem_sum[own_rows(core_ref, half), :]
    out_ref[...] = (base_ref[...] + b_ref[rows:].astype(F32)).astype(BF16)


def self_back_body(
    core_ref, a_ref, b_ref, h_ref, up_ref, gain_ref, wo_ref, v_ref, probs_ref, k_ref, q_ref, w_ref,
    g_ref, gt_ref, dq_ref, dk_ref, dv_ref, dn_ref, sent_ref, dgain_ref, diag_ref,
    d_mix_ref, total, g16_ref,
):
    rows, half = h_ref.shape[0], h_ref.shape[0] // 2
    own, theirs = own_rows(core_ref, half), their_rows(core_ref, half)
    up = a_ref[:rows].astype(F32) + b_ref[:rows].astype(F32)
    dv, dgain = norm_back(h_ref[...], gain_ref[...], up)
    dgain_ref[...] = gain_sum(core_ref, dgain)
    total[...] = up_ref[...] + dv
    g_ref[...] = total[own, :]
    g16_ref[...] = total[...].astype(BF16)
    d_mix_ref[...] = dot_nt(g16_ref[...], wo_ref[...]).astype(BF16)
    gt_ref[...] = g16_ref[...].T
    attend_back(
        q_ref, k_ref, v_ref, probs_ref, d_mix_ref, dq_ref, dk_ref, dv_ref, diag_ref, True
    )
    total[...] = (
        dot_nt(dq_ref[...], w_ref[0]) + dot_nt(dk_ref[...], w_ref[1]) + dot_nt(dv_ref[...], w_ref[2])
    )
    sent_ref[...] = total[theirs, :].astype(BF16)
    dn_ref[...] = total[own, :]


def extra_slots(count, peers, stride, place):
    lane = lax.broadcasted_iota(jnp.int32, (count, peers * stride), 1)
    row = lax.broadcasted_iota(jnp.int32, (count, peers * stride), 0)
    hot = lane < 0
    for peer in range(peers):
        hot = hot | (lane == peer * stride + place + row)
    return hot.astype(BF16)


def last_body(
    peers, core_ref, line_ref, b_ref, a_ref, x_ref, gain_ref, g_ref, two_ref, three_ref, diag_ref,
    hot_ref, packed_ref,
):
    half, width = b_ref.shape
    x = need(x_ref, 0)[own_rows(core_ref, half), :].astype(F32)
    dv, dgain = norm_back(x, gain_ref[...], a_ref[...] + b_ref[...].astype(F32))
    rows = (g_ref[...] + dv).astype(BF16)
    heads, buckets = diag_ref.shape[0], hot_ref.shape[1]
    lines = jnp.concatenate([diag_ref[head][:1] for head in range(heads)], axis=0)
    sums = jnp.dot(lines, hot_ref[...], preferred_element_type=F32, precision=lax.Precision.HIGHEST)
    twice = jnp.concatenate([sums, sums], axis=1)
    lane = lax.broadcasted_iota(jnp.int32, twice.shape, 1)
    first = core_ref[0] * buckets
    twice = jnp.where((lane >= first) & (lane < first + buckets), twice, 0.0)
    bias = [twice[head : head + 1] for head in range(heads)]
    bias.append(jnp.zeros((1, width - 2 * heads * buckets), F32))
    small = jnp.concatenate(
        [
            jnp.sum(dgain, axis=0, keepdims=True), two_ref[...], three_ref[...],
            jnp.concatenate(bias, axis=1),
        ],
        axis=0,
    )
    high = small.astype(BF16)
    low = (small - high.astype(F32)).astype(BF16)
    small = jnp.concatenate([high, low, jnp.zeros((8, width), BF16)], axis=0)
    stride = packed_ref.shape[0] // peers
    extra = extra_slots(16, peers, stride, stride - EXTRA)
    extra = jnp.where(lax.broadcasted_iota(jnp.int32, extra.shape, 0) < EXTRA, extra, 0.0).astype(BF16)
    packed_ref[...] = (
        dot_tn(rows_of(line_ref[...], half), rows) + dot_tn(extra, small)
    ).astype(BF16)


def unpack_last_body(peers, line_ref, packed_ref, rows_ref, small_ref):
    stride = packed_ref.shape[0] // peers
    rows_ref[...] = dot(rows_of(line_ref[...], rows_ref.shape[0]), packed_ref[...]).astype(BF16)
    flush(rows_ref)
    halves = dot(extra_slots(8, peers, stride, stride - EXTRA), packed_ref[...])
    small_ref[...] = jnp.concatenate(
        [halves[:4] + halves[4:], jnp.zeros((4, small_ref.shape[1]), F32)], axis=0
    )


def grads_in_body(core_ref, own_ref, other_ref, og_ref, turned_ref):
    half = own_ref.shape[0]
    og_ref[own_rows(core_ref, half), :] = own_ref[...]
    og_ref[their_rows(core_ref, half), :] = other_ref[...]
    turned_ref[...] = og_ref[...].T


def relative_block(order, place):
    steps = len(order)
    return sum(((place >> (steps - 1 - at)) & 1) << bit for at, bit in enumerate(order))


def weights_into(plan, peers, me_ref, refs, outs):
    for side, (order, steps) in enumerate(plan):
        keep, send = outs[2 * side], outs[2 * side + 1]
        at = 0
        for left, rights in steps:
            width = refs[left].shape[0]
            size = width // peers

            def rows(first, last):
                ref = need(refs[left], 0)
                if order is None:
                    return ref[first * size : last * size, :]
                blocks = [
                    ref[pl.ds(pl.multiple_of((relative_block(order, p) ^ me_ref[0]) * size, size), size), :]
                    for p in range(first, last)
                ]
                return jnp.concatenate(blocks, axis=0)

            for out, left_rows in ((send, rows(peers // 2, peers)), (keep, rows(0, peers // 2))):
                edge = at
                for right, low, high in rights:
                    out[: width // 2, edge : edge + high - low] = dot(
                        left_rows, refs[right][:, low:high]
                    ).astype(BF16)
                    edge += high - low
            at = edge
        flush(keep)


def weight_body(plan, peers, me_ref, *refs):
    weights_into(plan, peers, me_ref, refs, refs[-2 * len(plan) :])


def split_sum(kept, arrived, keep, send, columns=slice(None), skip=0):
    half = kept.shape[0] // 2
    send[skip : skip + half, columns] = (kept[half:].astype(F32) + arrived[half:].astype(F32)).astype(BF16)
    keep[:, columns] = (kept[:half].astype(F32) + arrived[:half].astype(F32)).astype(BF16)


def weight_add_body(plan, peers, me_ref, *refs):
    keep_a, send_x, keep_b, send_y, keep_ca, keep_cb = refs[-6:]
    ca, from_x, cb, from_y = refs[-10:-6]
    weights_into(plan, peers, me_ref, refs, [keep_a, send_x, keep_b, send_y])
    skip = keep_a.shape[0]
    split_sum(need(ca, 0)[...], from_x[...], keep_ca, send_y, skip=skip)
    split_sum(need(cb, 0)[...], from_y[...], keep_cb, send_x, skip=skip)


def add_both_body(
    sa, sb, ca, cb, from_x, from_y,
    keep_sa, keep_sb, send_x, send_y, keep_c, send_z,
):
    skip, wide = sa.shape[0], ca.shape[1]
    split_sum(sa[...], from_x[:skip], keep_sa, send_y)
    split_sum(sb[...], from_y[:skip], keep_sb, send_x)
    split_sum(ca[...], from_y[skip:], keep_c, send_z, slice(0, wide))
    split_sum(cb[...], from_x[skip:], keep_c, send_z, slice(wide, 2 * wide))


def add_last_body(sa, sb, c, from_x, from_y, from_z, keep_s, send_z, keep_c, send_w):
    wide = sa.shape[1]
    split_sum(sa[...], from_y[...], keep_s, send_z, slice(0, wide))
    split_sum(sb[...], from_x[...], keep_s, send_z, slice(wide, 2 * wide))
    split_sum(c[...], from_z[...], keep_c, send_w)


def weight_halves(me, peers, orders, sides, after=(), weight=WEIGHT, also=None):
    args, plan, outs = [me], [], []
    flops = 0

    def place(array):
        far = isinstance(array, Far)
        for i, known in enumerate(args):
            if known is array or (far and isinstance(known, Far) and known.array is array.array):
                return i
        args.append(array)
        return len(args) - 1

    for order, side in zip(orders, sides):
        steps, total = [], 0
        for left, rights in side:
            width, rows = left.shape
            if (width // peers) % 16:
                array = left.array if isinstance(left, Far) else left
                blocks = np.array([relative_block(order, p) for p in range(peers)])
                index = (blocks ^ me[0])[:, None] * (width // peers) + np.arange(width // peers)
                left = jnp.take(array, index.reshape(-1), axis=0)
                order_here = None
            else:
                order_here = order
            steps.append((
                place(left) - 1,
                tuple((place(right) - 1, low, high) for right, low, high in rights),
            ))
            columns = sum(high - low for _, low, high in rights)
            total += columns
            flops += 2 * rows * width * columns
        plan.append((order_here, tuple(steps)))
        outs += pieces(width // 2, total)
    body = weight_body
    if also is not None:
        body = weight_add_body
        args += also
        keep_a, send_a, keep_b, send_b = outs
        tall = shape((width // 2 + also[0].shape[0] // 2, total), BF16)
        small = Far(shape((also[0].shape[0] // 2, also[0].shape[1]), BF16))
        outs = [keep_a, tall, keep_b, tall, small, small]
    return call(
        partial(body, tuple(plan), peers), outs, args, flops=flops, smem=(0,),
        after=after, weight=weight,
    )


def add_split_body(*refs):
    count = len(refs) // 4
    for i in range(count):
        kept, arrived = refs[2 * i], refs[2 * i + 1]
        keep, send = refs[2 * count + 2 * i], refs[2 * count + 2 * i + 1]
        half = keep.shape[0]
        send[...] = (kept[half:].astype(F32) + arrived[half:].astype(F32)).astype(BF16)
        flush(send)
        keep[...] = (kept[:half].astype(F32) + arrived[:half].astype(F32)).astype(BF16)
        flush(keep)


def add_join_body(*refs):
    keep, send = refs[-2:]
    half, at = keep.shape[0], 0
    for i in range(len(refs) // 2 - 1):
        kept, arrived = refs[2 * i], refs[2 * i + 1]
        columns = slice(at, at + kept.shape[1])
        at += kept.shape[1]
        send[:, columns] = (kept[half:].astype(F32) + arrived[half:].astype(F32)).astype(BF16)
        keep[:, columns] = (kept[:half].astype(F32) + arrived[:half].astype(F32)).astype(BF16)


def finish_body(moves, kept_ref, arrived_ref, *outs):
    total = kept_ref[...].astype(F32) + arrived_ref[...].astype(F32)
    for out, index, spans in moves:
        at = 0
        for low, high in spans:
            part = total[:, low:high]
            edge = at + high - low
            if index is None:
                outs[out][:, at:edge] = part
            else:
                outs[out][index, :, at:edge] = part
            at = edge


def exchange_rows(packed, peers):
    dims = packed.shape
    blocks = packed.reshape(peers, dims[0] // peers, dims[1])
    return lax.all_to_all(blocks, "dp", split_axis=0, concat_axis=0, tiled=True).reshape(dims)


def swap(values):
    return lax.ppermute(values, "mp", [(0, 1), (1, 0)])


def neighbour(values, bit, peers):
    return lax.ppermute(values, "dp", [(i, i ^ (1 << bit)) for i in range(peers)])


def pieces(rows, *columns):
    return [kind(shape((rows, n), BF16)) for n in columns for kind in (Far, lambda s: s)]


class Sum:
    def __init__(self, halves, orders, peers):
        self.halves, self.orders, self.peers, self.place = halves, orders, peers, 0
        self.send()

    def send(self):
        self.arrived = [
            neighbour(self.halves[2 * i + 1], order[self.place], self.peers)
            for i, order in enumerate(self.orders[: len(self.halves) // 2])
        ]
        self.place += 1

    def pairs(self):
        return [
            a for i, got in enumerate(self.arrived) for a in (self.halves[2 * i], got)
        ]

    def step(self, after=()):
        kept = self.halves[0::2]
        half = kept[0].shape[0] // 2
        if half % 16:
            total = (kept[0].astype(F32) + self.arrived[0].astype(F32)).astype(BF16)
            self.halves = [total[:half], total[half:]]
        elif self.place < len(self.orders) or len(kept) == 1:
            outs = pieces(half, *(k.shape[1] for k in kept))
            self.halves = call(add_split_body, outs, self.pairs(), after=after, weight=LIGHT)
        else:
            outs = pieces(half, sum(k.shape[1] for k in kept))
            self.halves = call(add_join_body, outs, self.pairs(), after=after, weight=LIGHT)
        self.send()
        return self.halves[0]

    def finish(self, outs, moves, after=(), weight=LIGHT):
        while self.place < len(self.orders[0]):
            self.step()
        return call(
            partial(finish_body, moves), [Far(o) for o in outs], self.pairs(), after=after, weight=weight
        )


def local(
    hidden_in,
    memory,
    output_grad,
    segment_ids,
    route_counts,
    norm_gains,
    self_qkv,
    self_out,
    cross_qkv,
    cross_out,
    ff_in,
    ff_out,
    rel_bias,
):
    peers = lax.axis_size("dp")
    me = lax.axis_index("dp")
    core = lax.axis_index("mp")
    core_ref = core.astype(jnp.int32)[None]
    half_rows, width = hidden_in.shape
    rows = 2 * half_rows
    capacity = 2 * (half_rows // peers)
    buckets, heads = rel_bias.shape
    columns = self_out.shape[0]
    units = ff_out.shape[0]
    block = width // peers
    bits = peers.bit_length() - 1
    rest = tuple(range(3, bits))
    orders = ((0, 1, 2) + rest, (1, 2, 0) + rest, (2, 0, 1) + rest)
    pair_orders = ((0, 1, 2) + rest, (1, 0, 2) + rest)
    me_ref = me.astype(jnp.int32)[None]
    slots = peers * capacity
    wide, narrow = shape((rows, width), BF16), shape((rows, columns), BF16)
    wide32, gain_shape = shape((rows, width), F32), shape((1, width), F32)
    half16, half32 = shape((half_rows, width), BF16), shape((half_rows, width), F32)
    more16 = shape((rows + half_rows, width), BF16)
    turned = shape((width, rows), BF16)
    probs_shape = shape((heads, rows, rows), BF16)
    square = rows * width * columns
    scores = heads * rows * rows

    packed, sent = call(
        pack_body,
        [shape((slots, 2 * width), BF16), Far(shape((1, slots), jnp.int32))],
        [route_counts, me_ref, Far(hidden_in), Far(memory)],
        smem=(0, 1),
    )
    arrived = exchange_rows(packed, peers)

    gains = norm_gains.astype(F32)
    gain_one, gain_two, gain_three = gains[0:1], gains[1:2], gains[2:3]
    edges = bucket_edges(buckets, MAX_DIST)
    offset = MAX_DIST - np.arange(3 * MAX_DIST)
    bucket_of = np.where(
        (offset >= 0), np.searchsorted(edges, offset, side="right"), buckets - 1
    )
    bucket_hot = bucket_of[:, None] == np.arange(buckets)[None, :]
    lines = jnp.dot(
        bucket_hot[: 2 * MAX_DIST].astype(jnp.bfloat16), rel_bias, preferred_element_type=F32
    ).T
    line = Far(shape((1, slots), jnp.int32))
    line_wide = Far(shape((1, slots + peers * EXTRA), jnp.int32))
    bias, mask, taken, sent_wide, taken_wide = call(
        tables_body,
        [
            Far(shape((heads, TILE, rows), BF16)), Far(shape((rows, rows), F32)), line, line_wide,
            line_wide,
        ],
        [route_counts, me_ref, lines, segment_ids],
        smem=(0, 1),
        after=[sent],
    )
    og, og_turned = call(
        grads_in_body,
        [Far(wide), Far(turned)],
        [core_ref, output_grad, swap(output_grad)],
        smem=(0,),
        after=[mask],
    )
    [own] = call(
        unpack_body,
        [shape((half_rows, 2 * width), BF16)],
        [taken, arrived],
        after=[mask, og_turned],
    )
    other = swap(own)

    by_head = partial(Far, axis=0, count=heads)
    x, n1_turned, sq, sk, sv, self_probs, self_mix, part_one = call(
        self_forward_body,
        [
            Far(wide), Far(turned), Far(narrow), Far(narrow), Far(narrow), by_head(probs_shape),
            Far(narrow), wide,
        ],
        [core_ref, own, other, gain_one, self_qkv, mask, bias, self_out],
        flops=8 * square + 8 * scores * HEAD_DIM,
        scratch=[pltpu.VMEM((rows, width), BF16)],
        smem=(0,),
    )
    part_there = swap(part_one)
    ck, cv, mem_turned = call(
        keys_body,
        [narrow, narrow, Far(turned)],
        [core_ref, own, other, cross_qkv],
        flops=4 * square,
        scratch=[pltpu.VMEM((rows, width), BF16)],
        smem=(0,),
        after=[x],
    )
    h1, h1_far, n2_turned, cq, cross_probs, cross_mix, part_two = call(
        cross_forward_body,
        [wide32, Far(wide32), Far(turned), Far(narrow), by_head(probs_shape), Far(narrow), wide],
        [part_one, part_there, Far(x), gain_two, cross_qkv, ck, mask, cv, cross_out],
        flops=4 * square + 8 * scores * HEAD_DIM,
        scratch=[pltpu.VMEM((rows, width), BF16)],
    )
    n3_turned, h2, act, d_pre, base, pack3 = call(
        ff_body,
        [turned, wide32, shape((rows, units), BF16), shape((rows, units), BF16), half32, more16],
        [core_ref, part_two, swap(part_two), h1, gain_three, ff_in, og, ff_out],
        flops=8 * rows * width * units,
        scratch=[
            pltpu.VMEM((rows, width), F32), pltpu.VMEM((rows, width), F32),
            pltpu.VMEM((rows, width), BF16),
        ],
        smem=(0,),
    )
    pack3_there = swap(pack3)

    third = 2 * units // 3
    ff_sum = Sum(
        weight_halves(me_ref, peers, orders, [
            [(Far(og_turned), [(act, 0, third)])],
            [
                (Far(og_turned), [(act, third, units)]),
                (n3_turned, [(d_pre, 0, 2 * third - units)]),
            ],
            [(n3_turned, [(d_pre, 2 * third - units, units)])],
        ]),
        orders, peers,
    )
    g2, g2_turned, dcq, dck, dcv, pack2, d_mem, dgain3, block_out = call(
        cross_back_body,
        [
            Far(wide32), turned, narrow, narrow, narrow, Far(more16), half32, Far(gain_shape), Far(half16),
        ],
        [
            core_ref, pack3, pack3_there, h2, og, gain_three, cross_out, cv,
            cross_probs, ck, cq, cross_qkv, base,
        ],
        flops=8 * square + 14 * scores * HEAD_DIM,
        scratch=[
            pltpu.VMEM((rows, columns), BF16), pltpu.VMEM((rows, width), F32),
            pltpu.VMEM((rows, width), BF16),
        ],
        smem=(0,),
        after=[ff_sum.halves[0]],
    )
    pack2_there = swap(pack2)
    cross_sum = Sum(
        weight_halves(me_ref, peers, pair_orders, [
            [(g2_turned, [(cross_mix, 0, columns)]), (n2_turned, [(dcq, 0, columns)])],
            [(mem_turned, [(dck, 0, columns), (dcv, 0, columns)])],
        ]),
        pair_orders, peers,
    )
    mem_packed, mem_token = call(
        pack_sum_body, [shape((slots, width), BF16), Far(shape((8, 128), F32))], [taken, d_mem, pack2_there],
        after=[cross_sum.halves[0]],
        weight=LIGHT,
    )
    mem_back = exchange_rows(mem_packed, peers)
    ff_token = ff_sum.step(after=[mem_token])
    g1_own, g1_turned, dsq, dsk, dsv, dn1, dn1_sent, dgain2, diag = call(
        self_back_body,
        [Far(half32), turned, narrow, narrow, narrow, Far(half32), half16, Far(gain_shape),
         Far(shape((heads, 8, 3 * MAX_DIST), F32))],
        [
            core_ref, Far(pack2), pack2_there, h1_far, g2, gain_two, self_out, Far(sv),
            Far(self_probs), Far(sk), Far(sq), Far(self_qkv),
        ],
        flops=8 * square + 14 * scores * HEAD_DIM,
        scratch=[
            pltpu.VMEM((rows, columns), BF16), pltpu.VMEM((rows, width), F32),
            pltpu.VMEM((rows, width), BF16),
        ],
        smem=(0,),
        after=[ff_token],
    )

    def unpack(values, line):
        return call(unpack_body, [Far(half16)], [line, values], weight=LIGHT)[0]

    dn1_there = swap(dn1_sent)
    self_sides = [
        [(g1_turned, [(Far(self_mix), 0, columns)]), (Far(n1_turned), [(dsq, 0, columns)])],
        [(Far(n1_turned), [(dsk, 0, columns), (dsv, 0, columns)])],
    ]
    merged = bits == 4
    if merged:
        ca, _, cb, _ = cross_sum.halves
        keep_sa, send_x, keep_sb, send_y, keep_ca, keep_cb = weight_halves(
            me_ref, peers, pair_orders, self_sides, weight=AFTER_SELF, after=[dgain2],
            also=[ca, cross_sum.arrived[0], cb, cross_sum.arrived[1]],
        )
        from_x, from_y = neighbour(send_x, 0, peers), neighbour(send_y, 1, peers)
        self_token = keep_sa
    else:
        self_sum = Sum(
            weight_halves(
                me_ref, peers, pair_orders, self_sides, weight=AFTER_SELF, after=[dgain2]
            ),
            pair_orders, peers,
        )
        self_token = self_sum.halves[0]
    ff_token = self_token
    if FF_FIRST:
        ff_token = ff_sum.step(after=[self_token])
    [packed] = call(
        partial(last_body, peers),
        [shape((slots + peers * EXTRA, width), BF16)],
        [
            core_ref, taken_wide, dn1_there, Far(dn1), Far(x), gain_one, Far(g1_own), dgain2, dgain3,
            diag, jnp.asarray(bucket_hot, F32),
        ],
        smem=(0,),
        after=[ff_token, Near(mem_back)],
        weight=LIGHT,
    )
    back = exchange_rows(packed, peers)
    token = Near(packed)
    half = width // 8
    if merged:
        if not FF_FIRST:
            token = ff_sum.step(after=[token])
        wide_pair = columns * 4

        def two():
            keep_sa2, keep_sb2, send_x2, send_y2, keep_c, send_z = call(
                add_both_body,
                [Far(shape((2 * half, 2 * columns), BF16))] * 2
                + [shape((2 * half, 2 * columns), BF16)] * 2
                + [Far(shape((half, wide_pair), BF16)), shape((half, wide_pair), BF16)],
                [keep_sa, keep_sb, keep_ca, keep_cb, from_x, from_y],
                after=[token],
                weight=LIGHT,
            )
            return keep_sa2, keep_sb2, keep_c, (
                neighbour(send_x2, 0, peers), neighbour(send_y2, 1, peers), neighbour(send_z, 2, peers)
            )

        if TWO_FIRST:
            keep_sa2, keep_sb2, keep_c, arrived_two = two()
            token = ff_sum.step(after=[keep_sa2])
        else:
            token = ff_sum.step(after=[token])
            keep_sa2, keep_sb2, keep_c, arrived_two = two()
            token = keep_sa2
        keep_s, send_z, keep_c, send_w = call(
            add_last_body,
            pieces(half, wide_pair) + pieces(half // 2, wide_pair),
            [keep_sa2, keep_sb2, keep_c, *arrived_two],
            after=[token],
            weight=LIGHT,
        )
        cross_arrived, from_z = neighbour(send_w, 3, peers), neighbour(send_z, 2, peers)
        keep_s, send_w = call(
            add_split_body, pieces(half // 2, wide_pair), [keep_s, from_z], weight=LIGHT
        )
        self_arrived = neighbour(send_w, 3, peers)
        cross_pair, self_pair = [keep_c, cross_arrived], [keep_s, self_arrived]
    else:
        for group in (cross_sum, ff_sum, self_sum, cross_sum, ff_sum, self_sum):
            token = group.step(after=[token])
        for group in (cross_sum, self_sum):
            while group.place < bits:
                group.step()
        cross_pair, self_pair = cross_sum.pairs(), self_sum.pairs()
    ff_in_total, ff_out_total = ff_sum.finish(
        [shape((block, units), F32), shape((block, units), F32)],
        ((0, None, [(units, 2 * units)]), (1, None, [(0, units)])),
        weight=LAST_WEIGHT,
    )
    memory_grad = unpack(mem_back, sent)
    input_grad, small = call(
        partial(unpack_last_body, peers),
        [Far(half16), shape((8, width), F32)],
        [sent_wide, back],
        after=[ff_in_total, memory_grad],
        weight=LIGHT,
    )
    moves = ((0, None, [(0, columns)]),) + tuple(
        (1, i, [((i + 1) * columns, (i + 2) * columns)]) for i in range(3)
    )

    def finish(pair, after):
        outs = [Far(shape((block, columns), F32)), Far(shape((3, block, columns), F32))]
        return call(partial(finish_body, moves), outs, pair, after=after, weight=LIGHT)

    cross_out_total, cross_qkv_total = finish(cross_pair, [input_grad])
    self_out_total, self_qkv_total = finish(self_pair, [cross_out_total])
    small = small + swap(small)
    gains_total = small[:3]
    bias_total = small[3, : 2 * heads * buckets].reshape(heads, 2, buckets).transpose(2, 1, 0)
    bias_total = bias_total.reshape(buckets, 2 * heads)
    return (
        block_out,
        input_grad,
        memory_grad,
        gains_total,
        bias_total,
        self_qkv_total,
        self_out_total.T,
        cross_qkv_total,
        cross_out_total.T,
        ff_in_total,
        ff_out_total.T,
    )


def solution(mesh):
    both = ("dp", "mp")
    in_specs = (
        P(both, None),
        P(both, None),
        P(both, None),
        P("dp", None),
        P(),
        P(),
        P(None, None, "mp"),
        P("mp", None),
        P(None, None, "mp"),
        P("mp", None),
        P(None, "mp"),
        P("mp", None),
        P(None, "mp"),
    )
    out_specs = (
        P(both, None),
        P(both, None),
        P(both, None),
        P(),
        P(),
        P(None, "dp", "mp"),
        P("mp", "dp"),
        P(None, "dp", "mp"),
        P("mp", "dp"),
        P("dp", "mp"),
        P("mp", "dp"),
    )
    return jax.shard_map(local, mesh=mesh, in_specs=in_specs, out_specs=out_specs, check_vma=False)
```

```python
from functools import partial

import jax
import jax.numpy as jnp
import numpy as np
from jax import lax
from jax.experimental import pallas as pl
from jax.experimental.pallas import tpu as pltpu
from jax.sharding import PartitionSpec as P

HEAD_DIM = 64
MAX_DIST = 128
EPS = 1e-06
MASKED = -1e30
TILE = 256
F32 = jnp.float32
BF16 = jnp.bfloat16
VMEM_LIMIT = 24 * 1024 * 1024
WEIGHT = 3 * 10**10
LIGHT = 10**6
AFTER_SELF = 3 * 10**9
LAST_WEIGHT = 7 * 10**9
FF_STEPS = 3
EXTRA = 8


def bucket_edges(buckets, distance):
    exact_span = buckets // 2
    edge_list = []
    for offset in range(1, 4 * distance):
        if offset < exact_span:
            bucket_now = offset
        else:
            log_ratio = np.log(offset / exact_span) / np.log(distance / exact_span)
            bucket_now = min(buckets - 1, exact_span + int(log_ratio * (buckets - exact_span)))
        while len(edge_list) < bucket_now:
            edge_list.append(offset)
    return np.array(edge_list, dtype=np.int32)


def dot(a, b):
    return jnp.dot(a, b, preferred_element_type=F32)


def dot_nt(a, b):
    return lax.dot_general(a, b, (((1,), (1,)), ((), ())), preferred_element_type=F32)


def dot_tn(a, b):
    return lax.dot_general(a, b, (((0,), (0,)), ((), ())), preferred_element_type=F32)


def rms_scale(values):
    return lax.rsqrt(jnp.mean(values * values, axis=-1, keepdims=True) + EPS)


def norm_back(values, gain_row, upstream):
    scale = rms_scale(values)
    scaled = gain_row * upstream
    back = scale * scaled - values * (
        scale * scale * scale * jnp.mean(scaled * values, axis=-1, keepdims=True)
    )
    return back, upstream * values * scale


class Near:
    def __init__(self, array):
        self.array = array


class Far:
    def __init__(self, array, axis=0, count=1):
        self.array, self.axis, self.count = array, axis, count
        self.shape, self.dtype = array.shape, array.dtype


def part(ref, axis, count, i):
    size = ref.shape[axis] // count
    index = tuple(
        pl.ds(i * size, size) if at == axis else slice(None) for at in range(len(ref.shape))
    )
    return ref.at[index]


class Inbound:
    def __init__(self, ref, copies):
        self.ref, self.copies, self.shape = ref, copies, ref.shape
        self.waiting = set(range(len(copies)))

    def need(self, i):
        if i in self.waiting:
            self.waiting.discard(i)
            self.copies[i].wait()

    def __getitem__(self, index):
        for i in range(len(self.copies)):
            self.need(i)
        return self.ref[index]


class Outbound:
    def __init__(self, ref, copies):
        self.ref, self.copies, self.shape, self.dtype = ref, copies, ref.shape, ref.dtype
        self.pending, self.flying = set(range(len(copies))), set()

    def __getitem__(self, index):
        return self.ref[index]

    def __setitem__(self, index, value):
        self.ref[index] = value

    def flush(self, i=None):
        for at in sorted(self.pending) if i is None else [i]:
            self.pending.discard(at)
            self.flying.add(at)
            self.copies[at].start()

    def end(self):
        self.flush()
        for at in sorted(self.flying):
            self.copies[at].wait()


def need(ref, i):
    if isinstance(ref, Inbound):
        ref.need(i % len(ref.copies))
        return ref.ref
    return ref


def flush(*refs, i=None):
    for ref in refs:
        if isinstance(ref, Outbound):
            ref.flush(i)


def call(body, outs, args, flops=0, scratch=(), smem=(), after=(), weight=WEIGHT):
    count, extra, made = len(args), len(after), len(outs)
    far_in = [i for i in range(count) if isinstance(args[i], Far)]
    far_out = [i for i in range(made) if isinstance(outs[i], Far)]
    arrays = [a.array if isinstance(a, Far) else a for a in args]
    shapes = [o.array if isinstance(o, Far) else o for o in outs]
    size = sum(a.size * a.dtype.itemsize for a in arrays + shapes)
    sems = sum(args[i].count for i in far_in) + sum(outs[i].count for i in far_out)

    given = [
        pltpu.with_memory_space_constraint(a, pltpu.HBM) if i in far_in else a
        for i, a in enumerate(arrays)
    ]

    def kernel(*refs):
        ins, refs = list(refs[:count]), refs[count + extra :]
        to, refs = list(refs[:made]), refs[made:]
        rooms, refs = refs[: len(far_in)], refs[len(far_in) :]
        shelves, rest = refs[: len(far_out)], refs[len(far_out) :]
        if sems:
            sem, rest = rest[0], rest[1:]
        at = 0
        for i, room in zip(far_in, rooms):
            copies = []
            for j in range(args[i].count):
                cut = (args[i].axis, args[i].count, j)
                copies.append(
                    pltpu.make_async_copy(part(ins[i], *cut), part(room, *cut), sem.at[at])
                )
                copies[-1].start()
                at += 1
            ins[i] = Inbound(room, copies)
        for i, shelf in zip(far_out, shelves):
            copies = []
            for j in range(outs[i].count):
                cut = (outs[i].axis, outs[i].count, j)
                copies.append(
                    pltpu.make_async_copy(part(shelf, *cut), part(to[i], *cut), sem.at[at])
                )
                at += 1
            to[i] = Outbound(shelf, copies)
        body(*ins, *to, *rest)
        for i in far_in:
            for j in sorted(ins[i].waiting):
                ins[i].need(j)
        for i in far_out:
            to[i].flush()
        for i in far_out:
            to[i].end()

    hbm, vmem = pl.BlockSpec(memory_space=pltpu.HBM), pl.BlockSpec(memory_space=pltpu.VMEM)
    return pl.pallas_call(
        kernel,
        out_shape=[
            (pltpu.HBM if i in far_out else pltpu.VMEM)(o.shape, o.dtype) for i, o in enumerate(shapes)
        ],
        in_specs=[
            pl.BlockSpec(memory_space=pltpu.SMEM) if i in smem else hbm if i in far_in else vmem
            for i in range(count)
        ]
        + [pl.BlockSpec(memory_space=pl.ANY) if isinstance(a, Near) else hbm for a in after],
        out_specs=[hbm if i in far_out else vmem for i in range(made)],
        scratch_shapes=[pltpu.VMEM(arrays[i].shape, arrays[i].dtype) for i in far_in]
        + [pltpu.VMEM(shapes[i].shape, shapes[i].dtype) for i in far_out]
        + ([pltpu.SemaphoreType.DMA((sems,))] if sems else [])
        + list(scratch),
        compiler_params=pltpu.CompilerParams(vmem_limit_bytes=VMEM_LIMIT),
        cost_estimate=pl.CostEstimate(
            flops=int(weight), bytes_accessed=0, transcendentals=0
        ),
    )(
        *given,
        *(
            a.array if isinstance(a, Near) else pltpu.with_memory_space_constraint(a, pltpu.HBM)
            for a in after
        ),
    )


def shape(dims, dtype):
    return jax.ShapeDtypeStruct(dims, dtype)


def own_rows(core_ref, half):
    return pl.ds(pl.multiple_of(core_ref[0] * half, half), half)


def their_rows(core_ref, half):
    return pl.ds(pl.multiple_of((1 - core_ref[0]) * half, half), half)


def tables_body(
    counts_ref, me_ref, vec_ref, ids_ref, bias_ref, mask_ref, taken_ref, sent_wide_ref, taken_wide_ref
):
    peers = counts_ref.shape[0]
    capacity = taken_ref.shape[1] // peers
    taken_ref[...] = slot_line(lambda s: counts_ref[s, me_ref[0]], peers, capacity)
    stride = capacity + EXTRA
    sent_wide_ref[...] = slot_line(lambda o: counts_ref[me_ref[0], o], peers, stride)
    taken_wide_ref[...] = slot_line(lambda s: counts_ref[s, me_ref[0]], peers, stride)
    heads, rows = bias_ref.shape[0], mask_ref.shape[0]
    row = lax.broadcasted_iota(jnp.int32, (MAX_DIST, 2 * MAX_DIST), 0)
    column = lax.broadcasted_iota(jnp.int32, (MAX_DIST, 2 * MAX_DIST), 1)
    for head in range(heads):
        line = vec_ref[head : head + 1, :]
        near = pltpu.roll(
            jnp.broadcast_to(line, (MAX_DIST, 2 * MAX_DIST)), 0, 1, stride=1, stride_axis=0
        )
        near = jnp.where(column > row + MAX_DIST, MASKED, near)
        far = jnp.broadcast_to(line[:, 2 * MAX_DIST - 1 :], (MAX_DIST, MAX_DIST))
        none = jnp.full((MAX_DIST, MAX_DIST), MASKED, F32)
        upper = jnp.concatenate([far, near, none], axis=1)
        lower = jnp.concatenate([far, far, near], axis=1)
        bias_ref[head] = jnp.concatenate([upper, lower], axis=0).astype(BF16)
    ids = ids_ref[...].astype(F32)
    down = jnp.broadcast_to(ids, (128, rows)).T[:, :1]
    mask_ref[...] = jnp.where(down == ids, 0.0, MASKED)


def slot_line(count_of, peers, capacity):
    lane = lax.broadcasted_iota(jnp.int32, (1, peers * capacity), 1)
    line = jnp.full_like(lane, -1)
    start = jnp.int32(0)
    for peer in range(peers):
        count, within = count_of(peer), lane - peer * capacity
        line = jnp.where((within >= 0) & (within < count), start + within, line)
        start = start + count
    return line


def rows_of(line, rows):
    row = lax.broadcasted_iota(jnp.int32, (rows, line.shape[1]), 0)
    return (line == row).astype(BF16)


def pack_body(counts_ref, me_ref, a_ref, b_ref, packed_ref, sent_ref):
    peers, (half, width) = counts_ref.shape[0], a_ref.shape
    capacity = packed_ref.shape[0] // peers
    sent = slot_line(lambda o: counts_ref[me_ref[0], o], peers, capacity)
    sent_ref[...] = sent
    flush(sent_ref)
    slots = rows_of(sent, half)
    packed_ref[:, :width] = dot_tn(slots, a_ref[...]).astype(BF16)
    packed_ref[:, width:] = dot_tn(slots, b_ref[...]).astype(BF16)


def pack_sum_body(line_ref, a_ref, b_ref, packed_ref, token_ref):
    half = a_ref.shape[0]
    skip = b_ref.shape[0] - half
    token_ref[...] = jnp.zeros_like(token_ref)
    rows = (a_ref[...] + b_ref[skip:].astype(F32)).astype(BF16)
    packed_ref[...] = dot_tn(rows_of(line_ref[...], half), rows).astype(BF16)


def unpack_body(line_ref, packed_ref, rows_ref):
    rows_ref[...] = dot(rows_of(line_ref[...], rows_ref.shape[0]), packed_ref[...]).astype(BF16)


def lane_half(values, which):
    lane = lax.broadcasted_iota(jnp.int32, values.shape, 1)
    keep = (lane < HEAD_DIM) if which == 0 else (lane >= HEAD_DIM)
    return jnp.where(keep, values, jnp.zeros_like(values))


def attend(q_ref, k_ref, v_ref, mask_ref, bias_ref, probs_ref, mix_ref):
    rows, columns = q_ref.shape
    causal = bias_ref is not None
    for pair in range(columns // (2 * HEAD_DIM)):
        lanes = slice(pair * 2 * HEAD_DIM, (pair + 1) * 2 * HEAD_DIM)
        for tile in range(rows // TILE):
            here = slice(tile * TILE, (tile + 1) * TILE)
            reach = (tile + 1) * TILE if causal else rows
            q, k, v = q_ref[here, lanes], k_ref[:reach, lanes], v_ref[:reach, lanes]
            mixed = None
            for which in range(2):
                head = 2 * pair + which
                scores = dot_nt(lane_half(q, which), k) + mask_ref[here, :reach]
                if causal:
                    bias = need(bias_ref, head)[head, :, rows - reach :]
                    scores = scores + bias.astype(F32)
                peak = jnp.max(scores, axis=-1, keepdims=True)
                weights = jnp.exp(scores - peak)
                total = jnp.sum(weights, axis=-1, keepdims=True)
                probs = (weights * (1.0 / total)).astype(BF16)
                probs_ref[head, here, :reach] = probs
                each = dot(probs, lane_half(v, which))
                mixed = each if mixed is None else mixed + each
            mix_ref[here, lanes] = mixed.astype(BF16)
        flush(probs_ref, i=2 * pair)
        flush(probs_ref, i=2 * pair + 1)
    flush(mix_ref)


def attend_back(
    q_ref, k_ref, v_ref, probs_ref, d_mix_ref, dq_ref, dk_ref, dv_ref, diag_ref, causal
):
    rows, columns = q_ref.shape
    for pair in range(columns // (2 * HEAD_DIM)):
        lanes = slice(pair * 2 * HEAD_DIM, (pair + 1) * 2 * HEAD_DIM)
        q_turned = q_ref[:, lanes].T
        d_turned = d_mix_ref[:, lanes].T
        dk_turned, dv_turned = [], []
        near = [None, None]
        for which in range(2):
            head = 2 * pair + which
            halves = slice(which * HEAD_DIM, (which + 1) * HEAD_DIM)
            dk_sum = dv_sum = None
            grown = None
            for tile in reversed(range(rows // TILE)):
                here = slice(tile * TILE, (tile + 1) * TILE)
                reach = (tile + 1) * TILE if causal else rows
                k, v = k_ref[:reach, lanes], v_ref[:reach, lanes]
                probs16 = need(probs_ref, head)[head, here, :reach]
                probs = probs16.astype(F32)
                d_probs = dot_nt(lane_half(d_mix_ref[here, lanes], which), v)
                product = probs * d_probs
                delta = jnp.sum(product, axis=-1, keepdims=True)
                d_scores = product - probs * delta
                d_scores16 = d_scores.astype(BF16)
                dq = dot(d_scores16, lane_half(k, which))
                if which == 0:
                    near[tile] = dq
                else:
                    dq_ref[here, lanes] = (near[tile] + dq).astype(BF16)
                dk = dot(q_turned[halves, here], d_scores16)
                dv = dot(d_turned[halves, here], probs16)
                if causal and reach < rows:
                    pad = jnp.zeros((HEAD_DIM, rows - reach), F32)
                    dk = jnp.concatenate([dk, pad], axis=1)
                    dv = jnp.concatenate([dv, pad], axis=1)
                dk_sum = dk if dk_sum is None else dk_sum + dk
                dv_sum = dv if dv_sum is None else dv_sum + dv
                if causal:
                    kept = d_scores16.astype(F32)
                    if reach < rows:
                        kept = jnp.concatenate(
                            [jnp.zeros((TILE, rows - reach), F32), kept], axis=1
                        )
                    grown = kept if grown is None else grown + kept
            dk_turned.append(dk_sum)
            dv_turned.append(dv_sum)
            if causal:
                d = MAX_DIST
                close = grown[:d, d : 3 * d] + grown[d:, 2 * d :]
                row = lax.broadcasted_iota(jnp.int32, close.shape, 0)
                turned, shift = close, 1
                while shift < d:
                    moved = pltpu.roll(turned, 2 * d - shift, 1)
                    turned = jnp.where((row & shift) > 0, moved, turned)
                    shift *= 2
                far = jnp.sum(grown[:d, :d] + grown[d:, :d] + grown[d:, d : 2 * d], axis=0)
                line = jnp.sum(turned, axis=0, keepdims=True)
                spread = jnp.concatenate([line, far[None]], axis=1)
                diag_ref[head] = jnp.broadcast_to(spread, (8, 3 * d))
        dk_ref[:, lanes] = jnp.concatenate(dk_turned, axis=0).T.astype(BF16)
        dv_ref[:, lanes] = jnp.concatenate(dv_turned, axis=0).T.astype(BF16)


def self_forward_body(
    core_ref, own_ref, other_ref, gain_ref, w_ref, mask_ref, bias_ref, wo_ref,
    x_ref, x_far_ref, nt_ref, q_ref, k_ref, v_ref, probs_ref, mix_ref, part_ref, n_ref,
):
    half, width = own_ref.shape[0], gain_ref.shape[1]
    x_ref[own_rows(core_ref, half), :] = own_ref[:, :width]
    x_ref[their_rows(core_ref, half), :] = other_ref[:, :width]
    x_far_ref[...] = x_ref[...]
    flush(x_far_ref)
    x = x_ref[...].astype(F32)
    n_ref[...] = (x * rms_scale(x) * gain_ref[...]).astype(BF16)
    for i, out in enumerate((q_ref, k_ref, v_ref)):
        out[...] = dot(n_ref[...], need(w_ref, i)[i]).astype(BF16)
    nt_ref[...] = n_ref[...].T
    flush(q_ref, k_ref, v_ref, nt_ref)
    attend(q_ref, k_ref, v_ref, mask_ref, bias_ref, probs_ref, mix_ref)
    part_ref[...] = dot(mix_ref[...], wo_ref[...]).astype(BF16)


def keys_body(core_ref, own_ref, other_ref, w_ref, k_ref, v_ref, memt_ref, mem_ref):
    half, width = own_ref.shape[0], w_ref.shape[1]
    mem_ref[own_rows(core_ref, half), :] = own_ref[:, width:]
    mem_ref[their_rows(core_ref, half), :] = other_ref[:, width:]
    for i, out in ((1, k_ref), (2, v_ref)):
        out[...] = dot(mem_ref[...], need(w_ref, i)[i]).astype(BF16)
    memt_ref[...] = mem_ref[...].T


def cross_forward_body(
    a_ref, b_ref, x_ref, gain_ref, w_ref, k_ref, mask_ref, v_ref, wo_ref,
    h_ref, h_far_ref, nt_ref, q_ref, probs_ref, mix_ref, part_ref, n_ref,
):
    h_ref[...] = x_ref[...].astype(F32) + (a_ref[...].astype(F32) + b_ref[...].astype(F32))
    h_far_ref[...] = h_ref[...]
    flush(h_far_ref)
    h = h_ref[...]
    n_ref[...] = (h * rms_scale(h) * gain_ref[...]).astype(BF16)
    q_ref[...] = dot(n_ref[...], need(w_ref, 0)[0]).astype(BF16)
    nt_ref[...] = n_ref[...].T
    flush(q_ref, nt_ref)
    attend(q_ref, k_ref, v_ref, mask_ref, None, probs_ref, mix_ref)
    part_ref[...] = dot(mix_ref[...], wo_ref[...]).astype(BF16)


def gelu_pair(v):
    scale = float(np.sqrt(2 / np.pi))
    square = v * v
    t = jnp.tanh(scale * (v + 0.044715 * (square * v)))
    half = 0.5 * (1.0 + t)
    slope = half + 0.5 * v * (1.0 - t * t) * (scale * (1.0 + 3 * 0.044715 * square))
    return v * half, slope


def ff_body(
    core_ref, a_ref, b_ref, h_ref, gain_ref, win_ref, og_ref, wout_ref,
    nt_ref, h2_ref, act_ref, d_pre_ref, base_ref, both_ref, out_sum, back_sum, n_ref,
):
    rows, half = h_ref.shape[0], h_ref.shape[0] // 2
    h = h_ref[...] + (a_ref[...].astype(F32) + b_ref[...].astype(F32))
    h2_ref[...] = h
    n_ref[...] = (h * rms_scale(h) * gain_ref[...]).astype(BF16)
    nt_ref[...] = n_ref[...].T
    steps = FF_STEPS
    block = win_ref.shape[1] // steps
    for step in range(steps):
        units = slice(step * block, (step + 1) * block)
        win, wout = need(win_ref, step), need(wout_ref, step)
        value, slope = gelu_pair(dot(n_ref[...], win[:, units]))
        act_ref[:, units] = value.astype(BF16)
        d_act = dot_nt(og_ref[...], wout[units, :])
        d_pre_ref[:, units] = (d_act * slope).astype(BF16)
        out = dot(act_ref[:, units], wout[units, :])
        back = dot_nt(d_pre_ref[:, units], win[:, units])
        if step:
            out, back = out_sum[...] + out, back_sum[...] + back
        out_sum[...] = out
        if step < steps - 1:
            back_sum[...] = back
        else:
            both_ref[:rows] = back.astype(BF16)
    own, theirs = own_rows(core_ref, half), their_rows(core_ref, half)
    both_ref[rows:] = out_sum[theirs, :].astype(BF16)
    base_ref[...] = h2_ref[own, :] + out_sum[own, :]


def gain_sum(core_ref, dgain):
    row = lax.broadcasted_iota(jnp.int32, dgain.shape, 0)
    half = dgain.shape[0] // 2
    mine = (row >= core_ref[0] * half) & (row < (core_ref[0] + 1) * half)
    return jnp.sum(jnp.where(mine, dgain, 0.0), axis=0, keepdims=True)


def cross_back_body(
    core_ref, a_ref, b_ref, h_ref, up_ref, gain_ref, wo_ref, v_ref, probs_ref, k_ref, q_ref,
    w_ref, base_ref,
    g_ref, gt_ref, dq_ref, dk_ref, dv_ref, both_ref, dmem_ref, dgain_ref, out_ref,
    d_mix_ref, dmem_sum, g16_ref,
):
    rows, half = h_ref.shape[0], h_ref.shape[0] // 2
    up = a_ref[:rows].astype(F32) + b_ref[:rows].astype(F32)
    dv, dgain = norm_back(h_ref[...], gain_ref[...], up)
    dgain_ref[...] = gain_sum(core_ref, dgain)
    g = up_ref[...].astype(F32) + dv
    g_ref[...] = g
    g16_ref[...] = g.astype(BF16)
    d_mix_ref[...] = dot_nt(g16_ref[...], wo_ref[...]).astype(BF16)
    gt_ref[...] = g16_ref[...].T
    attend_back(
        q_ref, k_ref, v_ref, probs_ref, d_mix_ref, dq_ref, dk_ref, dv_ref, None, False
    )
    both_ref[:rows] = dot_nt(dq_ref[...], w_ref[0]).astype(BF16)
    dmem_sum[...] = dot_nt(dk_ref[...], w_ref[1]) + dot_nt(dv_ref[...], w_ref[2])
    both_ref[rows:] = dmem_sum[their_rows(core_ref, half), :].astype(BF16)
    dmem_ref[...] = dmem_sum[own_rows(core_ref, half), :]
    out_ref[...] = (base_ref[...] + b_ref[rows:].astype(F32)).astype(BF16)


def self_back_body(
    core_ref, a_ref, b_ref, h_ref, up_ref, gain_ref, wo_ref, v_ref, probs_ref, k_ref, q_ref, w_ref,
    g_ref, gt_ref, dq_ref, dk_ref, dv_ref, dn_ref, sent_ref, dgain_ref, diag_ref,
    d_mix_ref, total, g16_ref,
):
    rows, half = h_ref.shape[0], h_ref.shape[0] // 2
    own, theirs = own_rows(core_ref, half), their_rows(core_ref, half)
    up = a_ref[:rows].astype(F32) + b_ref[:rows].astype(F32)
    dv, dgain = norm_back(h_ref[...], gain_ref[...], up)
    dgain_ref[...] = gain_sum(core_ref, dgain)
    total[...] = up_ref[...] + dv
    g_ref[...] = total[own, :]
    g16_ref[...] = total[...].astype(BF16)
    d_mix_ref[...] = dot_nt(g16_ref[...], wo_ref[...]).astype(BF16)
    gt_ref[...] = g16_ref[...].T
    attend_back(
        q_ref, k_ref, v_ref, probs_ref, d_mix_ref, dq_ref, dk_ref, dv_ref, diag_ref, True
    )
    total[...] = (
        dot_nt(dq_ref[...], w_ref[0]) + dot_nt(dk_ref[...], w_ref[1]) + dot_nt(dv_ref[...], w_ref[2])
    )
    sent_ref[...] = total[theirs, :].astype(BF16)
    dn_ref[...] = total[own, :]


def extra_slots(count, peers, stride, place):
    lane = lax.broadcasted_iota(jnp.int32, (count, peers * stride), 1)
    row = lax.broadcasted_iota(jnp.int32, (count, peers * stride), 0)
    hot = lane < 0
    for peer in range(peers):
        hot = hot | (lane == peer * stride + place + row)
    return hot.astype(BF16)


def last_body(
    peers, core_ref, line_ref, b_ref, a_ref, x_ref, gain_ref, g_ref, two_ref, three_ref, diag_ref,
    hot_ref, packed_ref,
):
    half, width = b_ref.shape
    x = need(x_ref, 0)[own_rows(core_ref, half), :].astype(F32)
    dv, dgain = norm_back(x, gain_ref[...], a_ref[...] + b_ref[...].astype(F32))
    rows = (g_ref[...] + dv).astype(BF16)
    heads, buckets = diag_ref.shape[0], hot_ref.shape[1]
    lines = jnp.concatenate([diag_ref[head][:1] for head in range(heads)], axis=0)
    sums = jnp.dot(lines, hot_ref[...], preferred_element_type=F32, precision=lax.Precision.HIGHEST)
    twice = jnp.concatenate([sums, sums], axis=1)
    lane = lax.broadcasted_iota(jnp.int32, twice.shape, 1)
    first = core_ref[0] * buckets
    twice = jnp.where((lane >= first) & (lane < first + buckets), twice, 0.0)
    bias = [twice[head : head + 1] for head in range(heads)]
    bias.append(jnp.zeros((1, width - 2 * heads * buckets), F32))
    small = jnp.concatenate(
        [
            jnp.sum(dgain, axis=0, keepdims=True), two_ref[...], three_ref[...],
            jnp.concatenate(bias, axis=1),
        ],
        axis=0,
    )
    high = small.astype(BF16)
    low = (small - high.astype(F32)).astype(BF16)
    small = jnp.concatenate([high, low, jnp.zeros((8, width), BF16)], axis=0)
    stride = packed_ref.shape[0] // peers
    extra = extra_slots(16, peers, stride, stride - EXTRA)
    extra = jnp.where(lax.broadcasted_iota(jnp.int32, extra.shape, 0) < EXTRA, extra, 0.0).astype(BF16)
    packed_ref[...] = (
        dot_tn(rows_of(line_ref[...], half), rows) + dot_tn(extra, small)
    ).astype(BF16)


def unpack_last_body(peers, line_ref, packed_ref, rows_ref, small_ref):
    stride = packed_ref.shape[0] // peers
    rows_ref[...] = dot(rows_of(line_ref[...], rows_ref.shape[0]), packed_ref[...]).astype(BF16)
    flush(rows_ref)
    halves = dot(extra_slots(8, peers, stride, stride - EXTRA), packed_ref[...])
    small_ref[...] = jnp.concatenate(
        [halves[:4] + halves[4:], jnp.zeros((4, small_ref.shape[1]), F32)], axis=0
    )


def grads_in_body(core_ref, own_ref, other_ref, og_ref, turned_ref):
    half = own_ref.shape[0]
    og_ref[own_rows(core_ref, half), :] = own_ref[...]
    og_ref[their_rows(core_ref, half), :] = other_ref[...]
    turned_ref[...] = og_ref[...].T


def relative_block(order, place):
    steps = len(order)
    return sum(((place >> (steps - 1 - at)) & 1) << bit for at, bit in enumerate(order))


def weights_into(plan, peers, me_ref, refs, outs):
    for side, (order, steps) in enumerate(plan):
        keep, send = outs[2 * side], outs[2 * side + 1]
        at = 0
        for left, rights in steps:
            width = refs[left].shape[0]
            size = width // peers

            def rows(first, last):
                ref = need(refs[left], 0)
                if order is None:
                    return ref[first * size : last * size, :]
                blocks = [
                    ref[pl.ds(pl.multiple_of((relative_block(order, p) ^ me_ref[0]) * size, size), size), :]
                    for p in range(first, last)
                ]
                return jnp.concatenate(blocks, axis=0)

            for out, left_rows in ((send, rows(peers // 2, peers)), (keep, rows(0, peers // 2))):
                edge = at
                for right, low, high in rights:
                    out[: width // 2, edge : edge + high - low] = dot(
                        left_rows, refs[right][:, low:high]
                    ).astype(BF16)
                    edge += high - low
            at = edge
        flush(keep)


def weight_body(plan, peers, me_ref, *refs):
    weights_into(plan, peers, me_ref, refs, refs[-2 * len(plan) :])


def split_sum(kept, arrived, keep, send, columns=slice(None), skip=0):
    half = kept.shape[0] // 2
    send[skip : skip + half, columns] = (kept[half:].astype(F32) + arrived[half:].astype(F32)).astype(BF16)
    keep[:, columns] = (kept[:half].astype(F32) + arrived[:half].astype(F32)).astype(BF16)


def fold_in(ref, row, value):
    rows, width = value.shape[0], ref.shape[1]
    more = value.shape[1] - width
    blocks = width // more
    size = rows // blocks
    ref[row : row + rows, :] = value[:, :width]
    for i in range(blocks):
        ref[row + rows : row + rows + size, i * more : (i + 1) * more] = value[
            i * size : (i + 1) * size, width:
        ]


def fold_out(ref, row, rows, columns):
    width = ref.shape[1]
    more = columns - width
    blocks = width // more
    size = rows // blocks
    below = [
        ref[row + rows : row + rows + size, i * more : (i + 1) * more] for i in range(blocks)
    ]
    return jnp.concatenate([ref[row : row + rows, :], jnp.concatenate(below, axis=0)], axis=1)


def weight_add_body(plan, peers, me_ref, *refs):
    keep_a, send_x, keep_b, send_y, keep_ca, keep_cb, keep_fa, keep_fb, keep_fc, send_z = refs[-10:]
    ca, from_x, cb, from_y, fa, fa_there, fb, fb_there, fc, fc_there = refs[-20:-10]
    weights_into(plan, peers, me_ref, refs, [keep_a, send_x, keep_b, send_y])
    skip = keep_a.shape[0]
    split_sum(ca[...], from_x[...], keep_ca, send_y, skip=skip)
    split_sum(cb[...], from_y[...], keep_cb, send_x, skip=skip)
    skip += keep_ca.shape[0]
    split_sum(fa[...], fa_there[...], keep_fa, send_z)
    half = keep_fb.shape[0]
    for f, there, keep, send in ((fb, fb_there, keep_fb, send_x), (fc, fc_there, keep_fc, send_y)):
        total = f[...].astype(F32) + there[...].astype(F32)
        keep[...] = total[:half].astype(BF16)
        fold_in(send, skip, total[half:].astype(BF16))


def add_both_body(
    sa, sb, ca, cb, fa, fb, fc, from_x, from_y, from_z,
    keep_sa, keep_sb, send_x, send_y, keep_c, send_z, keep_f, send_w,
):
    skip, wide = sa.shape[0], ca.shape[1]
    low = skip + ca.shape[0]
    split_sum(sa[...], from_x[:skip], keep_sa, send_y)
    split_sum(sb[...], from_y[:skip], keep_sb, send_x)
    split_sum(ca[...], from_y[skip:low], keep_c, send_z, slice(0, wide))
    split_sum(cb[...], from_x[skip:low], keep_c, send_z, slice(wide, 2 * wide))
    rows, columns = fa.shape[0], fa.shape[1]
    split_sum(fa[...], from_z[...], keep_f, send_w, slice(0, columns))
    for i, (f, ref) in enumerate(((fb, from_x), (fc, from_y))):
        arrived = fold_out(ref, low, rows, columns)
        split_sum(f[...], arrived, keep_f, send_w, slice((i + 1) * columns, (i + 2) * columns))


def add_last_body(sa, sb, c, from_x, from_y, from_z, keep_s, send_z, keep_c, send_w):
    wide = sa.shape[1]
    split_sum(sa[...], from_y[...], keep_s, send_z, slice(0, wide))
    split_sum(sb[...], from_x[...], keep_s, send_z, slice(wide, 2 * wide))
    split_sum(c[...], from_z[...], keep_c, send_w)


def weight_halves(me, peers, orders, sides, after=(), weight=WEIGHT, also=None):
    args, plan, outs = [me], [], []
    flops = 0

    def place(array):
        far = isinstance(array, Far)
        for i, known in enumerate(args):
            if known is array or (far and isinstance(known, Far) and known.array is array.array):
                return i
        args.append(array)
        return len(args) - 1

    for order, side in zip(orders, sides):
        steps, total = [], 0
        for left, rights in side:
            width, rows = left.shape
            if (width // peers) % 16:
                array = left.array if isinstance(left, Far) else left
                blocks = np.array([relative_block(order, p) for p in range(peers)])
                index = (blocks ^ me[0])[:, None] * (width // peers) + np.arange(width // peers)
                left = jnp.take(array, index.reshape(-1), axis=0)
                order_here = None
            else:
                order_here = order
            steps.append((
                place(left) - 1,
                tuple((place(right) - 1, low, high) for right, low, high in rights),
            ))
            columns = sum(high - low for _, low, high in rights)
            total += columns
            flops += 2 * rows * width * columns
        plan.append((order_here, tuple(steps)))
        outs += pieces(width // 2, total)
    body = weight_body
    if also is not None:
        body = weight_add_body
        args += also
        keep_a, send_a, keep_b, send_b = outs
        cross, ff = also[0], also[4]
        rows, more = cross.shape[0] // 2, ff.shape[0] // 2
        tall = width // 2 + rows + more * ff.shape[1] // total
        small, thin = Far(shape((rows, total), BF16)), Far(shape((more, ff.shape[1]), BF16))
        outs = [keep_a, shape((tall, total), BF16), keep_b, shape((tall, total), BF16)]
        outs += [small] * 2 + [thin] * 3 + [thin.array]
    return call(
        partial(body, tuple(plan), peers), outs, args, flops=flops, smem=(0,),
        after=after, weight=weight,
    )


def add_split_body(*refs):
    count = len(refs) // 4
    for i in range(count):
        kept, arrived = refs[2 * i], refs[2 * i + 1]
        keep, send = refs[2 * count + 2 * i], refs[2 * count + 2 * i + 1]
        half = keep.shape[0]
        send[...] = (kept[half:].astype(F32) + arrived[half:].astype(F32)).astype(BF16)
        flush(send)
        keep[...] = (kept[:half].astype(F32) + arrived[:half].astype(F32)).astype(BF16)
        flush(keep)


def add_join_body(*refs):
    keep, send = refs[-2:]
    half, at = keep.shape[0], 0
    for i in range(len(refs) // 2 - 1):
        kept, arrived = refs[2 * i], refs[2 * i + 1]
        columns = slice(at, at + kept.shape[1])
        at += kept.shape[1]
        send[:, columns] = (kept[half:].astype(F32) + arrived[half:].astype(F32)).astype(BF16)
        keep[:, columns] = (kept[:half].astype(F32) + arrived[:half].astype(F32)).astype(BF16)


def finish_body(moves, kept_ref, arrived_ref, *outs):
    total = kept_ref[...].astype(F32) + arrived_ref[...].astype(F32)
    for out, index, spans in moves:
        at = 0
        for low, high in spans:
            part = total[:, low:high]
            edge = at + high - low
            if index is None:
                outs[out][:, at:edge] = part
            else:
                outs[out][index, :, at:edge] = part
            at = edge


def exchange_rows(packed, peers):
    dims = packed.shape
    blocks = packed.reshape(peers, dims[0] // peers, dims[1])
    return lax.all_to_all(blocks, "dp", split_axis=0, concat_axis=0, tiled=True).reshape(dims)


def swap(values):
    return lax.ppermute(values, "mp", [(0, 1), (1, 0)])


def neighbour(values, bit, peers):
    return lax.ppermute(values, "dp", [(i, i ^ (1 << bit)) for i in range(peers)])


def pieces(rows, *columns):
    return [kind(shape((rows, n), BF16)) for n in columns for kind in (Far, lambda s: s)]


class Sum:
    def __init__(self, halves, orders, peers):
        self.halves, self.orders, self.peers, self.place = halves, orders, peers, 0
        self.send()

    def send(self):
        self.arrived = [
            neighbour(self.halves[2 * i + 1], order[self.place], self.peers)
            for i, order in enumerate(self.orders[: len(self.halves) // 2])
        ]
        self.place += 1

    def pairs(self):
        return [
            a for i, got in enumerate(self.arrived) for a in (self.halves[2 * i], got)
        ]

    def step(self, after=()):
        kept = self.halves[0::2]
        half = kept[0].shape[0] // 2
        if half % 16:
            total = (kept[0].astype(F32) + self.arrived[0].astype(F32)).astype(BF16)
            self.halves = [total[:half], total[half:]]
        elif self.place < len(self.orders) or len(kept) == 1:
            outs = pieces(half, *(k.shape[1] for k in kept))
            self.halves = call(add_split_body, outs, self.pairs(), after=after, weight=LIGHT)
        else:
            outs = pieces(half, sum(k.shape[1] for k in kept))
            self.halves = call(add_join_body, outs, self.pairs(), after=after, weight=LIGHT)
        self.send()
        return self.halves[0]


def local(
    hidden_in,
    memory,
    output_grad,
    segment_ids,
    route_counts,
    norm_gains,
    self_qkv,
    self_out,
    cross_qkv,
    cross_out,
    ff_in,
    ff_out,
    rel_bias,
):
    peers = lax.axis_size("dp")
    me = lax.axis_index("dp")
    core = lax.axis_index("mp")
    core_ref = core.astype(jnp.int32)[None]
    half_rows, width = hidden_in.shape
    rows = 2 * half_rows
    capacity = 2 * (half_rows // peers)
    buckets, heads = rel_bias.shape
    columns = self_out.shape[0]
    units = ff_out.shape[0]
    block = width // peers
    bits = peers.bit_length() - 1
    rest = tuple(range(3, bits))
    orders = ((0, 1, 2) + rest, (1, 2, 0) + rest, (2, 0, 1) + rest)
    pair_orders = ((0, 1, 2) + rest, (1, 0, 2) + rest)
    me_ref = me.astype(jnp.int32)[None]
    slots = peers * capacity
    wide, narrow = shape((rows, width), BF16), shape((rows, columns), BF16)
    wide32, gain_shape = shape((rows, width), F32), shape((1, width), F32)
    half16, half32 = shape((half_rows, width), BF16), shape((half_rows, width), F32)
    more16 = shape((rows + half_rows, width), BF16)
    turned = shape((width, rows), BF16)
    probs_shape = shape((heads, rows, rows), BF16)
    square = rows * width * columns
    scores = heads * rows * rows

    packed, sent = call(
        pack_body,
        [shape((slots, 2 * width), BF16), Far(shape((1, slots), jnp.int32))],
        [route_counts, me_ref, Far(hidden_in), Far(memory)],
        smem=(0, 1),
    )
    arrived = exchange_rows(packed, peers)

    gains = norm_gains.astype(F32)
    gain_one, gain_two, gain_three = gains[0:1], gains[1:2], gains[2:3]
    edges = bucket_edges(buckets, MAX_DIST)
    offset = MAX_DIST - np.arange(3 * MAX_DIST)
    bucket_of = np.where(
        (offset >= 0), np.searchsorted(edges, offset, side="right"), buckets - 1
    )
    bucket_hot = bucket_of[:, None] == np.arange(buckets)[None, :]
    lines = jnp.dot(
        bucket_hot[: 2 * MAX_DIST].astype(jnp.bfloat16), rel_bias, preferred_element_type=F32
    ).T
    line = Far(shape((1, slots), jnp.int32))
    line_wide = Far(shape((1, slots + peers * EXTRA), jnp.int32))
    bias, mask, taken, sent_wide, taken_wide = call(
        tables_body,
        [
            Far(shape((heads, TILE, rows), BF16)), Far(shape((rows, rows), F32)), line, line_wide,
            line_wide,
        ],
        [route_counts, me_ref, lines, segment_ids],
        smem=(0, 1),
        after=[sent],
    )
    og, og_turned = call(
        grads_in_body,
        [Far(wide), Far(turned)],
        [core_ref, output_grad, swap(output_grad)],
        smem=(0,),
        after=[mask],
    )
    [own] = call(
        unpack_body,
        [shape((half_rows, 2 * width), BF16)],
        [taken, arrived],
        after=[mask, og_turned],
    )
    other = swap(own)

    by_head = partial(Far, axis=0, count=heads)
    x, x_far, n1_turned, sq, sk, sv, self_probs, self_mix, part_one = call(
        self_forward_body,
        [
            wide, Far(wide), Far(turned), Far(narrow), Far(narrow), Far(narrow),
            by_head(probs_shape), Far(narrow), wide,
        ],
        [core_ref, own, other, gain_one, self_qkv, mask, bias, self_out],
        flops=8 * square + 8 * scores * HEAD_DIM,
        scratch=[pltpu.VMEM((rows, width), BF16)],
        smem=(0,),
    )
    part_there = swap(part_one)
    ck, cv, mem_turned = call(
        keys_body,
        [narrow, narrow, Far(turned)],
        [core_ref, own, other, cross_qkv],
        flops=4 * square,
        scratch=[pltpu.VMEM((rows, width), BF16)],
        smem=(0,),
        after=[x_far],
    )
    h1, h1_far, n2_turned, cq, cross_probs, cross_mix, part_two = call(
        cross_forward_body,
        [wide32, Far(wide32), Far(turned), Far(narrow), by_head(probs_shape), Far(narrow), wide],
        [part_one, part_there, x, gain_two, cross_qkv, ck, mask, cv, cross_out],
        flops=4 * square + 8 * scores * HEAD_DIM,
        scratch=[pltpu.VMEM((rows, width), BF16)],
    )
    n3_turned, h2, act, d_pre, base, pack3 = call(
        ff_body,
        [turned, wide32, shape((rows, units), BF16), shape((rows, units), BF16), half32, more16],
        [core_ref, part_two, swap(part_two), h1, gain_three, ff_in, og, ff_out],
        flops=8 * rows * width * units,
        scratch=[
            pltpu.VMEM((rows, width), F32), pltpu.VMEM((rows, width), F32),
            pltpu.VMEM((rows, width), BF16),
        ],
        smem=(0,),
    )
    pack3_there = swap(pack3)

    third = 2 * units // 3
    ff_sum = Sum(
        weight_halves(me_ref, peers, orders, [
            [(og_turned, [(act, 0, third)])],
            [
                (og_turned, [(act, third, units)]),
                (n3_turned, [(d_pre, 0, 2 * third - units)]),
            ],
            [(n3_turned, [(d_pre, 2 * third - units, units)])],
        ]),
        orders, peers,
    )
    g2, g2_turned, dcq, dck, dcv, pack2, d_mem, dgain3, block_out = call(
        cross_back_body,
        [
            Far(wide32), turned, narrow, narrow, narrow, Far(more16), half32, Far(gain_shape), Far(half16),
        ],
        [
            core_ref, pack3, pack3_there, h2, og, gain_three, cross_out, cv,
            cross_probs, ck, cq, cross_qkv, base,
        ],
        flops=8 * square + 14 * scores * HEAD_DIM,
        scratch=[
            pltpu.VMEM((rows, columns), BF16), pltpu.VMEM((rows, width), F32),
            pltpu.VMEM((rows, width), BF16),
        ],
        smem=(0,),
        after=[ff_sum.halves[0]],
    )
    pack2_there = swap(pack2)
    cross_sum = Sum(
        weight_halves(me_ref, peers, pair_orders, [
            [(g2_turned, [(cross_mix, 0, columns)]), (n2_turned, [(dcq, 0, columns)])],
            [(mem_turned, [(dck, 0, columns), (dcv, 0, columns)])],
        ]),
        pair_orders, peers,
    )
    mem_packed, mem_token = call(
        pack_sum_body, [shape((slots, width), BF16), Far(shape((8, 128), F32))], [taken, d_mem, pack2_there],
        after=[cross_sum.halves[0]],
        weight=LIGHT,
    )
    mem_back = exchange_rows(mem_packed, peers)
    ff_token = ff_sum.step(after=[mem_token])
    g1_own, g1_turned, dsq, dsk, dsv, dn1, dn1_sent, dgain2, diag = call(
        self_back_body,
        [Far(half32), turned, narrow, narrow, narrow, Far(half32), half16, Far(gain_shape),
         Far(shape((heads, 8, 3 * MAX_DIST), F32))],
        [
            core_ref, Far(pack2), pack2_there, h1_far, g2, gain_two, self_out, Far(sv),
            Far(self_probs), Far(sk), Far(sq), Far(self_qkv),
        ],
        flops=8 * square + 14 * scores * HEAD_DIM,
        scratch=[
            pltpu.VMEM((rows, columns), BF16), pltpu.VMEM((rows, width), F32),
            pltpu.VMEM((rows, width), BF16),
        ],
        smem=(0,),
        after=[ff_token],
    )

    def unpack(values, line):
        return call(unpack_body, [Far(half16)], [line, values], weight=LIGHT)[0]

    dn1_there = swap(dn1_sent)
    self_sides = [
        [(g1_turned, [(Far(self_mix), 0, columns)]), (Far(n1_turned), [(dsq, 0, columns)])],
        [(Far(n1_turned), [(dsk, 0, columns), (dsv, 0, columns)])],
    ]
    merged = bits == 4
    if merged:
        ca, cb = cross_sum.halves[0::2]
        fa, fb, fc = ff_sum.halves[0::2]
        fa_there, fb_there, fc_there = ff_sum.arrived
        keep_sa, send_x, keep_sb, send_y, keep_ca, keep_cb, keep_fa, keep_fb, keep_fc, send_z = (
            weight_halves(
                me_ref, peers, pair_orders, self_sides, weight=AFTER_SELF, after=[dgain2],
                also=[
                    ca, cross_sum.arrived[0], cb, cross_sum.arrived[1],
                    fa, fa_there, fb, fb_there, fc, fc_there,
                ],
            )
        )
        from_x, from_y = neighbour(send_x, 0, peers), neighbour(send_y, 1, peers)
        from_z = neighbour(send_z, 2, peers)
        self_token = keep_sa
    else:
        self_sum = Sum(
            weight_halves(
                me_ref, peers, pair_orders, self_sides, weight=AFTER_SELF, after=[dgain2]
            ),
            pair_orders, peers,
        )
        self_token = self_sum.halves[0]
    [packed] = call(
        partial(last_body, peers),
        [shape((slots + peers * EXTRA, width), BF16)],
        [
            core_ref, taken_wide, dn1_there, Far(dn1), Far(x_far), gain_one, Far(g1_own), dgain2, dgain3,
            diag, jnp.asarray(bucket_hot, F32),
        ],
        smem=(0,),
        after=[self_token, Near(mem_back)],
        weight=LIGHT,
    )
    back = exchange_rows(packed, peers)
    token = Near(packed)
    half = width // 8

    def ff_finish(ff_pair, after):
        return call(
            partial(finish_body, ((0, None, [(units, 2 * units)]), (1, None, [(0, units)]))),
            [Far(shape((block, units), F32))] * 2, ff_pair, after=after, weight=LAST_WEIGHT,
        )

    if merged:
        pair, ff_wide = columns * 4, units * 2
        narrow_pair = shape((2 * half, 2 * columns), BF16)
        keep_sa, keep_sb, send_x, send_y, keep_c, send_z, keep_f, send_w = call(
            add_both_body,
            [Far(narrow_pair), Far(narrow_pair), narrow_pair, narrow_pair]
            + pieces(half, pair)
            + pieces(half // 2, ff_wide),
            [*map(Far, (keep_sa, keep_sb, keep_ca, keep_cb, keep_fa, keep_fb, keep_fc)), from_x, from_y, from_z],
            after=[token],
            weight=LIGHT,
        )
        ff_pair = [keep_f, neighbour(send_w, 3, peers)]
        keep_s, send_z, keep_c, send_w = call(
            add_last_body,
            pieces(half, pair) + pieces(half // 2, pair),
            [
                Far(keep_sa), Far(keep_sb), Far(keep_c),
                neighbour(send_x, 0, peers), neighbour(send_y, 1, peers),
                neighbour(send_z, 2, peers),
            ],
            weight=LIGHT,
        )
        cross_arrived, from_z = neighbour(send_w, 3, peers), neighbour(send_z, 2, peers)
        ff_in_total, ff_out_total = ff_finish(ff_pair, [keep_s])
        keep_s, send_w = call(
            add_split_body, pieces(half // 2, pair), [keep_s, from_z], after=[ff_in_total], weight=LIGHT
        )
        self_arrived = neighbour(send_w, 3, peers)
        cross_pair, self_pair = [keep_c, cross_arrived], [keep_s, self_arrived]
    else:
        for group in (cross_sum, ff_sum, self_sum):
            while group.place < bits:
                group.step()
        cross_pair, self_pair = cross_sum.pairs(), self_sum.pairs()
        ff_in_total, ff_out_total = ff_finish(ff_sum.pairs(), [])
        keep_s = ff_in_total
    memory_grad = unpack(mem_back, sent)
    input_grad, small = call(
        partial(unpack_last_body, peers),
        [Far(half16), shape((8, width), F32)],
        [sent_wide, back],
        after=[keep_s, memory_grad],
        weight=LIGHT,
    )
    moves = ((0, None, [(0, columns)]),) + tuple(
        (1, i, [((i + 1) * columns, (i + 2) * columns)]) for i in range(3)
    )

    def finish(pair, after):
        outs = [Far(shape((block, columns), F32)), Far(shape((3, block, columns), F32))]
        return call(partial(finish_body, moves), outs, pair, after=after, weight=LIGHT)

    cross_out_total, cross_qkv_total = finish(cross_pair, [input_grad])
    self_out_total, self_qkv_total = finish(self_pair, [cross_out_total])
    small = small + swap(small)
    gains_total = small[:3]
    bias_total = small[3, : 2 * heads * buckets].reshape(heads, 2, buckets).transpose(2, 1, 0)
    bias_total = bias_total.reshape(buckets, 2 * heads)
    return (
        block_out,
        input_grad,
        memory_grad,
        gains_total,
        bias_total,
        self_qkv_total,
        self_out_total.T,
        cross_qkv_total,
        cross_out_total.T,
        ff_in_total,
        ff_out_total.T,
    )


def solution(mesh):
    both = ("dp", "mp")
    in_specs = (
        P(both, None),
        P(both, None),
        P(both, None),
        P("dp", None),
        P(),
        P(),
        P(None, None, "mp"),
        P("mp", None),
        P(None, None, "mp"),
        P("mp", None),
        P(None, "mp"),
        P("mp", None),
        P(None, "mp"),
    )
    out_specs = (
        P(both, None),
        P(both, None),
        P(both, None),
        P(),
        P(),
        P(None, "dp", "mp"),
        P("mp", "dp"),
        P(None, "dp", "mp"),
        P("mp", "dp"),
        P("dp", "mp"),
        P("mp", "dp"),
    )
    return jax.shard_map(local, mesh=mesh, in_specs=in_specs, out_specs=out_specs, check_vma=False)
```

```python
from functools import partial

import jax
import jax.numpy as jnp
import numpy as np
from jax import lax
from jax.experimental import pallas as pl
from jax.experimental.pallas import tpu as pltpu
from jax.sharding import PartitionSpec as P

HEAD_DIM = 64
MAX_DIST = 128
EPS = 1e-06
MASKED = -1e30
TILE = 256
F32 = jnp.float32
BF16 = jnp.bfloat16
VMEM_LIMIT = 24 * 1024 * 1024
WEIGHT = 3 * 10**10
LIGHT = 10**6
AFTER_SELF = 3 * 10**9
LAST_WEIGHT = 7 * 10**9
FF_STEPS = 3
EXTRA = 8


def bucket_edges(buckets, distance):
    exact_span = buckets // 2
    edge_list = []
    for offset in range(1, 4 * distance):
        if offset < exact_span:
            bucket_now = offset
        else:
            log_ratio = np.log(offset / exact_span) / np.log(distance / exact_span)
            bucket_now = min(buckets - 1, exact_span + int(log_ratio * (buckets - exact_span)))
        while len(edge_list) < bucket_now:
            edge_list.append(offset)
    return np.array(edge_list, dtype=np.int32)


def dot(a, b):
    return jnp.dot(a, b, preferred_element_type=F32)


def dot_nt(a, b):
    return lax.dot_general(a, b, (((1,), (1,)), ((), ())), preferred_element_type=F32)


def dot_tn(a, b):
    return lax.dot_general(a, b, (((0,), (0,)), ((), ())), preferred_element_type=F32)


def rms_scale(values):
    return lax.rsqrt(jnp.mean(values * values, axis=-1, keepdims=True) + EPS)


def norm_back(values, gain_row, upstream):
    scale = rms_scale(values)
    scaled = gain_row * upstream
    back = scale * scaled - values * (
        scale * scale * scale * jnp.mean(scaled * values, axis=-1, keepdims=True)
    )
    return back, upstream * values * scale


class Near:
    def __init__(self, array):
        self.array = array


class Far:
    def __init__(self, array, axis=0, count=1):
        self.array, self.axis, self.count = array, axis, count
        self.shape, self.dtype = array.shape, array.dtype


def part(ref, axis, count, i):
    size = ref.shape[axis] // count
    index = tuple(
        pl.ds(i * size, size) if at == axis else slice(None) for at in range(len(ref.shape))
    )
    return ref.at[index]


class Inbound:
    def __init__(self, ref, copies):
        self.ref, self.copies, self.shape = ref, copies, ref.shape
        self.waiting = set(range(len(copies)))

    def need(self, i):
        if i in self.waiting:
            self.waiting.discard(i)
            self.copies[i].wait()

    def __getitem__(self, index):
        for i in range(len(self.copies)):
            self.need(i)
        return self.ref[index]


class Outbound:
    def __init__(self, ref, copies):
        self.ref, self.copies, self.shape, self.dtype = ref, copies, ref.shape, ref.dtype
        self.pending, self.flying = set(range(len(copies))), set()

    def __getitem__(self, index):
        return self.ref[index]

    def __setitem__(self, index, value):
        self.ref[index] = value

    def flush(self, i=None):
        for at in sorted(self.pending) if i is None else [i]:
            self.pending.discard(at)
            self.flying.add(at)
            self.copies[at].start()

    def end(self):
        self.flush()
        for at in sorted(self.flying):
            self.copies[at].wait()


def need(ref, i):
    if isinstance(ref, Inbound):
        ref.need(i % len(ref.copies))
        return ref.ref
    return ref


def flush(*refs, i=None):
    for ref in refs:
        if isinstance(ref, Outbound):
            ref.flush(i)


def call(body, outs, args, flops=0, scratch=(), smem=(), after=(), weight=WEIGHT):
    count, extra, made = len(args), len(after), len(outs)
    far_in = [i for i in range(count) if isinstance(args[i], Far)]
    far_out = [i for i in range(made) if isinstance(outs[i], Far)]
    arrays = [a.array if isinstance(a, Far) else a for a in args]
    shapes = [o.array if isinstance(o, Far) else o for o in outs]
    size = sum(a.size * a.dtype.itemsize for a in arrays + shapes)
    sems = sum(args[i].count for i in far_in) + sum(outs[i].count for i in far_out)

    given = [
        pltpu.with_memory_space_constraint(a, pltpu.HBM) if i in far_in else a
        for i, a in enumerate(arrays)
    ]

    def kernel(*refs):
        ins, refs = list(refs[:count]), refs[count + extra :]
        to, refs = list(refs[:made]), refs[made:]
        rooms, refs = refs[: len(far_in)], refs[len(far_in) :]
        shelves, rest = refs[: len(far_out)], refs[len(far_out) :]
        if sems:
            sem, rest = rest[0], rest[1:]
        at = 0
        for i, room in zip(far_in, rooms):
            copies = []
            for j in range(args[i].count):
                cut = (args[i].axis, args[i].count, j)
                copies.append(
                    pltpu.make_async_copy(part(ins[i], *cut), part(room, *cut), sem.at[at])
                )
                copies[-1].start()
                at += 1
            ins[i] = Inbound(room, copies)
        for i, shelf in zip(far_out, shelves):
            copies = []
            for j in range(outs[i].count):
                cut = (outs[i].axis, outs[i].count, j)
                copies.append(
                    pltpu.make_async_copy(part(shelf, *cut), part(to[i], *cut), sem.at[at])
                )
                at += 1
            to[i] = Outbound(shelf, copies)
        body(*ins, *to, *rest)
        for i in far_in:
            for j in sorted(ins[i].waiting):
                ins[i].need(j)
        for i in far_out:
            to[i].flush()
        for i in far_out:
            to[i].end()

    hbm, vmem = pl.BlockSpec(memory_space=pltpu.HBM), pl.BlockSpec(memory_space=pltpu.VMEM)
    return pl.pallas_call(
        kernel,
        out_shape=[
            (pltpu.HBM if i in far_out else pltpu.VMEM)(o.shape, o.dtype) for i, o in enumerate(shapes)
        ],
        in_specs=[
            pl.BlockSpec(memory_space=pltpu.SMEM) if i in smem else hbm if i in far_in else vmem
            for i in range(count)
        ]
        + [pl.BlockSpec(memory_space=pl.ANY) if isinstance(a, Near) else hbm for a in after],
        out_specs=[hbm if i in far_out else vmem for i in range(made)],
        scratch_shapes=[pltpu.VMEM(arrays[i].shape, arrays[i].dtype) for i in far_in]
        + [pltpu.VMEM(shapes[i].shape, shapes[i].dtype) for i in far_out]
        + ([pltpu.SemaphoreType.DMA((sems,))] if sems else [])
        + list(scratch),
        compiler_params=pltpu.CompilerParams(vmem_limit_bytes=VMEM_LIMIT),
        cost_estimate=pl.CostEstimate(
            flops=int(weight), bytes_accessed=0, transcendentals=0
        ),
    )(
        *given,
        *(
            a.array if isinstance(a, Near) else pltpu.with_memory_space_constraint(a, pltpu.HBM)
            for a in after
        ),
    )


def shape(dims, dtype):
    return jax.ShapeDtypeStruct(dims, dtype)


def own_rows(core_ref, half):
    return pl.ds(pl.multiple_of(core_ref[0] * half, half), half)


def their_rows(core_ref, half):
    return pl.ds(pl.multiple_of((1 - core_ref[0]) * half, half), half)


def tables_body(
    counts_ref, me_ref, vec_ref, ids_ref, bias_ref, mask_ref, taken_ref, sent_wide_ref, taken_wide_ref
):
    peers = counts_ref.shape[0]
    capacity = taken_ref.shape[1] // peers
    taken_ref[...] = slot_line(lambda s: counts_ref[s, me_ref[0]], peers, capacity)
    stride = capacity + EXTRA
    sent_wide_ref[...] = slot_line(lambda o: counts_ref[me_ref[0], o], peers, stride)
    taken_wide_ref[...] = slot_line(lambda s: counts_ref[s, me_ref[0]], peers, stride)
    heads, rows = bias_ref.shape[0], mask_ref.shape[0]
    row = lax.broadcasted_iota(jnp.int32, (MAX_DIST, 2 * MAX_DIST), 0)
    column = lax.broadcasted_iota(jnp.int32, (MAX_DIST, 2 * MAX_DIST), 1)
    for head in range(heads):
        line = vec_ref[head : head + 1, :]
        near = pltpu.roll(
            jnp.broadcast_to(line, (MAX_DIST, 2 * MAX_DIST)), 0, 1, stride=1, stride_axis=0
        )
        near = jnp.where(column > row + MAX_DIST, MASKED, near)
        far = jnp.broadcast_to(line[:, 2 * MAX_DIST - 1 :], (MAX_DIST, MAX_DIST))
        none = jnp.full((MAX_DIST, MAX_DIST), MASKED, F32)
        upper = jnp.concatenate([far, near, none], axis=1)
        lower = jnp.concatenate([far, far, near], axis=1)
        bias_ref[head] = jnp.concatenate([upper, lower], axis=0).astype(BF16)
    ids = ids_ref[...].astype(F32)
    down = jnp.broadcast_to(ids, (128, rows)).T[:, :1]
    mask_ref[...] = jnp.where(down == ids, 0.0, MASKED)


def slot_line(count_of, peers, capacity):
    lane = lax.broadcasted_iota(jnp.int32, (1, peers * capacity), 1)
    line = jnp.full_like(lane, -1)
    start = jnp.int32(0)
    for peer in range(peers):
        count, within = count_of(peer), lane - peer * capacity
        line = jnp.where((within >= 0) & (within < count), start + within, line)
        start = start + count
    return line


def rows_of(line, rows):
    row = lax.broadcasted_iota(jnp.int32, (rows, line.shape[1]), 0)
    return (line == row).astype(BF16)


def pack_body(counts_ref, me_ref, a_ref, b_ref, packed_ref, sent_ref):
    peers, (half, width) = counts_ref.shape[0], a_ref.shape
    capacity = packed_ref.shape[0] // peers
    sent = slot_line(lambda o: counts_ref[me_ref[0], o], peers, capacity)
    sent_ref[...] = sent
    flush(sent_ref)
    slots = rows_of(sent, half)
    packed_ref[:, :width] = dot_tn(slots, a_ref[...]).astype(BF16)
    packed_ref[:, width:] = dot_tn(slots, b_ref[...]).astype(BF16)


def pack_sum_body(line_ref, a_ref, b_ref, packed_ref, token_ref):
    half = a_ref.shape[0]
    skip = b_ref.shape[0] - half
    token_ref[...] = jnp.zeros_like(token_ref)
    rows = (a_ref[...] + b_ref[skip:].astype(F32)).astype(BF16)
    packed_ref[...] = dot_tn(rows_of(line_ref[...], half), rows).astype(BF16)


def unpack_body(line_ref, packed_ref, rows_ref):
    rows_ref[...] = dot(rows_of(line_ref[...], rows_ref.shape[0]), packed_ref[...]).astype(BF16)


def lane_half(values, which):
    lane = lax.broadcasted_iota(jnp.int32, values.shape, 1)
    keep = (lane < HEAD_DIM) if which == 0 else (lane >= HEAD_DIM)
    return jnp.where(keep, values, jnp.zeros_like(values))


def attend(q_ref, k_ref, v_ref, mask_ref, bias_ref, probs_ref, mix_ref):
    rows, columns = q_ref.shape
    causal = bias_ref is not None
    for pair in range(columns // (2 * HEAD_DIM)):
        lanes = slice(pair * 2 * HEAD_DIM, (pair + 1) * 2 * HEAD_DIM)
        for tile in range(rows // TILE):
            here = slice(tile * TILE, (tile + 1) * TILE)
            reach = (tile + 1) * TILE if causal else rows
            q, k, v = q_ref[here, lanes], k_ref[:reach, lanes], v_ref[:reach, lanes]
            mixed = None
            for which in range(2):
                head = 2 * pair + which
                scores = dot_nt(lane_half(q, which), k) + mask_ref[here, :reach]
                if causal:
                    bias = need(bias_ref, head)[head, :, rows - reach :]
                    scores = scores + bias.astype(F32)
                peak = jnp.max(scores, axis=-1, keepdims=True)
                weights = jnp.exp(scores - peak)
                total = jnp.sum(weights, axis=-1, keepdims=True)
                probs = (weights * (1.0 / total)).astype(BF16)
                probs_ref[head, here, :reach] = probs
                each = dot(probs, lane_half(v, which))
                mixed = each if mixed is None else mixed + each
            mix_ref[here, lanes] = mixed.astype(BF16)
        flush(probs_ref, i=2 * pair)
        flush(probs_ref, i=2 * pair + 1)
    flush(mix_ref)


def attend_back(
    q_ref, k_ref, v_ref, probs_ref, d_mix_ref, dq_ref, dk_ref, dv_ref, diag_ref, causal
):
    rows, columns = q_ref.shape
    for pair in range(columns // (2 * HEAD_DIM)):
        lanes = slice(pair * 2 * HEAD_DIM, (pair + 1) * 2 * HEAD_DIM)
        q_turned = q_ref[:, lanes].T
        d_turned = d_mix_ref[:, lanes].T
        dk_turned, dv_turned = [], []
        near = [None, None]
        for which in range(2):
            head = 2 * pair + which
            halves = slice(which * HEAD_DIM, (which + 1) * HEAD_DIM)
            dk_sum = dv_sum = None
            grown = None
            for tile in reversed(range(rows // TILE)):
                here = slice(tile * TILE, (tile + 1) * TILE)
                reach = (tile + 1) * TILE if causal else rows
                k, v = k_ref[:reach, lanes], v_ref[:reach, lanes]
                probs16 = need(probs_ref, head)[head, here, :reach]
                probs = probs16.astype(F32)
                d_probs = dot_nt(lane_half(d_mix_ref[here, lanes], which), v)
                product = probs * d_probs
                delta = jnp.sum(product, axis=-1, keepdims=True)
                d_scores = product - probs * delta
                d_scores16 = d_scores.astype(BF16)
                dq = dot(d_scores16, lane_half(k, which))
                if which == 0:
                    near[tile] = dq
                else:
                    dq_ref[here, lanes] = (near[tile] + dq).astype(BF16)
                dk = dot(q_turned[halves, here], d_scores16)
                dv = dot(d_turned[halves, here], probs16)
                if causal and reach < rows:
                    pad = jnp.zeros((HEAD_DIM, rows - reach), F32)
                    dk = jnp.concatenate([dk, pad], axis=1)
                    dv = jnp.concatenate([dv, pad], axis=1)
                dk_sum = dk if dk_sum is None else dk_sum + dk
                dv_sum = dv if dv_sum is None else dv_sum + dv
                if causal:
                    kept = d_scores16.astype(F32)
                    if reach < rows:
                        kept = jnp.concatenate(
                            [jnp.zeros((TILE, rows - reach), F32), kept], axis=1
                        )
                    grown = kept if grown is None else grown + kept
            dk_turned.append(dk_sum)
            dv_turned.append(dv_sum)
            if causal:
                d = MAX_DIST
                close = grown[:d, d : 3 * d] + grown[d:, 2 * d :]
                row = lax.broadcasted_iota(jnp.int32, close.shape, 0)
                turned, shift = close, 1
                while shift < d:
                    moved = pltpu.roll(turned, 2 * d - shift, 1)
                    turned = jnp.where((row & shift) > 0, moved, turned)
                    shift *= 2
                far = jnp.sum(grown[:d, :d] + grown[d:, :d] + grown[d:, d : 2 * d], axis=0)
                line = jnp.sum(turned, axis=0, keepdims=True)
                spread = jnp.concatenate([line, far[None]], axis=1)
                diag_ref[head] = jnp.broadcast_to(spread, (8, 3 * d))
        dk_ref[:, lanes] = jnp.concatenate(dk_turned, axis=0).T.astype(BF16)
        dv_ref[:, lanes] = jnp.concatenate(dv_turned, axis=0).T.astype(BF16)


def self_forward_body(
    core_ref, own_ref, other_ref, gain_ref, w_ref, mask_ref, bias_ref, wo_ref,
    x_ref, x_far_ref, nt_ref, q_ref, k_ref, v_ref, probs_ref, mix_ref, part_ref, n_ref,
):
    half, width = own_ref.shape[0], gain_ref.shape[1]
    x_ref[own_rows(core_ref, half), :] = own_ref[:, :width]
    x_ref[their_rows(core_ref, half), :] = other_ref[:, :width]
    x_far_ref[...] = x_ref[...]
    flush(x_far_ref)
    x = x_ref[...].astype(F32)
    n_ref[...] = (x * rms_scale(x) * gain_ref[...]).astype(BF16)
    for i, out in enumerate((q_ref, k_ref, v_ref)):
        out[...] = dot(n_ref[...], need(w_ref, i)[i]).astype(BF16)
    nt_ref[...] = n_ref[...].T
    flush(q_ref, k_ref, v_ref, nt_ref)
    attend(q_ref, k_ref, v_ref, mask_ref, bias_ref, probs_ref, mix_ref)
    part_ref[...] = dot(mix_ref[...], wo_ref[...]).astype(BF16)


def keys_body(core_ref, own_ref, other_ref, w_ref, k_ref, v_ref, memt_ref, mem_ref):
    half, width = own_ref.shape[0], w_ref.shape[1]
    mem_ref[own_rows(core_ref, half), :] = own_ref[:, width:]
    mem_ref[their_rows(core_ref, half), :] = other_ref[:, width:]
    for i, out in ((1, k_ref), (2, v_ref)):
        out[...] = dot(mem_ref[...], need(w_ref, i)[i]).astype(BF16)
    memt_ref[...] = mem_ref[...].T


def cross_forward_body(
    a_ref, b_ref, x_ref, gain_ref, w_ref, k_ref, mask_ref, v_ref, wo_ref,
    h_ref, h_far_ref, nt_ref, q_ref, probs_ref, mix_ref, part_ref, n_ref,
):
    h_ref[...] = x_ref[...].astype(F32) + (a_ref[...].astype(F32) + b_ref[...].astype(F32))
    h_far_ref[...] = h_ref[...]
    flush(h_far_ref)
    h = h_ref[...]
    n_ref[...] = (h * rms_scale(h) * gain_ref[...]).astype(BF16)
    q_ref[...] = dot(n_ref[...], need(w_ref, 0)[0]).astype(BF16)
    nt_ref[...] = n_ref[...].T
    flush(q_ref, nt_ref)
    attend(q_ref, k_ref, v_ref, mask_ref, None, probs_ref, mix_ref)
    part_ref[...] = dot(mix_ref[...], wo_ref[...]).astype(BF16)


def gelu_pair(v):
    scale = float(np.sqrt(2 / np.pi))
    square = v * v
    t = jnp.tanh(scale * (v + 0.044715 * (square * v)))
    half = 0.5 * (1.0 + t)
    slope = half + 0.5 * v * (1.0 - t * t) * (scale * (1.0 + 3 * 0.044715 * square))
    return v * half, slope


def ff_body(
    core_ref, a_ref, b_ref, h_ref, gain_ref, win_ref, og_ref, wout_ref,
    nt_ref, h2_ref, act_ref, d_pre_ref, base_ref, both_ref, out_sum, back_sum, n_ref,
):
    rows, half = h_ref.shape[0], h_ref.shape[0] // 2
    h = h_ref[...] + (a_ref[...].astype(F32) + b_ref[...].astype(F32))
    h2_ref[...] = h
    n_ref[...] = (h * rms_scale(h) * gain_ref[...]).astype(BF16)
    nt_ref[...] = n_ref[...].T
    steps = FF_STEPS
    block = win_ref.shape[1] // steps
    for step in range(steps):
        units = slice(step * block, (step + 1) * block)
        win, wout = need(win_ref, step), need(wout_ref, step)
        value, slope = gelu_pair(dot(n_ref[...], win[:, units]))
        act_ref[:, units] = value.astype(BF16)
        d_act = dot_nt(og_ref[...], wout[units, :])
        d_pre_ref[:, units] = (d_act * slope).astype(BF16)
        out = dot(act_ref[:, units], wout[units, :])
        back = dot_nt(d_pre_ref[:, units], win[:, units])
        if step:
            out, back = out_sum[...] + out, back_sum[...] + back
        out_sum[...] = out
        if step < steps - 1:
            back_sum[...] = back
        else:
            both_ref[:rows] = back.astype(BF16)
    own, theirs = own_rows(core_ref, half), their_rows(core_ref, half)
    both_ref[rows:] = out_sum[theirs, :].astype(BF16)
    base_ref[...] = h2_ref[own, :] + out_sum[own, :]


def gain_sum(core_ref, dgain):
    row = lax.broadcasted_iota(jnp.int32, dgain.shape, 0)
    half = dgain.shape[0] // 2
    mine = (row >= core_ref[0] * half) & (row < (core_ref[0] + 1) * half)
    return jnp.sum(jnp.where(mine, dgain, 0.0), axis=0, keepdims=True)


def cross_back_body(
    core_ref, a_ref, b_ref, h_ref, up_ref, gain_ref, wo_ref, v_ref, probs_ref, k_ref, q_ref,
    w_ref, base_ref,
    g_ref, gt_ref, dq_ref, dk_ref, dv_ref, both_ref, dmem_ref, dgain_ref, out_ref,
    d_mix_ref, dmem_sum, g16_ref,
):
    rows, half = h_ref.shape[0], h_ref.shape[0] // 2
    up = a_ref[:rows].astype(F32) + b_ref[:rows].astype(F32)
    dv, dgain = norm_back(h_ref[...], gain_ref[...], up)
    dgain_ref[...] = gain_sum(core_ref, dgain)
    g = up_ref[...].astype(F32) + dv
    g_ref[...] = g
    g16_ref[...] = g.astype(BF16)
    d_mix_ref[...] = dot_nt(g16_ref[...], wo_ref[...]).astype(BF16)
    gt_ref[...] = g16_ref[...].T
    attend_back(
        q_ref, k_ref, v_ref, probs_ref, d_mix_ref, dq_ref, dk_ref, dv_ref, None, False
    )
    both_ref[:rows] = dot_nt(dq_ref[...], w_ref[0]).astype(BF16)
    dmem_sum[...] = dot_nt(dk_ref[...], w_ref[1]) + dot_nt(dv_ref[...], w_ref[2])
    both_ref[rows:] = dmem_sum[their_rows(core_ref, half), :].astype(BF16)
    dmem_ref[...] = dmem_sum[own_rows(core_ref, half), :]
    out_ref[...] = (base_ref[...] + b_ref[rows:].astype(F32)).astype(BF16)


def self_back_body(
    core_ref, a_ref, b_ref, h_ref, up_ref, gain_ref, wo_ref, v_ref, probs_ref, k_ref, q_ref, w_ref,
    g_ref, gt_ref, dq_ref, dk_ref, dv_ref, dn_ref, sent_ref, dgain_ref, diag_ref,
    d_mix_ref, total, g16_ref,
):
    rows, half = h_ref.shape[0], h_ref.shape[0] // 2
    own, theirs = own_rows(core_ref, half), their_rows(core_ref, half)
    up = a_ref[:rows].astype(F32) + b_ref[:rows].astype(F32)
    dv, dgain = norm_back(h_ref[...], gain_ref[...], up)
    dgain_ref[...] = gain_sum(core_ref, dgain)
    total[...] = up_ref[...] + dv
    g_ref[...] = total[own, :]
    g16_ref[...] = total[...].astype(BF16)
    d_mix_ref[...] = dot_nt(g16_ref[...], wo_ref[...]).astype(BF16)
    gt_ref[...] = g16_ref[...].T
    attend_back(
        q_ref, k_ref, v_ref, probs_ref, d_mix_ref, dq_ref, dk_ref, dv_ref, diag_ref, True
    )
    total[...] = (
        dot_nt(dq_ref[...], w_ref[0]) + dot_nt(dk_ref[...], w_ref[1]) + dot_nt(dv_ref[...], w_ref[2])
    )
    sent_ref[...] = total[theirs, :].astype(BF16)
    dn_ref[...] = total[own, :]


def extra_slots(count, peers, stride, place):
    lane = lax.broadcasted_iota(jnp.int32, (count, peers * stride), 1)
    row = lax.broadcasted_iota(jnp.int32, (count, peers * stride), 0)
    hot = lane < 0
    for peer in range(peers):
        hot = hot | (lane == peer * stride + place + row)
    return hot.astype(BF16)


def last_body(
    peers, core_ref, line_ref, b_ref, a_ref, x_ref, gain_ref, g_ref, two_ref, three_ref, diag_ref,
    hot_ref, packed_ref,
):
    half, width = b_ref.shape
    x = need(x_ref, 0)[own_rows(core_ref, half), :].astype(F32)
    dv, dgain = norm_back(x, gain_ref[...], a_ref[...] + b_ref[...].astype(F32))
    rows = (g_ref[...] + dv).astype(BF16)
    heads, buckets = diag_ref.shape[0], hot_ref.shape[1]
    lines = jnp.concatenate([diag_ref[head][:1] for head in range(heads)], axis=0)
    sums = jnp.dot(lines, hot_ref[...], preferred_element_type=F32, precision=lax.Precision.HIGHEST)
    twice = jnp.concatenate([sums, sums], axis=1)
    lane = lax.broadcasted_iota(jnp.int32, twice.shape, 1)
    first = core_ref[0] * buckets
    twice = jnp.where((lane >= first) & (lane < first + buckets), twice, 0.0)
    bias = [twice[head : head + 1] for head in range(heads)]
    bias.append(jnp.zeros((1, width - 2 * heads * buckets), F32))
    small = jnp.concatenate(
        [
            jnp.sum(dgain, axis=0, keepdims=True), two_ref[...], three_ref[...],
            jnp.concatenate(bias, axis=1),
        ],
        axis=0,
    )
    high = small.astype(BF16)
    low = (small - high.astype(F32)).astype(BF16)
    small = jnp.concatenate([high, low, jnp.zeros((8, width), BF16)], axis=0)
    stride = packed_ref.shape[0] // peers
    extra = extra_slots(16, peers, stride, stride - EXTRA)
    extra = jnp.where(lax.broadcasted_iota(jnp.int32, extra.shape, 0) < EXTRA, extra, 0.0).astype(BF16)
    packed_ref[...] = (
        dot_tn(rows_of(line_ref[...], half), rows) + dot_tn(extra, small)
    ).astype(BF16)


def unpack_last_body(peers, line_ref, packed_ref, rows_ref, small_ref):
    stride = packed_ref.shape[0] // peers
    rows_ref[...] = dot(rows_of(line_ref[...], rows_ref.shape[0]), packed_ref[...]).astype(BF16)
    flush(rows_ref)
    halves = dot(extra_slots(8, peers, stride, stride - EXTRA), packed_ref[...])
    small_ref[...] = jnp.concatenate(
        [halves[:4] + halves[4:], jnp.zeros((4, small_ref.shape[1]), F32)], axis=0
    )


def grads_in_body(core_ref, own_ref, other_ref, og_ref, turned_ref):
    half = own_ref.shape[0]
    og_ref[own_rows(core_ref, half), :] = own_ref[...]
    og_ref[their_rows(core_ref, half), :] = other_ref[...]
    turned_ref[...] = og_ref[...].T


def relative_block(order, place):
    steps = len(order)
    return sum(((place >> (steps - 1 - at)) & 1) << bit for at, bit in enumerate(order))


def weights_into(plan, peers, me_ref, refs, outs):
    for side, (order, steps) in enumerate(plan):
        keep, send = outs[2 * side], outs[2 * side + 1]
        at = 0
        for left, rights in steps:
            width = refs[left].shape[0]
            size = width // peers

            def rows(first, last):
                ref = need(refs[left], 0)
                if order is None:
                    return ref[first * size : last * size, :]
                blocks = [
                    ref[pl.ds(pl.multiple_of((relative_block(order, p) ^ me_ref[0]) * size, size), size), :]
                    for p in range(first, last)
                ]
                return jnp.concatenate(blocks, axis=0)

            edge = at
            for out, first in ((send, peers // 2), (keep, 0)):
                if out is None:
                    continue
                left_rows = rows(first, first + peers // 2)
                edge = at
                for right, low, high in rights:
                    out[: width // 2, edge : edge + high - low] = dot(
                        left_rows, refs[right][:, low:high]
                    ).astype(BF16)
                    edge += high - low
            at = edge
        flush(keep)


def weight_body(plan, peers, me_ref, *refs):
    weights_into(plan, peers, me_ref, refs, refs[-2 * len(plan) :])


def split_sum(kept, arrived, keep, send, columns=slice(None), skip=0):
    half = kept.shape[0] // 2
    send[skip : skip + half, columns] = (kept[half:].astype(F32) + arrived[half:].astype(F32)).astype(BF16)
    keep[:, columns] = (kept[:half].astype(F32) + arrived[:half].astype(F32)).astype(BF16)


def fold_in(ref, row, value):
    rows, width = value.shape[0], ref.shape[1]
    more = value.shape[1] - width
    blocks = width // more
    size = rows // blocks
    ref[row : row + rows, :] = value[:, :width]
    for i in range(blocks):
        ref[row + rows : row + rows + size, i * more : (i + 1) * more] = value[
            i * size : (i + 1) * size, width:
        ]


def fold_out(ref, row, rows, columns):
    width = ref.shape[1]
    more = columns - width
    blocks = width // more
    size = rows // blocks
    below = [
        ref[row + rows : row + rows + size, i * more : (i + 1) * more] for i in range(blocks)
    ]
    return jnp.concatenate([ref[row : row + rows, :], jnp.concatenate(below, axis=0)], axis=1)


def weight_keep_body(plan, peers, me_ref, *refs):
    keep_a, keep_b = refs[-2:]
    weights_into(plan, peers, me_ref, refs, [keep_a, None, keep_b, None])


def weight_add_body(plan, peers, me_ref, *refs):
    send_x, send_y, keep_ca, keep_cb, keep_fa, keep_fb, keep_fc, send_z = refs[-8:]
    ca, from_x, cb, from_y, fa, fa_there, fb, fb_there, fc, fc_there = refs[-18:-8]
    weights_into(plan, peers, me_ref, refs, [None, send_x, None, send_y])
    skip = ca.shape[0]
    split_sum(ca[...], from_x[...], keep_ca, send_y, skip=skip)
    split_sum(cb[...], from_y[...], keep_cb, send_x, skip=skip)
    skip += keep_ca.shape[0]
    split_sum(fa[...], fa_there[...], keep_fa, send_z)
    half = keep_fb.shape[0]
    for f, there, keep, send in ((fb, fb_there, keep_fb, send_x), (fc, fc_there, keep_fc, send_y)):
        total = f[...].astype(F32) + there[...].astype(F32)
        keep[...] = total[:half].astype(BF16)
        fold_in(send, skip, total[half:].astype(BF16))


def add_both_body(
    sa, sb, ca, cb, fa, fb, fc, from_x, from_y, from_z,
    keep_sa, keep_sb, send_x, send_y, keep_c, send_z, keep_f, send_w,
):
    skip, wide = sa.shape[0], ca.shape[1]
    low = skip + ca.shape[0]
    split_sum(sa[...], from_x[:skip], keep_sa, send_y)
    split_sum(sb[...], from_y[:skip], keep_sb, send_x)
    split_sum(ca[...], from_y[skip:low], keep_c, send_z, slice(0, wide))
    split_sum(cb[...], from_x[skip:low], keep_c, send_z, slice(wide, 2 * wide))
    rows, columns = fa.shape[0], fa.shape[1]
    split_sum(fa[...], from_z[...], keep_f, send_w, slice(0, columns))
    for i, (f, ref) in enumerate(((fb, from_x), (fc, from_y))):
        arrived = fold_out(ref, low, rows, columns)
        split_sum(f[...], arrived, keep_f, send_w, slice((i + 1) * columns, (i + 2) * columns))


def add_last_body(sa, sb, c, from_x, from_y, from_z, keep_s, send_z, keep_c, send_w):
    wide = sa.shape[1]
    split_sum(sa[...], from_y[...], keep_s, send_z, slice(0, wide))
    split_sum(sb[...], from_x[...], keep_s, send_z, slice(wide, 2 * wide))
    split_sum(c[...], from_z[...], keep_c, send_w)


def weight_halves(me, peers, orders, sides, after=(), weight=WEIGHT, also=None, kept=False):
    args, plan, outs = [me], [], []
    flops = 0

    def place(array):
        far = isinstance(array, Far)
        for i, known in enumerate(args):
            if known is array or (far and isinstance(known, Far) and known.array is array.array):
                return i
        args.append(array)
        return len(args) - 1

    for order, side in zip(orders, sides):
        steps, total = [], 0
        for left, rights in side:
            width, rows = left.shape
            if (width // peers) % 16:
                array = left.array if isinstance(left, Far) else left
                blocks = np.array([relative_block(order, p) for p in range(peers)])
                index = (blocks ^ me[0])[:, None] * (width // peers) + np.arange(width // peers)
                left = jnp.take(array, index.reshape(-1), axis=0)
                order_here = None
            else:
                order_here = order
            steps.append((
                place(left) - 1,
                tuple((place(right) - 1, low, high) for right, low, high in rights),
            ))
            columns = sum(high - low for _, low, high in rights)
            total += columns
            flops += 2 * rows * width * columns
        plan.append((order_here, tuple(steps)))
        outs += pieces(width // 2, total)
    body = weight_body
    if kept:
        body, outs = weight_keep_body, outs[0::2]
    if also is not None:
        body = weight_add_body
        args += also
        cross, ff = also[0], also[4]
        rows, more = cross.shape[0] // 2, ff.shape[0] // 2
        tall = width // 2 + rows + more * ff.shape[1] // total
        small, thin = Far(shape((rows, total), BF16)), Far(shape((more, ff.shape[1]), BF16))
        outs = [shape((tall, total), BF16)] * 2
        outs += [small] * 2 + [thin] * 3 + [thin.array]
    return call(
        partial(body, tuple(plan), peers), outs, args, flops=flops, smem=(0,),
        after=after, weight=weight,
    )


def add_split_body(*refs):
    count = len(refs) // 4
    for i in range(count):
        kept, arrived = refs[2 * i], refs[2 * i + 1]
        keep, send = refs[2 * count + 2 * i], refs[2 * count + 2 * i + 1]
        half = keep.shape[0]
        send[...] = (kept[half:].astype(F32) + arrived[half:].astype(F32)).astype(BF16)
        flush(send)
        keep[...] = (kept[:half].astype(F32) + arrived[:half].astype(F32)).astype(BF16)
        flush(keep)


def add_join_body(*refs):
    keep, send = refs[-2:]
    half, at = keep.shape[0], 0
    for i in range(len(refs) // 2 - 1):
        kept, arrived = refs[2 * i], refs[2 * i + 1]
        columns = slice(at, at + kept.shape[1])
        at += kept.shape[1]
        send[:, columns] = (kept[half:].astype(F32) + arrived[half:].astype(F32)).astype(BF16)
        keep[:, columns] = (kept[:half].astype(F32) + arrived[:half].astype(F32)).astype(BF16)


def finish_body(moves, kept_ref, arrived_ref, *outs):
    total = kept_ref[...].astype(F32) + arrived_ref[...].astype(F32)
    for out, index, spans in moves:
        at = 0
        for low, high in spans:
            part = total[:, low:high]
            edge = at + high - low
            if index is None:
                outs[out][:, at:edge] = part
            else:
                outs[out][index, :, at:edge] = part
            at = edge


def exchange_rows(packed, peers):
    dims = packed.shape
    blocks = packed.reshape(peers, dims[0] // peers, dims[1])
    return lax.all_to_all(blocks, "dp", split_axis=0, concat_axis=0, tiled=True).reshape(dims)


def swap(values):
    return lax.ppermute(values, "mp", [(0, 1), (1, 0)])


def neighbour(values, bit, peers):
    return lax.ppermute(values, "dp", [(i, i ^ (1 << bit)) for i in range(peers)])


def pieces(rows, *columns):
    return [kind(shape((rows, n), BF16)) for n in columns for kind in (Far, lambda s: s)]


class Sum:
    def __init__(self, halves, orders, peers):
        self.halves, self.orders, self.peers, self.place = halves, orders, peers, 0
        self.send()

    def send(self):
        self.arrived = [
            neighbour(self.halves[2 * i + 1], order[self.place], self.peers)
            for i, order in enumerate(self.orders[: len(self.halves) // 2])
        ]
        self.place += 1

    def pairs(self):
        return [
            a for i, got in enumerate(self.arrived) for a in (self.halves[2 * i], got)
        ]

    def step(self, after=()):
        kept = self.halves[0::2]
        half = kept[0].shape[0] // 2
        if half % 16:
            total = (kept[0].astype(F32) + self.arrived[0].astype(F32)).astype(BF16)
            self.halves = [total[:half], total[half:]]
        elif self.place < len(self.orders) or len(kept) == 1:
            outs = pieces(half, *(k.shape[1] for k in kept))
            self.halves = call(add_split_body, outs, self.pairs(), after=after, weight=LIGHT)
        else:
            outs = pieces(half, sum(k.shape[1] for k in kept))
            self.halves = call(add_join_body, outs, self.pairs(), after=after, weight=LIGHT)
        self.send()
        return self.halves[0]


def local(
    hidden_in,
    memory,
    output_grad,
    segment_ids,
    route_counts,
    norm_gains,
    self_qkv,
    self_out,
    cross_qkv,
    cross_out,
    ff_in,
    ff_out,
    rel_bias,
):
    peers = lax.axis_size("dp")
    me = lax.axis_index("dp")
    core = lax.axis_index("mp")
    core_ref = core.astype(jnp.int32)[None]
    half_rows, width = hidden_in.shape
    rows = 2 * half_rows
    capacity = 2 * (half_rows // peers)
    buckets, heads = rel_bias.shape
    columns = self_out.shape[0]
    units = ff_out.shape[0]
    block = width // peers
    bits = peers.bit_length() - 1
    rest = tuple(range(3, bits))
    orders = ((0, 1, 2) + rest, (1, 2, 0) + rest, (2, 0, 1) + rest)
    pair_orders = ((0, 1, 2) + rest, (1, 0, 2) + rest)
    me_ref = me.astype(jnp.int32)[None]
    slots = peers * capacity
    wide, narrow = shape((rows, width), BF16), shape((rows, columns), BF16)
    wide32, gain_shape = shape((rows, width), F32), shape((1, width), F32)
    half16, half32 = shape((half_rows, width), BF16), shape((half_rows, width), F32)
    more16 = shape((rows + half_rows, width), BF16)
    turned = shape((width, rows), BF16)
    probs_shape = shape((heads, rows, rows), BF16)
    square = rows * width * columns
    scores = heads * rows * rows

    packed, sent = call(
        pack_body,
        [shape((slots, 2 * width), BF16), Far(shape((1, slots), jnp.int32))],
        [route_counts, me_ref, Far(hidden_in), Far(memory)],
        smem=(0, 1),
    )
    arrived = exchange_rows(packed, peers)

    gains = norm_gains.astype(F32)
    gain_one, gain_two, gain_three = gains[0:1], gains[1:2], gains[2:3]
    edges = bucket_edges(buckets, MAX_DIST)
    offset = MAX_DIST - np.arange(3 * MAX_DIST)
    bucket_of = np.where(
        (offset >= 0), np.searchsorted(edges, offset, side="right"), buckets - 1
    )
    bucket_hot = bucket_of[:, None] == np.arange(buckets)[None, :]
    lines = jnp.dot(
        bucket_hot[: 2 * MAX_DIST].astype(jnp.bfloat16), rel_bias, preferred_element_type=F32
    ).T
    line = Far(shape((1, slots), jnp.int32))
    line_wide = Far(shape((1, slots + peers * EXTRA), jnp.int32))
    bias, mask, taken, sent_wide, taken_wide = call(
        tables_body,
        [
            Far(shape((heads, TILE, rows), BF16)), Far(shape((rows, rows), F32)), line, line_wide,
            line_wide,
        ],
        [route_counts, me_ref, lines, segment_ids],
        smem=(0, 1),
        after=[sent],
    )
    og, og_turned = call(
        grads_in_body,
        [Far(wide), Far(turned)],
        [core_ref, output_grad, swap(output_grad)],
        smem=(0,),
        after=[mask],
    )
    [own] = call(
        unpack_body,
        [shape((half_rows, 2 * width), BF16)],
        [taken, arrived],
        after=[mask, og_turned],
    )
    other = swap(own)

    by_head = partial(Far, axis=0, count=heads)
    x, x_far, n1_turned, sq, sk, sv, self_probs, self_mix, part_one = call(
        self_forward_body,
        [
            wide, Far(wide), Far(turned), Far(narrow), Far(narrow), Far(narrow),
            by_head(probs_shape), Far(narrow), wide,
        ],
        [core_ref, own, other, gain_one, self_qkv, mask, bias, self_out],
        flops=8 * square + 8 * scores * HEAD_DIM,
        scratch=[pltpu.VMEM((rows, width), BF16)],
        smem=(0,),
    )
    part_there = swap(part_one)
    ck, cv, mem_turned = call(
        keys_body,
        [narrow, narrow, Far(turned)],
        [core_ref, own, other, cross_qkv],
        flops=4 * square,
        scratch=[pltpu.VMEM((rows, width), BF16)],
        smem=(0,),
        after=[x_far],
    )
    h1, h1_far, n2_turned, cq, cross_probs, cross_mix, part_two = call(
        cross_forward_body,
        [wide32, Far(wide32), Far(turned), Far(narrow), by_head(probs_shape), Far(narrow), wide],
        [part_one, part_there, x, gain_two, cross_qkv, ck, mask, cv, cross_out],
        flops=4 * square + 8 * scores * HEAD_DIM,
        scratch=[pltpu.VMEM((rows, width), BF16)],
    )
    n3_turned, h2, act, d_pre, base, pack3 = call(
        ff_body,
        [turned, wide32, shape((rows, units), BF16), shape((rows, units), BF16), half32, more16],
        [core_ref, part_two, swap(part_two), h1, gain_three, ff_in, og, ff_out],
        flops=8 * rows * width * units,
        scratch=[
            pltpu.VMEM((rows, width), F32), pltpu.VMEM((rows, width), F32),
            pltpu.VMEM((rows, width), BF16),
        ],
        smem=(0,),
    )
    pack3_there = swap(pack3)

    third = 2 * units // 3
    ff_sum = Sum(
        weight_halves(me_ref, peers, orders, [
            [(og_turned, [(act, 0, third)])],
            [
                (og_turned, [(act, third, units)]),
                (n3_turned, [(d_pre, 0, 2 * third - units)]),
            ],
            [(n3_turned, [(d_pre, 2 * third - units, units)])],
        ]),
        orders, peers,
    )
    g2, g2_turned, dcq, dck, dcv, pack2, d_mem, dgain3, block_out = call(
        cross_back_body,
        [
            Far(wide32), turned, narrow, narrow, narrow, Far(more16), half32, Far(gain_shape), Far(half16),
        ],
        [
            core_ref, pack3, pack3_there, h2, og, gain_three, cross_out, cv,
            cross_probs, ck, cq, cross_qkv, base,
        ],
        flops=8 * square + 14 * scores * HEAD_DIM,
        scratch=[
            pltpu.VMEM((rows, columns), BF16), pltpu.VMEM((rows, width), F32),
            pltpu.VMEM((rows, width), BF16),
        ],
        smem=(0,),
        after=[ff_sum.halves[0]],
    )
    pack2_there = swap(pack2)
    cross_sum = Sum(
        weight_halves(me_ref, peers, pair_orders, [
            [(g2_turned, [(cross_mix, 0, columns)]), (n2_turned, [(dcq, 0, columns)])],
            [(mem_turned, [(dck, 0, columns), (dcv, 0, columns)])],
        ]),
        pair_orders, peers,
    )
    mem_packed, mem_token = call(
        pack_sum_body, [shape((slots, width), BF16), Far(shape((8, 128), F32))], [taken, d_mem, pack2_there],
        after=[cross_sum.halves[0]],
        weight=LIGHT,
    )
    mem_back = exchange_rows(mem_packed, peers)
    ff_token = ff_sum.step(after=[mem_token])
    g1_own, g1_turned, dsq, dsk, dsv, dn1, dn1_sent, dgain2, diag = call(
        self_back_body,
        [Far(half32), turned, narrow, narrow, narrow, Far(half32), half16, Far(gain_shape),
         Far(shape((heads, 8, 3 * MAX_DIST), F32))],
        [
            core_ref, Far(pack2), pack2_there, h1_far, g2, gain_two, self_out, Far(sv),
            Far(self_probs), Far(sk), Far(sq), Far(self_qkv),
        ],
        flops=8 * square + 14 * scores * HEAD_DIM,
        scratch=[
            pltpu.VMEM((rows, columns), BF16), pltpu.VMEM((rows, width), F32),
            pltpu.VMEM((rows, width), BF16),
        ],
        smem=(0,),
        after=[ff_token],
    )

    def unpack(values, line):
        return call(unpack_body, [Far(half16)], [line, values], weight=LIGHT)[0]

    dn1_there = swap(dn1_sent)
    self_sides = [
        [(g1_turned, [(Far(self_mix), 0, columns)]), (Far(n1_turned), [(dsq, 0, columns)])],
        [(Far(n1_turned), [(dsk, 0, columns), (dsv, 0, columns)])],
    ]
    merged = bits == 4
    if merged:
        ca, cb = cross_sum.halves[0::2]
        fa, fb, fc = ff_sum.halves[0::2]
        fa_there, fb_there, fc_there = ff_sum.arrived
        send_x, send_y, keep_ca, keep_cb, keep_fa, keep_fb, keep_fc, send_z = (
            weight_halves(
                me_ref, peers, pair_orders, self_sides, weight=AFTER_SELF, after=[dgain2],
                also=[
                    ca, cross_sum.arrived[0], cb, cross_sum.arrived[1],
                    fa, fa_there, fb, fb_there, fc, fc_there,
                ],
            )
        )
        from_x, from_y = neighbour(send_x, 0, peers), neighbour(send_y, 1, peers)
        from_z = neighbour(send_z, 2, peers)
        self_token = keep_ca
    else:
        self_sum = Sum(
            weight_halves(
                me_ref, peers, pair_orders, self_sides, weight=AFTER_SELF, after=[dgain2]
            ),
            pair_orders, peers,
        )
        self_token = self_sum.halves[0]
    [packed] = call(
        partial(last_body, peers),
        [shape((slots + peers * EXTRA, width), BF16)],
        [
            core_ref, taken_wide, dn1_there, Far(dn1), Far(x_far), gain_one, Far(g1_own), dgain2, dgain3,
            diag, jnp.asarray(bucket_hot, F32),
        ],
        smem=(0,),
        after=[self_token, Near(mem_back)],
        weight=LIGHT,
    )
    back = exchange_rows(packed, peers)
    token = Near(packed)
    half = width // 8

    def ff_finish(ff_pair, after):
        return call(
            partial(finish_body, ((0, None, [(units, 2 * units)]), (1, None, [(0, units)]))),
            [Far(shape((block, units), F32))] * 2, ff_pair, after=after, weight=LAST_WEIGHT,
        )

    if merged:
        pair, ff_wide = columns * 4, units * 2
        keep_sa, keep_sb = weight_halves(
            me_ref, peers, pair_orders, self_sides, weight=LIGHT, after=[token], kept=True
        )
        token = keep_sa
        narrow_pair = shape((2 * half, 2 * columns), BF16)
        keep_sa, keep_sb, send_x, send_y, keep_c, send_z, keep_f, send_w = call(
            add_both_body,
            [Far(narrow_pair), Far(narrow_pair), narrow_pair, narrow_pair]
            + pieces(half, pair)
            + pieces(half // 2, ff_wide),
            [*map(Far, (keep_sa, keep_sb, keep_ca, keep_cb, keep_fa, keep_fb, keep_fc)), from_x, from_y, from_z],
            after=[token],
            weight=LIGHT,
        )
        ff_pair = [keep_f, neighbour(send_w, 3, peers)]
        keep_s, send_z, keep_c, send_w = call(
            add_last_body,
            pieces(half, pair) + pieces(half // 2, pair),
            [
                Far(keep_sa), Far(keep_sb), Far(keep_c),
                neighbour(send_x, 0, peers), neighbour(send_y, 1, peers),
                neighbour(send_z, 2, peers),
            ],
            weight=LIGHT,
        )
        cross_arrived, from_z = neighbour(send_w, 3, peers), neighbour(send_z, 2, peers)
        ff_in_total, ff_out_total = ff_finish(ff_pair, [keep_s])
        keep_s, send_w = call(
            add_split_body, pieces(half // 2, pair), [keep_s, from_z], after=[ff_in_total], weight=LIGHT
        )
        self_arrived = neighbour(send_w, 3, peers)
        cross_pair, self_pair = [keep_c, cross_arrived], [keep_s, self_arrived]
    else:
        for group in (cross_sum, ff_sum, self_sum):
            while group.place < bits:
                group.step()
        cross_pair, self_pair = cross_sum.pairs(), self_sum.pairs()
        ff_in_total, ff_out_total = ff_finish(ff_sum.pairs(), [])
        keep_s = ff_in_total
    memory_grad = unpack(mem_back, sent)
    input_grad, small = call(
        partial(unpack_last_body, peers),
        [Far(half16), shape((8, width), F32)],
        [sent_wide, back],
        after=[keep_s, memory_grad],
        weight=LIGHT,
    )
    moves = ((0, None, [(0, columns)]),) + tuple(
        (1, i, [((i + 1) * columns, (i + 2) * columns)]) for i in range(3)
    )

    def finish(pair, after):
        outs = [Far(shape((block, columns), F32)), Far(shape((3, block, columns), F32))]
        return call(partial(finish_body, moves), outs, pair, after=after, weight=LIGHT)

    cross_out_total, cross_qkv_total = finish(cross_pair, [input_grad])
    self_out_total, self_qkv_total = finish(self_pair, [cross_out_total])
    small = small + swap(small)
    gains_total = small[:3]
    bias_total = small[3, : 2 * heads * buckets].reshape(heads, 2, buckets).transpose(2, 1, 0)
    bias_total = bias_total.reshape(buckets, 2 * heads)
    return (
        block_out,
        input_grad,
        memory_grad,
        gains_total,
        bias_total,
        self_qkv_total,
        self_out_total.T,
        cross_qkv_total,
        cross_out_total.T,
        ff_in_total,
        ff_out_total.T,
    )


def solution(mesh):
    both = ("dp", "mp")
    in_specs = (
        P(both, None),
        P(both, None),
        P(both, None),
        P("dp", None),
        P(),
        P(),
        P(None, None, "mp"),
        P("mp", None),
        P(None, None, "mp"),
        P("mp", None),
        P(None, "mp"),
        P("mp", None),
        P(None, "mp"),
    )
    out_specs = (
        P(both, None),
        P(both, None),
        P(both, None),
        P(),
        P(),
        P(None, "dp", "mp"),
        P("mp", "dp"),
        P(None, "dp", "mp"),
        P("mp", "dp"),
        P("dp", "mp"),
        P("mp", "dp"),
    )
    return jax.shard_map(local, mesh=mesh, in_specs=in_specs, out_specs=out_specs, check_vma=False)
```
